32 devices in a mesh: dp: 8 (over z, y), mp: 4 (over x, core).
Axes of the slice: x: 2, y: 2, z: 4, core: 2. Of those that a mesh axis runs over, the one named last changes fastest.
Arguments:
- inputs: float32 [12288, 768], P('dp'), may hold values from -6 to 6
- cotangent: float32 [12288, 768], P('dp'), may hold values from -6 to 6
- word_lengths: int32 [24, 170], P('dp'), may hold values from 1 to 3
- word_count: int32 [24], P('dp'), may hold values from 20 to 170, as said below
- attn_in: float32 [2, 3, 768, 768], P(None, None, 'dp', 'mp'), may hold values from -0.3125 to 0.3125
- attn_out: float32 [2, 768, 768], P(None, 'dp', 'mp'), may hold values from -0.3125 to 0.3125
- ffn_up: float32 [2, 768, 3072], P(None, 'dp', 'mp'), may hold values from -0.21875 to 0.21875
- ffn_down: float32 [2, 768, 3072], P(None, 'dp', 'mp'), may hold values from -0.109375 to 0.109375
- head_bias: float32 [2, 2, 768], P(None, None, 'mp'), may hold values from -3 to 3
- ffn_bias: float32 [2, 3072], P(None, 'mp'), may hold values from -3 to 3
- row_params: float32 [2, 6, 768], replicated
- attn_in_mom: float32 [2, 3, 768, 768], P(None, None, 'dp', 'mp'), may hold values from -192 to 192
- attn_out_mom: float32 [2, 768, 768], P(None, 'dp', 'mp'), may hold values from -96 to 96
- ffn_up_mom: float32 [2, 768, 3072], P(None, 'dp', 'mp'), may hold values from -128 to 128
- ffn_down_mom: float32 [2, 768, 3072], P(None, 'dp', 'mp'), may hold values from -160 to 160
- head_bias_mom: float32 [2, 2, 768], P(None, None, 'mp'), may hold values from -256 to 256
- ffn_bias_mom: float32 [2, 3072], P(None, 'mp'), may hold values from -128 to 128
- row_params_mom: float32 [2, 6, 768], replicated, may hold values from -256 to 256
- attn_in_var: float32 [2, 3, 768, 768], P(None, None, 'dp', 'mp'), may hold values from 1105.92 to 4423.68
- attn_out_var: float32 [2, 768, 768], P(None, 'dp', 'mp'), may hold values from 276.48 to 1105.92
- ffn_up_var: float32 [2, 768, 3072], P(None, 'dp', 'mp'), may hold values from 491.52 to 1966.08
- ffn_down_var: float32 [2, 768, 3072], P(None, 'dp', 'mp'), may hold values from 768 to 3072
- head_bias_var: float32 [2, 2, 768], P(None, None, 'mp'), may hold values from 1966.08 to 7864.32
- ffn_bias_var: float32 [2, 3072], P(None, 'mp'), may hold values from 122.88 to 491.52
- row_params_var: float32 [2, 6, 768], replicated, may hold values from 1966.08 to 7864.32
Outputs:
- encoded: float32 [12288, 768], P('dp')
- input_grad: float32 [12288, 768], P('dp')
- attn_in_new: float32 [2, 3, 768, 768], P(None, None, 'dp', 'mp')
- attn_out_new: float32 [2, 768, 768], P(None, 'dp', 'mp')
- ffn_up_new: float32 [2, 768, 3072], P(None, 'dp', 'mp')
- ffn_down_new: float32 [2, 768, 3072], P(None, 'dp', 'mp')
- head_bias_new: float32 [2, 2, 768], P(None, None, 'mp')
- ffn_bias_new: float32 [2, 3072], P(None, 'mp')
- row_params_new: float32 [2, 6, 768], replicated
- attn_in_mom_new: float32 [2, 3, 768, 768], P(None, None, 'dp', 'mp')
- attn_out_mom_new: float32 [2, 768, 768], P(None, 'dp', 'mp')
- ffn_up_mom_new: float32 [2, 768, 3072], P(None, 'dp', 'mp')
- ffn_down_mom_new: float32 [2, 768, 3072], P(None, 'dp', 'mp')
- head_bias_mom_new: float32 [2, 2, 768], P(None, None, 'mp')
- ffn_bias_mom_new: float32 [2, 3072], P(None, 'mp')
- row_params_mom_new: float32 [2, 6, 768], replicated
- attn_in_var_new: float32 [2, 3, 768, 768], P(None, None, 'dp', 'mp')
- attn_out_var_new: float32 [2, 768, 768], P(None, 'dp', 'mp')
- ffn_up_var_new: float32 [2, 768, 3072], P(None, 'dp', 'mp')
- ffn_down_var_new: float32 [2, 768, 3072], P(None, 'dp', 'mp')
- head_bias_var_new: float32 [2, 2, 768], P(None, None, 'mp')
- ffn_bias_var_new: float32 [2, 3072], P(None, 'mp')
- row_params_var_new: float32 [2, 6, 768], replicated
- attn_in_copy: bfloat16 [2, 3, 768, 768], P(None, None, 'dp', 'mp')
- attn_out_copy: bfloat16 [2, 768, 768], P(None, 'dp', 'mp')
- ffn_up_copy: bfloat16 [2, 768, 3072], P(None, 'dp', 'mp')
- ffn_down_copy: bfloat16 [2, 768, 3072], P(None, 'dp', 'mp')
The draws below stay inside these ranges and needn't reach their ends.
Inputs may be any that keep to these rules, and one draw needn't show every extreme that they name: `word_count`: how many word slots at the head of each sequence hold text; the rest of the sequence is padding.
All inputs are finite; a program needn't handle non-finite values.
Results may differ from the reference program's by a relative error of at most 0.04.
The reference program's roundings to bfloat16 on the way count: a program that leaves them out, or rounds other values in their place, can miss the bound.
Values may be sent and summed in bfloat16 or wider, within the bound.
No kernel may reach another device: no remote copies, remote signals or barrier semaphores. Data moves between devices by JAX's collectives and lax.ppermute only.
A program may use at most 256 MiB of HBM per device.

```python
import math
import jax
import jax.numpy as jnp
from jax import lax

D = 768
HEADS = 12
HEAD_DIM = 64
FF = 3072
LAYERS = 2
SEQ_LEN = 512
ADAM_STEP = 10
WORDS = 170
SEQS = 24
TOKENS = 12288
N_MP = 4


def draw_word_count(key, part):
    key = jax.random.fold_in(key, 7)
    seq_order = jnp.arange(SEQS, dtype=jnp.int32)
    lowest = WORDS // 4
    floor_count = max(WORDS // 4 - WORDS // 8 - 1, 1)
    base_count = lowest + (WORDS - lowest) * seq_order // (SEQS - 1)
    jitter = jax.random.randint(key, (SEQS,), 0, WORDS // 8 + 2, dtype=jnp.int32)
    counts = jnp.clip(base_count - jitter, 1, WORDS)
    counts = jnp.where(seq_order == 0, floor_count, counts)
    return jnp.where(seq_order == SEQS - 1, WORDS, counts).astype(jnp.int32)


def draw_row_params(key, part):
    key = jax.random.fold_in(key, 11)
    noise_key, gain_key = jax.random.split(key)
    shifts = jax.random.normal(noise_key, (LAYERS, 6, D), jnp.float32) * 0.3
    gains = jax.random.uniform(gain_key, (LAYERS, 6, D), jnp.float32, 0.6, 1.4)
    slots = jnp.arange(6, dtype=jnp.int32)
    is_gain = (slots == 2) | (slots == 4)
    return jnp.where(is_gain[None, :, None], gains, shifts).astype(jnp.float32)


def touch_ends(array, stream_key, low, top_value):
    dims = array.shape
    index_at = [jax.random.randint(jax.random.fold_in(stream_key, axis), (), 0, dims[axis]) for axis in range(len(dims))]
    array = array.at[tuple(index_at)].set(low)
    longest = dims.index(max(dims))
    index_at[longest] = (index_at[longest] + 1) % dims[longest]
    return array.at[tuple(index_at)].set(top_value)


def levels(key, shape, cuts, least, top_value):
    gain = 1.0
    for axis_at, parts in cuts:
        heights = jax.random.uniform(jax.random.fold_in(jax.random.fold_in(key, 6), axis_at), (parts,), jnp.float32, least / len(cuts), top_value / len(cuts))
        gain = gain * jnp.repeat(jnp.exp(heights), shape[axis_at] // parts).reshape((-1,) + (1,) * (len(shape) - 1 - axis_at))
    return gain


def normal_values(rng, dims, spread, most, shards=(), held_as=jnp.bfloat16):
    factor_of = levels(rng, dims, shards, -0.22, 0.18) if shards else 1.0
    values = jax.random.normal(rng, dims, jnp.float32) * spread * factor_of
    return jnp.minimum(jnp.maximum(values, -most), most).astype(held_as)


def setup_inputs(seed: int = 0) -> dict:
    key_of = jax.random.split(jax.random.key(seed), 26)
    inputs = normal_values(key_of[0], (TOKENS, D), 1.0, 6.0, ((0, 8),), jnp.float32)
    cotangent = normal_values(key_of[1], (TOKENS, D), 1.0, 6.0, ((0, 8),), jnp.float32)
    word_lengths = touch_ends(jax.random.randint(key_of[2], (SEQS, WORDS), 1, 4), jax.random.fold_in(key_of[2], 1), 1, 3).astype(jnp.int32)
    word_count = draw_word_count(jax.random.fold_in(key_of[25], 71), 0)
    attn_in = normal_values(key_of[4], (LAYERS, 3, D, D), (D // 2) ** -0.5, 0.3125, ((2, 8), (3, 4)), jnp.float32)
    attn_out = normal_values(key_of[5], (LAYERS, D, D), (D // 2) ** -0.5, 0.3125, ((1, 8), (2, 4)), jnp.float32)
    ffn_up = normal_values(key_of[6], (LAYERS, D, FF), D ** -0.5, 0.21875, ((1, 8), (2, 4)), jnp.float32)
    ffn_down = normal_values(key_of[7], (LAYERS, D, FF), FF ** -0.5, 0.109375, ((1, 8), (2, 4)), jnp.float32)
    head_bias = normal_values(key_of[8], (LAYERS, 2, D), 0.5, 3.0, ((2, 4),), jnp.float32)
    ffn_bias = normal_values(key_of[9], (LAYERS, FF), 0.5, 3.0, ((1, 4),), jnp.float32)
    row_params = draw_row_params(jax.random.fold_in(key_of[25], 71), 0)
    attn_in_mom = normal_values(key_of[11], (LAYERS, 3, D, D), (0.3 * TOKENS ** 0.5), 192.0, ((2, 8), (3, 4)), jnp.float32)
    attn_out_mom = normal_values(key_of[12], (LAYERS, D, D), (0.15 * TOKENS ** 0.5), 96.0, ((1, 8), (2, 4)), jnp.float32)
    ffn_up_mom = normal_values(key_of[13], (LAYERS, D, FF), (0.2 * TOKENS ** 0.5), 128.0, ((1, 8), (2, 4)), jnp.float32)
    ffn_down_mom = normal_values(key_of[14], (LAYERS, D, FF), (0.25 * TOKENS ** 0.5), 160.0, ((1, 8), (2, 4)), jnp.float32)
    head_bias_mom = normal_values(key_of[15], (LAYERS, 2, D), (0.4 * TOKENS ** 0.5), 256.0, ((2, 4),), jnp.float32)
    ffn_bias_mom = normal_values(key_of[16], (LAYERS, FF), (0.2 * TOKENS ** 0.5), 128.0, ((1, 4),), jnp.float32)
    row_params_mom = normal_values(key_of[17], (LAYERS, 6, D), (0.4 * TOKENS ** 0.5), 256.0, (), jnp.float32)
    attn_in_var = jnp.clip(jnp.exp(math.log(4423.68) - 1.3862944 * jax.random.uniform(key_of[18], (LAYERS, 3, D, D), jnp.float32) ** levels(key_of[18], (LAYERS, 3, D, D), ((2, 8), (3, 4)), -0.2, 0.2)), 1105.92, 4423.68)
    attn_out_var = jnp.clip(jnp.exp(math.log(1105.92) - 1.3862944 * jax.random.uniform(key_of[19], (LAYERS, D, D), jnp.float32) ** levels(key_of[19], (LAYERS, D, D), ((1, 8), (2, 4)), -0.2, 0.2)), 276.48, 1105.92)
    ffn_up_var = jnp.clip(jnp.exp(math.log(1966.08) - 1.3862944 * jax.random.uniform(key_of[20], (LAYERS, D, FF), jnp.float32) ** levels(key_of[20], (LAYERS, D, FF), ((1, 8), (2, 4)), -0.2, 0.2)), 491.52, 1966.08)
    ffn_down_var = jnp.clip(jnp.exp(math.log(3072.0) - 1.3862944 * jax.random.uniform(key_of[21], (LAYERS, D, FF), jnp.float32) ** levels(key_of[21], (LAYERS, D, FF), ((1, 8), (2, 4)), -0.2, 0.2)), 768.0, 3072.0)
    head_bias_var = jnp.clip(jnp.exp(math.log(7864.32) - 1.3862944 * jax.random.uniform(key_of[22], (LAYERS, 2, D), jnp.float32) ** levels(key_of[22], (LAYERS, 2, D), ((2, 4),), -0.2, 0.2)), 1966.08, 7864.32)
    ffn_bias_var = jnp.clip(jnp.exp(math.log(491.52) - 1.3862944 * jax.random.uniform(key_of[23], (LAYERS, FF), jnp.float32) ** levels(key_of[23], (LAYERS, FF), ((1, 4),), -0.2, 0.2)), 122.88, 491.52)
    row_params_var = jnp.clip(jnp.exp(jax.random.uniform(key_of[24], (LAYERS, 6, D), jnp.float32, math.log(1966.08), math.log(7864.32))), 1966.08, 7864.32)
    return {"inputs": inputs, "cotangent": cotangent, "word_lengths": word_lengths, "word_count": word_count, "attn_in": attn_in, "attn_out": attn_out, "ffn_up": ffn_up, "ffn_down": ffn_down, "head_bias": head_bias, "ffn_bias": ffn_bias, "row_params": row_params, "attn_in_mom": attn_in_mom, "attn_out_mom": attn_out_mom, "ffn_up_mom": ffn_up_mom, "ffn_down_mom": ffn_down_mom, "head_bias_mom": head_bias_mom, "ffn_bias_mom": ffn_bias_mom, "row_params_mom": row_params_mom, "attn_in_var": attn_in_var, "attn_out_var": attn_out_var, "ffn_up_var": ffn_up_var, "ffn_down_var": ffn_down_var, "head_bias_var": head_bias_var, "ffn_bias_var": ffn_bias_var, "row_params_var": row_params_var}


HIGH = lax.Precision.HIGHEST
EPS_NORM = 1e-12
EPS_ADAM = 1e-08
RATE_MATRIX = 0.04
RATE_VECTOR = 0.3
DECAY_MATRIX = 0.01

@jax.custom_vjp
def low(v):
    return lax.optimization_barrier(v.astype(jnp.bfloat16)).astype(jnp.float32)

@jax.custom_vjp
def low_back(v):
    return v

def low_keep(v):
    return (low(v), None)

def low_pass(kept, grad):
    return (grad,)

def back_keep(v):
    return (v, None)

def back_low(kept, grad):
    return (low(grad),)
low.defvjp(low_keep, low_pass)
low_back.defvjp(back_keep, back_low)

def both_ways(value_in):
    return low_back(low(value_in))

def layer_norm(residual, gain_row, shift_row):
    center = residual - lax.optimization_barrier(jnp.mean(residual, axis=-1, keepdims=True))
    scaled = center * lax.rsqrt(lax.optimization_barrier(jnp.mean(center * center, axis=-1, keepdims=True)) + EPS_NORM)
    return scaled * gain_row + shift_row

def encoder_layer(hidden_in, pieces, key_mask):
    weight_in, weight_out, weight_up, weight_down, head_b, ffn_b, rows = pieces
    tokens = hidden_in.shape[0]
    seq_count = tokens // SEQ_LEN
    width_dev = D // N_MP
    hidden_dev = FF // N_MP
    heads_dev = HEADS // N_MP
    in_low = low(hidden_in)
    qkv_low = low(weight_in).reshape(3, D, N_MP, width_dev)
    projected = jnp.einsum('td,kdgc->kgtc', in_low, qkv_low, precision=HIGH)
    bias_query = head_b[0].reshape(N_MP, 1, width_dev)
    bias_value = head_b[1].reshape(N_MP, 1, width_dev)
    head_shape = (N_MP, seq_count, SEQ_LEN, heads_dev, HEAD_DIM)
    queries = both_ways((projected[0] + bias_query) * 0.125).reshape(head_shape)
    key_rows = both_ways(projected[1]).reshape(head_shape)
    value_rows = both_ways(projected[2] + bias_value).reshape(head_shape)
    scores = low_back(jnp.einsum('gsqhe,gskhe->gshqk', queries, key_rows, precision=HIGH))
    scores = jnp.where(key_mask[None, :, None, None, :], scores, -1000000000.0)
    shifted = jnp.exp(scores - lax.optimization_barrier(jnp.max(scores, axis=-1, keepdims=True)))
    attn_probs = shifted / lax.optimization_barrier(jnp.sum(shifted, axis=-1, keepdims=True))
    context = jnp.einsum('gshqk,gskhe->gsqhe', low(attn_probs), value_rows, precision=HIGH)
    context = both_ways(context.reshape(N_MP, tokens, width_dev))
    out_low = low(weight_out).reshape(D, N_MP, width_dev)
    partial_attn = jnp.einsum('gtc,ogc->gto', context, out_low, precision=HIGH)
    attended = low_back(lax.optimization_barrier(jnp.sum(partial_attn, axis=0))) + rows[0]
    normed = layer_norm(hidden_in + attended, rows[2], rows[3])
    normed_low = low(normed)
    up_low = low(weight_up).reshape(D, N_MP, hidden_dev)
    pre_act = jnp.einsum('td,dgf->gtf', normed_low, up_low, precision=HIGH) + ffn_b.reshape(N_MP, 1, hidden_dev)
    activated = low(jax.nn.gelu(low_back(pre_act), approximate=False))
    down_low = low(weight_down).reshape(D, N_MP, hidden_dev)
    partial_ffn = jnp.einsum('gtf,ogf->gto', activated, down_low, precision=HIGH)
    ffn_result = low_back(lax.optimization_barrier(jnp.sum(partial_ffn, axis=0))) + rows[1]
    return layer_norm(normed + ffn_result, rows[4], rows[5])

def adam_step(master, moment, second, gradient, step_rate, decay_rate):
    correction = 1.0 - 0.5 ** ADAM_STEP
    moment_new = 0.5 * moment + 0.5 * gradient
    second_new = 0.5 * second + 0.5 * gradient * gradient
    update = moment_new / correction / (jnp.sqrt(second_new / correction) + EPS_ADAM) + decay_rate * master
    return (master - step_rate * update, moment_new, second_new)

def reference(inputs, cotangent, word_lengths, word_count, attn_in, attn_out, ffn_up, ffn_down, head_bias, ffn_bias, row_params, attn_in_mom, attn_out_mom, ffn_up_mom, ffn_down_mom, head_bias_mom, ffn_bias_mom, row_params_mom, attn_in_var, attn_out_var, ffn_up_var, ffn_down_var, head_bias_var, ffn_bias_var, row_params_var):
    word_slots = jnp.arange(WORDS, dtype=jnp.int32)
    used_tokens = lax.optimization_barrier(jnp.sum(jnp.where(word_slots[None, :] < word_count[:, None], word_lengths, 0), axis=1))
    key_mask = jnp.arange(SEQ_LEN, dtype=jnp.int32)[None, :] < used_tokens[:, None]
    row_mask = key_mask.reshape(TOKENS, 1).astype(jnp.float32)
    target = cotangent * row_mask
    params = (attn_in, attn_out, ffn_up, ffn_down, head_bias, ffn_bias, row_params)
    groups = SEQS // 8
    group_rows = 8 * SEQ_LEN

    def forward(hidden, weights, group_mask):
        for layer_index in range(LAYERS):
            pieces = tuple((weight[layer_index] for weight in weights))
            hidden = encoder_layer(hidden, pieces, group_mask)
        return hidden

    def one_group(totals, group_data):
        rows_in, rows_back, group_mask = group_data
        result, pullback = jax.vjp(lambda hidden, weights: forward(hidden, weights, group_mask), rows_in, params)
        grad_in, grad_params = pullback(rows_back)
        return (jax.tree.map(jnp.add, totals, grad_params), (result, grad_in))
    zero_grads = jax.tree.map(jnp.zeros_like, params)
    totals, (encoded, input_grad) = lax.scan(one_group, zero_grads, (inputs.reshape(groups, group_rows, D), target.reshape(groups, group_rows, D), key_mask.reshape(groups, 8, SEQ_LEN)))
    moments = (attn_in_mom, attn_out_mom, ffn_up_mom, ffn_down_mom, head_bias_mom, ffn_bias_mom, row_params_mom)
    seconds = (attn_in_var, attn_out_var, ffn_up_var, ffn_down_var, head_bias_var, ffn_bias_var, row_params_var)
    new_params = []
    new_moments = []
    new_seconds = []
    for index in range(7):
        step_rate = RATE_MATRIX if index < 4 else RATE_VECTOR
        decay_rate = DECAY_MATRIX if index < 4 else 0.0
        master_new, moment_new, second_new = adam_step(params[index], moments[index], seconds[index], totals[index], step_rate, decay_rate)
        new_params.append(master_new)
        new_moments.append(moment_new)
        new_seconds.append(second_new)
    return (encoded.reshape(TOKENS, D), input_grad.reshape(TOKENS, D), new_params[0], new_params[1], new_params[2], new_params[3], new_params[4], new_params[5], new_params[6], new_moments[0], new_moments[1], new_moments[2], new_moments[3], new_moments[4], new_moments[5], new_moments[6], new_seconds[0], new_seconds[1], new_seconds[2], new_seconds[3], new_seconds[4], new_seconds[5], new_seconds[6], new_params[0].astype(jnp.bfloat16), new_params[1].astype(jnp.bfloat16), new_params[2].astype(jnp.bfloat16), new_params[3].astype(jnp.bfloat16))
```

```python
import jax
import jax.numpy as jnp
from jax import lax
from jax.sharding import PartitionSpec as P

HEAD_DIM = 64
LAYERS = 2
ADAM_STEP = 10

EPS_NORM = 1e-12
EPS_ADAM = 1e-08
RATE_MATRIX = 0.04
RATE_VECTOR = 0.3
DECAY_MATRIX = 0.01

F32 = jnp.float32
BF16 = jnp.bfloat16
AXES = ("dp", "mp")


class Links:
    def __init__(self, n_dp):
        self.count = n_dp * 4
        self.bits = n_dp.bit_length() - 1
        dp_at = lax.axis_index("dp")
        mp_at = lax.axis_index("mp")
        self.at_x = mp_at // 2
        self.core = mp_at % 2
        self.at_y = dp_at % 2
        self.dp_at = dp_at

    def swap(self, array, mask0, mask1=None):
        mask1 = mask0 if mask1 is None else mask1
        pairs = [(i, i ^ (mask1 if i & 1 else mask0)) for i in range(self.count)]
        return lax.ppermute(array, AXES, pairs)

    def swap_core(self, array):
        return self.swap(array, 1)

    def swap_x(self, array):
        return self.swap(array, 2)

    def gather(self, piece):
        block = piece[None]
        for bit in range(1, self.bits):
            other = self.swap(block, 4 << bit)
            mine = ((self.dp_at >> bit) & 1) == 0
            block = jnp.concatenate([jnp.where(mine, block, other), jnp.where(mine, other, block)])
        near = self.swap(block, 4, 2)
        far = self.swap(jnp.stack([block, near]), 2, 4)
        first = self.core == 0
        own_far = jnp.where(first, near, far[0])
        other_near = jnp.where(first, far[0], near)
        other_far = far[1]
        return self.rows(block, own_far), self.rows(other_near, other_far)

    def rows(self, same, other):
        low = self.at_y == 0
        both = jnp.stack([jnp.where(low, same, other), jnp.where(low, other, same)], axis=1)
        return both.reshape(-1, both.shape[-1])

    def scatter(self, grad_own, grad_other):
        rows = grad_own.shape[0] >> self.bits
        low = self.at_y == 0

        def halves(grad):
            grad = grad.reshape(-1, 2, rows, grad.shape[-1])
            return jnp.where(low, grad[:, 0], grad[:, 1]), jnp.where(low, grad[:, 1], grad[:, 0])

        own_same, own_far = halves(grad_own)
        other_same, other_far = halves(grad_other)
        first = self.core == 0
        came = self.swap(jnp.stack([jnp.where(first, other_same, own_far), other_far]), 2, 4)
        keep = own_same.astype(F32) + came[0].astype(F32)
        give = jnp.where(first, own_far, other_same).astype(F32) + came[1].astype(F32)
        came = self.swap(give.astype(BF16), 4, 2)
        keep = keep + came.astype(F32)
        for bit in reversed(range(1, self.bits)):
            half = keep.shape[0] // 2
            mine = ((self.dp_at >> bit) & 1) == 0
            give = jnp.where(mine, keep[half:], keep[:half]).astype(BF16)
            keep = jnp.where(mine, keep[:half], keep[half:])
            keep = keep + self.swap(give, 4 << bit).astype(F32)
        return keep[0]


def norm_parts(residual, gain_row, shift_row):
    center = residual - jnp.mean(residual, axis=-1, keepdims=True)
    inv_std = lax.rsqrt(jnp.mean(center * center, axis=-1, keepdims=True) + EPS_NORM)
    scaled = center * inv_std
    return (scaled * gain_row + shift_row, scaled, inv_std)


def norm_back(grad_output, scaled, inv_std, gain_row):
    upstream = grad_output * gain_row
    mean_up = jnp.mean(upstream, axis=-1, keepdims=True)
    mean_cross = jnp.mean(upstream * scaled, axis=-1, keepdims=True)
    return inv_std * (upstream - mean_up - scaled * mean_cross)


def dot(a, b, dims):
    return lax.dot_general(a, b, (dims, ((), ())), preferred_element_type=F32)


NN = ((1,), (0,))
NT = ((1,), (1,))
TN = ((0,), (0,))


def both_cores(links, partial):
    low = partial.astype(BF16)
    return low.astype(F32) + links.swap_core(low).astype(F32)


def heads_of(rows_in):
    return rows_in.reshape(rows_in.shape[0], -1, HEAD_DIM)


def attend(queries, keys, values, mask):
    scores = jnp.einsum("qhe,khe->hqk", heads_of(queries), heads_of(keys), preferred_element_type=F32)
    scores = jnp.where(mask[None, None, :], scores, -1000000000.0)
    shifted = jnp.exp(scores - jnp.max(scores, axis=-1, keepdims=True))
    probs = shifted / jnp.sum(shifted, axis=-1, keepdims=True)
    context = jnp.einsum("hqk,khe->qhe", probs.astype(BF16), heads_of(values), preferred_element_type=F32)
    return context.reshape(queries.shape).astype(BF16), probs


def attend_back(grad_context, queries, keys, values, probs):
    low = probs.astype(BF16)
    grad_heads = heads_of(grad_context)
    grad_values = jnp.einsum("hqk,qhe->khe", low, grad_heads, preferred_element_type=F32)
    grad_probs = jnp.einsum("qhe,khe->hqk", grad_heads, heads_of(values), preferred_element_type=F32)
    inner = jnp.sum(probs * grad_probs, axis=-1, keepdims=True)
    grad_scores = (probs * (grad_probs - inner)).astype(BF16)
    grad_queries = jnp.einsum("hqk,khe->qhe", grad_scores, heads_of(keys), preferred_element_type=F32)
    grad_queries = (grad_queries.astype(BF16) * 0.125).reshape(queries.shape)
    grad_keys = jnp.einsum("hqk,qhe->khe", grad_scores, heads_of(queries), preferred_element_type=F32)
    return grad_queries, grad_keys.reshape(keys.shape), grad_values.reshape(values.shape)


def gelu_parts(pre):
    cdf = 0.5 * (1.0 + lax.erf(pre * 0.7071067811865476))
    pdf = jnp.exp(-0.5 * pre * pre) * 0.3989422804014327
    return (pre * cdf).astype(BF16), cdf + pre * pdf


def forward_layer(links, hidden, low_other, weights, head_b, ffn_b, rows, masks, full):
    in_low = hidden.astype(BF16)
    third = head_b[0].shape[-1]
    columns = 3 * third
    parts, near, far = [], [], []
    for g in range(2):
        weight = weights[0][g]
        projected = dot(in_low, weight[:, :columns], NN)
        queries = ((projected[:, :third] + head_b[g][0]) * 0.125).astype(BF16)
        keys = projected[:, third : 2 * third].astype(BF16)
        values = (projected[:, 2 * third :] + head_b[g][1]).astype(BF16)
        near.append((queries, keys, values))
        if low_other is not None:
            other = dot(low_other, weight[:, third:columns], NN)
            far += [other[:, :third].astype(BF16), (other[:, third:] + head_b[g][1]).astype(BF16)]
    if low_other is None:
        sent = jnp.concatenate([near[1][1][full:], near[1][2][full:], near[0][1][full:], near[0][2][full:]], axis=1)
        far = jnp.split(links.swap_x(sent), 4, axis=1)
    partial = 0.0
    for g in range(2):
        queries, keys, values = near[g]
        keys_half = jnp.concatenate([keys[full:], far[2 * g]])
        values_half = jnp.concatenate([values[full:], far[2 * g + 1]])
        context_full, probs_full = attend(queries[:full], keys[:full], values[:full], masks[0])
        context_half, probs_half = attend(queries[full:], keys_half, values_half, masks[1])
        context = jnp.concatenate([context_full, context_half])
        partial = partial + dot(context, weights[0][g][:, columns:], NT)
        parts.append((queries, keys, values, keys_half, values_half, probs_full, probs_half, context))
    attended = both_cores(links, partial) + rows[0]
    normed, scaled_one, inv_one = norm_parts(hidden + attended, rows[2], rows[3])
    normed_low = normed.astype(BF16)
    partial = 0.0
    ffn_parts = []
    wide = ffn_b[0].shape[-1]
    for g in range(2):
        weight = weights[1][g]
        activated, slope = gelu_parts(dot(normed_low, weight[:, :wide], NN) + ffn_b[g])
        partial = partial + dot(activated, weight[:, wide:], NT)
        ffn_parts.append((activated, slope))
    result, scaled_two, inv_two = norm_parts(normed + both_cores(links, partial) + rows[1], rows[4], rows[5])
    return result, (in_low, parts, scaled_one, inv_one, normed_low, ffn_parts, scaled_two, inv_two)


def backward_layer(links, grad_output, record, weights, rows, full):
    in_low, parts, scaled_one, inv_one, normed_low, ffn_parts, scaled_two, inv_two = record
    gain_two = jnp.sum(grad_output * scaled_two, axis=0)
    shift_two = jnp.sum(grad_output, axis=0)
    upper = norm_back(grad_output, scaled_two, inv_two, rows[4])
    upper_low = upper.astype(BF16)
    partial = 0.0
    ffn_grads, ffn_vecs = [], []
    for g in range(2):
        weight = weights[1][g]
        activated, slope = ffn_parts[g]
        wide = activated.shape[1]
        grad_pre = (dot(upper_low, weight[:, wide:], NN) * slope).astype(BF16)
        partial = partial + dot(grad_pre, weight[:, :wide], NT)
        grad_up = dot(normed_low, grad_pre, TN).astype(BF16)
        grad_down = dot(upper_low, activated, TN).astype(BF16)
        ffn_grads.append(jnp.concatenate([grad_up, grad_down], axis=1))
        ffn_vecs.append(jnp.sum(grad_pre.astype(F32), axis=0))
    grad_normed = upper + both_cores(links, partial)
    gain_one = jnp.sum(grad_normed * scaled_one, axis=0)
    shift_one = jnp.sum(grad_normed, axis=0)
    lower = norm_back(grad_normed, scaled_one, inv_one, rows[2])
    lower_low = lower.astype(BF16)
    partial = 0.0
    attn_grads, head_vecs, contexts, halves = [], [], [], []
    for g in range(2):
        queries, keys, values, keys_half, values_half, probs_full, probs_half, context = parts[g]
        grad_context = dot(lower_low, weights[0][g][:, 3 * queries.shape[1] :], NN).astype(BF16)
        contexts.append(grad_context)
        halves.append(attend_back(grad_context[full:], queries[full:], keys_half, values_half, probs_half))
    own = halves[0][0].shape[0]
    sent = jnp.concatenate([halves[1][1][own:], halves[1][2][own:], halves[0][1][own:], halves[0][2][own:]], axis=1)
    came = jnp.split(links.swap_x(sent.astype(BF16)).astype(F32), 4, axis=1)
    for g in range(2):
        weight = weights[0][g]
        queries, keys, values, keys_half, values_half, probs_full, probs_half, context = parts[g]
        third = queries.shape[1]
        dq_half, dk_half, dv_half = halves[g]
        dq_full, dk_full, dv_full = attend_back(
            contexts[g][:full], queries[:full], keys[:full], values[:full], probs_full
        )
        dk = jnp.concatenate([dk_full, dk_half[:own] + came[2 * g]]).astype(BF16)
        dv = jnp.concatenate([dv_full, dv_half[:own] + came[2 * g + 1]]).astype(BF16)
        grad_qkv = jnp.concatenate([jnp.concatenate([dq_full, dq_half]), dk, dv], axis=1)
        partial = partial + dot(grad_qkv, weight[:, : 3 * third], NT)
        grad_in = dot(in_low, grad_qkv, TN).astype(BF16)
        grad_out = dot(lower_low, context, TN).astype(BF16)
        attn_grads.append(jnp.concatenate([grad_in, grad_out], axis=1))
        sums = jnp.sum(grad_qkv.astype(F32), axis=0)
        head_vecs.append(jnp.stack([sums[:third], sums[2 * third :]]))
    grad_hidden = lower + both_cores(links, partial)
    row_grads = jnp.stack(
        [jnp.sum(lower, axis=0), jnp.sum(upper, axis=0), gain_one, shift_one, gain_two, shift_two]
    )
    return grad_hidden, attn_grads, ffn_grads, (head_vecs, ffn_vecs, row_grads)


def adam_step(master, moment, second, gradient, step_rate, decay_rate):
    correction = 1.0 - 0.5**ADAM_STEP
    moment_new = 0.5 * moment + 0.5 * gradient
    second_new = 0.5 * second + 0.5 * gradient * gradient
    update = (
        moment_new / correction / (jnp.sqrt(second_new / correction) + EPS_ADAM)
        + decay_rate * master
    )
    return (master - step_rate * update, moment_new, second_new)


def to_groups(vector, at, count):
    zeros = jnp.zeros(vector.shape[:-1] + (count, vector.shape[-1]), F32)
    zeros = lax.dynamic_update_index_in_dim(zeros, vector, at, axis=vector.ndim - 1)
    return zeros.reshape(vector.shape[:-1] + (-1,))


def local(n_dp, *args):
    (
        inputs,
        cotangent,
        word_lengths,
        word_count,
        attn_in,
        attn_out,
        ffn_up,
        ffn_down,
        head_bias,
        ffn_bias,
        row_params,
    ) = args[:11]
    moments, seconds = args[11:18], args[18:25]
    links = Links(n_dp)
    at_x = links.at_x
    seq_len = inputs.shape[0] // word_count.shape[0]
    half = seq_len // 2
    third, wide = attn_in.shape[3], ffn_up.shape[2]
    slots = jnp.arange(word_lengths.shape[1], dtype=jnp.int32)
    used = jnp.sum(jnp.where(slots[None, :] < word_count[:, None], word_lengths, 0), axis=1)

    def own_rows(array):
        whole = lax.dynamic_slice_in_dim(array, at_x * 2 * seq_len, seq_len)
        return jnp.concatenate([whole, lax.dynamic_slice_in_dim(array, seq_len + at_x * half, half)])

    def all_rows(array):
        low = array.astype(BF16)
        other = links.swap_x(low)
        low, other = low.astype(F32), other.astype(F32)
        first = at_x == 0
        return jnp.concatenate(
            [
                jnp.where(first, low[:seq_len], other[:seq_len]),
                jnp.where(first, low[seq_len:], other[seq_len:]),
                jnp.where(first, other[seq_len:], low[seq_len:]),
                jnp.where(first, other[:seq_len], low[:seq_len]),
            ]
        )

    places = jnp.arange(half, dtype=jnp.int32)
    used_full = jnp.where(at_x == 0, used[0], used[2])
    mask_full = jnp.arange(seq_len, dtype=jnp.int32) < used_full
    mask_half = jnp.concatenate([places + at_x * half, places + (1 - at_x) * half]) < used[1]
    masks = (mask_full, mask_half)
    row_mask = jnp.concatenate([mask_full, mask_half[:half]]).astype(F32)[:, None]

    weights = []
    for layer in range(LAYERS):
        attn = jnp.concatenate([attn_in[layer, 0], attn_in[layer, 1], attn_in[layer, 2], attn_out[layer]], axis=1)
        ffn = jnp.concatenate([ffn_up[layer], ffn_down[layer]], axis=1)
        weights.append((links.gather(attn.astype(BF16)), links.gather(ffn.astype(BF16))))
    bias_far = links.swap_x(jnp.concatenate([head_bias.reshape(-1), ffn_bias.reshape(-1)]))
    head_b = (head_bias, bias_far[: head_bias.size].reshape(head_bias.shape))
    ffn_b = (ffn_bias, bias_far[head_bias.size :].reshape(ffn_bias.shape))

    hidden = own_rows(inputs)
    low_other = lax.dynamic_slice_in_dim(inputs, seq_len + (1 - at_x) * half, half).astype(BF16)
    records = []
    for layer in range(LAYERS):
        hidden, record = forward_layer(
            links,
            hidden,
            low_other if layer == 0 else None,
            weights[layer],
            [b[layer] for b in head_b],
            [b[layer] for b in ffn_b],
            row_params[layer],
            masks,
            seq_len,
        )
        records.append(record)
    encoded = all_rows(hidden)
    grad_hidden = own_rows(cotangent) * row_mask
    matrix_grads, vector_grads = [None] * LAYERS, [None] * LAYERS
    for layer in reversed(range(LAYERS)):
        grad_hidden, attn_grads, ffn_grads, vector_grads[layer] = backward_layer(
            links, grad_hidden, records[layer], weights[layer], row_params[layer], seq_len
        )
        matrix_grads[layer] = (links.scatter(*attn_grads), links.scatter(*ffn_grads))
    input_grad = all_rows(grad_hidden)

    group = at_x * 2 + links.core
    other_group = (1 - at_x) * 2 + links.core
    head_sum = jnp.stack(
        [
            to_groups(v[0][0], group, 4) + to_groups(v[0][1], other_group, 4)
            for v in vector_grads
        ]
    )
    ffn_sum = jnp.stack(
        [
            to_groups(v[1][0], group, 4) + to_groups(v[1][1], other_group, 4)
            for v in vector_grads
        ]
    )
    row_sum = jnp.where(links.core == 0, jnp.stack([v[2] for v in vector_grads]), 0.0)
    head_sum, ffn_sum, row_sum = lax.psum((head_sum, ffn_sum, row_sum), AXES)
    head_grad = lax.dynamic_slice_in_dim(head_sum, group * third, third, axis=2)
    ffn_grad = lax.dynamic_slice_in_dim(ffn_sum, group * wide, wide, axis=1)

    attn = jnp.stack([m[0] for m in matrix_grads])
    ffn = jnp.stack([m[1] for m in matrix_grads])
    gradients = (
        jnp.stack([attn[:, :, k * third : (k + 1) * third] for k in range(3)], axis=1),
        attn[:, :, 3 * third :],
        ffn[:, :, :wide],
        ffn[:, :, wide:],
        head_grad,
        ffn_grad,
        row_sum,
    )
    params = (attn_in, attn_out, ffn_up, ffn_down, head_bias, ffn_bias, row_params)
    stepped = [
        adam_step(
            params[i],
            moments[i],
            seconds[i],
            gradients[i],
            RATE_MATRIX if i < 4 else RATE_VECTOR,
            DECAY_MATRIX if i < 4 else 0.0,
        )
        for i in range(7)
    ]
    news, moms, vars_ = zip(*stepped)
    copies = tuple(news[i].astype(BF16) for i in range(4))
    return (encoded, input_grad) + news + moms + vars_ + copies


def solution(mesh):
    n_dp = mesh.shape["dp"]
    row = P("dp", None)
    state = (
        P(None, None, "dp", "mp"),
        P(None, "dp", "mp"),
        P(None, "dp", "mp"),
        P(None, "dp", "mp"),
        P(None, None, "mp"),
        P(None, "mp"),
        P(),
    )

    def step(*args):
        return local(n_dp, *args)

    return jax.shard_map(
        step,
        mesh=mesh,
        in_specs=(row, row, row, P("dp")) + state * 3,
        out_specs=(row, row) + state * 3 + state[:4],
        check_vma=False,
    )
```

```python
import functools

import jax
import jax.numpy as jnp
from jax import lax
from jax.experimental import pallas as pl
from jax.experimental.pallas import tpu as pltpu
from jax.sharding import PartitionSpec as P

HEAD_DIM = 64
LAYERS = 2
ADAM_STEP = 10

EPS_NORM = 1e-12
EPS_ADAM = 1e-08
RATE_MATRIX = 0.04
RATE_VECTOR = 0.3
DECAY_MATRIX = 0.01

F32 = jnp.float32
BF16 = jnp.bfloat16
AXES = ("dp", "mp")
NN = ((1,), (0,))
NT = ((1,), (1,))
TN = ((0,), (0,))


def dot(a, b, dims):
    return lax.dot_general(a, b, (dims, ((), ())), preferred_element_type=F32)


def tie(*arrays):
    return lax.optimization_barrier(arrays)


class Links:
    def __init__(self, n_dp):
        self.n_dp = n_dp
        self.count = n_dp * 4
        self.bits = n_dp.bit_length() - 1
        dp_at = lax.axis_index("dp")
        mp_at = lax.axis_index("mp")
        self.at_x = mp_at // 2
        self.core = mp_at % 2
        self.at_y = dp_at % 2
        self.dp_at = dp_at
        self.places = jnp.stack([self.core, self.at_y]).astype(jnp.int32)

    def swap(self, array, mask0, mask1=None):
        mask1 = mask0 if mask1 is None else mask1
        pairs = [(i, i ^ (mask1 if i & 1 else mask0)) for i in range(self.count)]
        return lax.ppermute(array, AXES, pairs)

    def swap_core(self, array):
        return self.swap(array, 1)

    def swap_x(self, array):
        return self.swap(array, 2)

    def gather_bit(self, block, bit):
        other = self.swap(block, 4 << bit)
        mine = ((self.dp_at >> bit) & 1) == 0
        return jnp.concatenate([jnp.where(mine, block, other), jnp.where(mine, other, block)])

    def gather_rest(self, block):
        for bit in range(2, self.bits):
            block = self.gather_bit(block, bit)
        return block

    def gather_near(self, block):
        return self.swap(block, 4, 2)

    def gather_far(self, block, near):
        far = self.swap(jnp.stack([block, near]), 2, 4)
        first = self.core == 0
        own_far = jnp.where(first, near, far[0])
        other_near = jnp.where(first, far[0], near)
        return self.rows(block, own_far), self.rows(other_near, far[1])

    def rows(self, same, other):
        low = self.at_y == 0
        both = jnp.stack([jnp.where(low, same, other), jnp.where(low, other, same)], axis=1)
        return both.reshape(-1, both.shape[-1])

    def scatter_first(self, keep, give):
        came = self.swap(give, 2, 4)
        return keep[0].astype(F32) + came[0].astype(F32), (keep[1].astype(F32) + came[1].astype(F32)).astype(BF16)

    def scatter_second(self, keep, give):
        return keep + self.swap(give, 4, 2).astype(F32)

    def scatter_bit(self, keep, bit):
        half = keep.shape[0] // 2
        mine = ((self.dp_at >> bit) & 1) == 0
        give = jnp.where(mine, keep[half:], keep[:half]).astype(BF16)
        keep = jnp.where(mine, keep[:half], keep[half:])
        return keep + self.swap(give, 4 << bit).astype(F32)

    def scatter_rest_from(self, keep, top):
        for bit in reversed(range(1, top + 1)):
            keep = self.scatter_bit(keep, bit)
        return keep[0]

    def scatter_rest(self, keep):
        return self.scatter_rest_from(keep, self.bits - 1)

def norm_parts(residual, gain_row, shift_row):
    center = residual - jnp.mean(residual, axis=-1, keepdims=True)
    inv_std = lax.rsqrt(jnp.mean(center * center, axis=-1, keepdims=True) + EPS_NORM)
    scaled = center * inv_std
    return (scaled * gain_row + shift_row, scaled, inv_std)


def norm_back(grad_output, scaled, inv_std, gain_row):
    upstream = grad_output * gain_row
    mean_up = jnp.mean(upstream, axis=-1, keepdims=True)
    mean_cross = jnp.mean(upstream * scaled, axis=-1, keepdims=True)
    return inv_std * (upstream - mean_up - scaled * mean_cross)


def adam_step(master, moment, second, gradient, step_rate, decay_rate):
    correction = 1.0 - 0.5**ADAM_STEP
    moment_new = 0.5 * moment + 0.5 * gradient
    second_new = 0.5 * second + 0.5 * gradient * gradient
    update = (
        moment_new / correction / (jnp.sqrt(second_new / correction) + EPS_ADAM)
        + decay_rate * master
    )
    return (master - step_rate * update, moment_new, second_new)


def key_bias(limit, count, lanes):
    places = lax.broadcasted_iota(jnp.int32, (count, lanes), 0)
    return jnp.where(places < limit, 0.0, -1000000000.0)


def head_parts(qkv, far, swapped, g, h, full):
    third = qkv[g].shape[1] // 3
    k_at, v_at = third + h * HEAD_DIM, 2 * third + h * HEAD_DIM
    f_at = (g ^ swapped) * 2 * third + h * HEAD_DIM
    keys = qkv[g][:full, k_at : k_at + HEAD_DIM]
    values = qkv[g][:full, v_at : v_at + HEAD_DIM]
    keys_half = jnp.concatenate([qkv[g][full:, k_at : k_at + HEAD_DIM], far[:, f_at : f_at + HEAD_DIM]])
    f_at += third
    values_half = jnp.concatenate([qkv[g][full:, v_at : v_at + HEAD_DIM], far[:, f_at : f_at + HEAD_DIM]])
    return keys, values, keys_half, values_half


def fill_bias(limits, bias, full, half):
    bias[0] = key_bias(limits[0], full, half)
    bias[1, :half] = key_bias(limits[1], half, half)
    bias[1, half:] = key_bias(limits[2], half, half)


def attend_unit(keys, values, queries, bias_rows):
    scores = dot(keys, queries, NT) + bias_rows
    peak = jnp.max(scores, axis=0, keepdims=True)
    shifted = jnp.exp(scores - peak)
    total = jnp.sum(shifted, axis=0, keepdims=True)
    probs = (shifted * (1.0 / total)).astype(BF16)
    return dot(values, probs, TN), peak + jnp.log(total)


def full_kernel(limits, qkv0, qkv1, ctx0, ctx1, lse, bias):
    qkv, ctx = (qkv0, qkv1), (ctx0, ctx1)
    full, half = bias.shape
    third = qkv0.shape[1] // 3
    heads = third // HEAD_DIM
    bias[...] = key_bias(limits[0], full, half)
    for g in range(2):
        outs = [[], []]
        for h in range(heads):
            columns = slice(h * HEAD_DIM, (h + 1) * HEAD_DIM)
            keys = qkv[g][:full, third + h * HEAD_DIM : third + (h + 1) * HEAD_DIM]
            values = qkv[g][:full, 2 * third + h * HEAD_DIM : 2 * third + (h + 1) * HEAD_DIM]
            for part in range(2):
                rows = slice(part * half, (part + 1) * half)
                out, log_total = attend_unit(keys, values, qkv[g][rows, columns], bias[...])
                lse[g * heads + h : g * heads + h + 1, rows] = log_total
                outs[part].append(out)
        for part in range(2):
            rows = slice(part * half, (part + 1) * half)
            ctx[g][rows, :] = jnp.concatenate(outs[part], axis=0).T.astype(BF16)


def half_kernel(swapped, limits, qkv0, qkv1, far, _a, _b, _c, ctx0, ctx1, lse, bias):
    qkv, ctx = (qkv0, qkv1), (ctx0, ctx1)
    half = far.shape[0]
    full = 2 * half
    heads = qkv0.shape[1] // 3 // HEAD_DIM
    bias[:half] = key_bias(limits[1], half, half)
    bias[half:] = key_bias(limits[2], half, half)
    for g in range(2):
        outs = []
        for h in range(heads):
            _, _, keys, values = head_parts(qkv, far, swapped, g, h, full)
            columns = slice(h * HEAD_DIM, (h + 1) * HEAD_DIM)
            out, log_total = attend_unit(keys, values, qkv[g][full:, columns], bias[...])
            lse[g * heads + h : g * heads + h + 1, :] = log_total
            outs.append(out)
        ctx[g][...] = jnp.concatenate(outs, axis=0).T.astype(BF16)


def attend_back_unit(keys, values, queries, grad_rows, log_total, bias_rows):
    probs = jnp.exp(dot(keys, queries, NT) + bias_rows - log_total)
    grad_probs = dot(values, grad_rows, NT)
    inner = jnp.sum(probs * grad_probs, axis=0, keepdims=True)
    grad_scores = (probs * (grad_probs - inner)).astype(BF16)
    grad_values = dot(probs.astype(BF16), grad_rows, NN)
    grad_keys = dot(grad_scores, queries, NN)
    grad_queries = dot(keys, grad_scores, TN)
    return grad_queries, grad_keys, grad_values


def half_back_kernel(swapped, limits, qkv0, qkv1, far, dctx0, dctx1, lse, dq0, dq1, own, sent, bias):
    qkv, dctx, dq = (qkv0, qkv1), (dctx0, dctx1), (dq0, dq1)
    half = far.shape[0]
    full = 2 * half
    third = qkv0.shape[1] // 3
    heads = third // HEAD_DIM
    fill_bias(limits, bias, full, half)
    for g in range(2):
        queries_out, keys_out, values_out = [], [], []
        for h in range(heads):
            _, _, keys, values = head_parts(qkv, far, swapped, g, h, full)
            columns = slice(h * HEAD_DIM, (h + 1) * HEAD_DIM)
            gq, gk, gv = attend_back_unit(
                keys,
                values,
                qkv[g][full:, columns],
                dctx[g][full:, columns],
                lse[g * heads + h : g * heads + h + 1, full:],
                bias[1],
            )
            queries_out.append(gq)
            keys_out.append(gk)
            values_out.append(gv)
        dq[g][...] = jnp.concatenate(queries_out, axis=0).T.astype(BF16) * 0.125
        both = jnp.concatenate(keys_out + values_out, axis=1)
        own[:, 2 * third * g : 2 * third * (g + 1)] = both[:half]
        other = 1 - g
        sent[:, 2 * third * other : 2 * third * (other + 1)] = both[half:].astype(BF16)


def full_back_kernel(limits, qkv0, qkv1, dctx0, dctx1, lse, dqkv0, dqkv1, bias):
    qkv, dctx, dqkv = (qkv0, qkv1), (dctx0, dctx1), (dqkv0, dqkv1)
    full = qkv0.shape[0] * 2 // 3
    half = full // 2
    third = qkv0.shape[1] // 3
    heads = third // HEAD_DIM
    bias[...] = key_bias(limits[0], full, half)
    for g in range(2):
        queries_out, keys_out, values_out = [[], []], [], []
        for h in range(heads):
            columns = slice(h * HEAD_DIM, (h + 1) * HEAD_DIM)
            keys = qkv[g][:full, third + h * HEAD_DIM : third + (h + 1) * HEAD_DIM]
            values = qkv[g][:full, 2 * third + h * HEAD_DIM : 2 * third + (h + 1) * HEAD_DIM]
            sums = None
            for part in range(2):
                rows = slice(part * half, (part + 1) * half)
                gq, gk, gv = attend_back_unit(
                    keys,
                    values,
                    qkv[g][rows, columns],
                    dctx[g][rows, columns],
                    lse[g * heads + h : g * heads + h + 1, rows],
                    bias[...],
                )
                queries_out[part].append(gq)
                sums = (gk, gv) if sums is None else (sums[0] + gk, sums[1] + gv)
            keys_out.append(sums[0].astype(BF16))
            values_out.append(sums[1].astype(BF16))
        for part in range(2):
            rows = slice(part * half, (part + 1) * half)
            dqkv[g][rows, :third] = jnp.concatenate(queries_out[part], axis=0).T.astype(BF16) * 0.125
        dqkv[g][:full, third:] = jnp.concatenate(keys_out + values_out, axis=1)


def half_fill_kernel(dq0, dq1, own, came, _a, _b, dqkv0, dqkv1):
    half = own.shape[0]
    full = 2 * half
    third = dq0.shape[1]
    for g, (dq, dqkv) in enumerate(((dq0, dqkv0), (dq1, dqkv1))):
        columns = slice(2 * third * g, 2 * third * (g + 1))
        both = (own[:, columns] + came[:, columns].astype(F32)).astype(BF16)
        dqkv[...] = jnp.concatenate([dq[...], both], axis=1)


VMEM = pl.BlockSpec(memory_space=pltpu.VMEM)
SMEM = pl.BlockSpec(memory_space=pltpu.SMEM)
ROOM = pltpu.CompilerParams(vmem_limit_bytes=32 * 1024 * 1024)


def call(kernel, outs, ins, scratch=()):
    specs = [SMEM if a.dtype == jnp.int32 else VMEM for a in ins]
    return pl.pallas_call(
        kernel,
        out_shape=[jax.ShapeDtypeStruct(s, d) for s, d in outs],
        in_specs=specs,
        out_specs=[VMEM] * len(outs),
        scratch_shapes=list(scratch),
        compiler_params=ROOM,
    )(*ins)


def attend_full(limits, qkv):
    tokens, third = qkv[0].shape[0], qkv[0].shape[1] // 3
    half = tokens // 3
    ctx0, ctx1, lse = call(
        full_kernel,
        [((tokens, third), BF16)] * 2 + [((2 * third // HEAD_DIM, tokens), F32)],
        (limits, *qkv),
        [pltpu.VMEM((2 * half, half), F32)],
    )
    return (ctx0, ctx1), lse


def attend_half(limits, qkv, far, ctx, lse, swapped):
    half, third = far.shape[0], ctx[0].shape[1]
    rows = pl.BlockSpec((half, third), lambda i: (2, 0))
    ctx0, ctx1, lse = pl.pallas_call(
        functools.partial(half_kernel, swapped),
        grid=(1,),
        out_shape=[jax.ShapeDtypeStruct(a.shape, a.dtype) for a in (*ctx, lse)],
        in_specs=[SMEM] + [VMEM] * 3 + [pl.BlockSpec(memory_space=pl.ANY)] * 3,
        out_specs=[rows, rows, pl.BlockSpec((lse.shape[0], half), lambda i: (0, 2))],
        scratch_shapes=[pltpu.VMEM((2 * half, half), F32)],
        input_output_aliases={4: 0, 5: 1, 6: 2},
        compiler_params=ROOM,
    )(limits, *qkv, far, *ctx, lse)
    return (ctx0, ctx1), lse


def attend_half_back(limits, qkv, far, dctx, lse, swapped):
    half, third = far.shape[0], qkv[0].shape[1] // 3
    dq0, dq1, own, sent = call(
        functools.partial(half_back_kernel, swapped),
        [((half, third), BF16)] * 2 + [((half, 4 * third), F32), ((half, 4 * third), BF16)],
        (limits, *qkv, far, *dctx, lse),
        [pltpu.VMEM((2, 2 * half, half), F32)],
    )
    return (dq0, dq1), own, sent


def attend_full_back(limits, qkv, dctx, lse):
    half = qkv[0].shape[0] // 3
    return call(
        full_back_kernel,
        [(qkv[0].shape, BF16)] * 2,
        (limits, *qkv, *dctx, lse),
        [pltpu.VMEM((2 * half, half), F32)],
    )


def fill_half(dqkv, dq, own, came):
    tokens, columns = dqkv[0].shape
    half = own.shape[0]
    rows = pl.BlockSpec((half, columns), lambda i: (2, 0))
    return pl.pallas_call(
        half_fill_kernel,
        grid=(1,),
        out_shape=[jax.ShapeDtypeStruct(d.shape, d.dtype) for d in dqkv],
        in_specs=[VMEM] * 4 + [pl.BlockSpec(memory_space=pl.ANY)] * 2,
        out_specs=[rows] * 2,
        input_output_aliases={4: 0, 5: 1},
        compiler_params=ROOM,
    )(*dq, own, came, *dqkv)

def wgrad_kernel(count, places, *refs):
    lefts, rights = refs[:count], (refs[count : 2 * count], refs[2 * count : 3 * count])
    keep, give, whole = refs[3 * count :]
    first, at_y = places[0] == 0, places[1]
    blocks, rows = keep.shape[1], keep.shape[2]
    turned = [left[...].T for left in lefts]
    for g in range(2):
        at = 0
        for left, right in zip(turned, rights[g]):
            wide = right.shape[1]
            whole[:, at : at + wide] = dot(left, right[...], NN).astype(BF16)
            at += wide
        for y in range(2):
            same = at_y == y
            if g == 0:
                targets = ((same, keep, 0), (~same & first, keep, 1), (~same & ~first, give, 0))
            else:
                targets = ((same & first, give, 0), (same & ~first, keep, 1), (~same, give, 1))
            for when, ref, slot in targets:

                @pl.when(when)
                def _(ref=ref, slot=slot, y=y):
                    for z in range(blocks):
                        ref[slot, z] = whole[(2 * z + y) * rows : (2 * z + y + 1) * rows, :]


def weight_grads(links, lefts, rights):
    features = lefts[0].shape[1]
    columns = sum(r.shape[1] for r in rights[0])
    blocks = links.n_dp // 2
    rows = features // links.n_dp
    if rows % 16 == 0:
        return call(
            functools.partial(wgrad_kernel, len(lefts)),
            [((2, blocks, rows, columns), BF16)] * 2,
            (links.places, *lefts, *rights[0], *rights[1]),
            [pltpu.VMEM((features, columns), BF16)],
        )
    low, first = links.at_y == 0, links.core == 0
    parts = []
    for group in rights:
        grad = jnp.concatenate([dot(a, b, TN) for a, b in zip(lefts, group)], axis=1).astype(BF16)
        grad = grad.reshape(blocks, 2, rows, columns)
        parts += [jnp.where(low, grad[:, 0], grad[:, 1]), jnp.where(low, grad[:, 1], grad[:, 0])]
    own_same, own_far, other_same, other_far = parts
    keep = jnp.stack([own_same, jnp.where(first, own_far, other_same)])
    return keep, jnp.stack([jnp.where(first, other_same, own_far), other_far])

def both_cores(links, partial):
    low = partial.astype(BF16)
    return low.astype(F32) + links.swap_core(low).astype(F32)


def gelu_parts(pre):
    cdf = 0.5 * (1.0 + lax.erf(pre * 0.7071067811865476))
    pdf = jnp.exp(-0.5 * pre * pre) * 0.3989422804014327
    return (pre * cdf).astype(BF16), cdf + pre * pdf


def project(low, weight, bias, scale):
    return ((dot(low, weight, NN) + bias) * scale).astype(BF16)


def up_part(normed_low, weights, ffn_b):
    wide = ffn_b[0].shape[-1]
    return [gelu_parts(dot(normed_low, weights[g][:, :wide], NN) + ffn_b[g]) for g in range(2)]


def down_part(ffn_parts, weights):
    wide = ffn_parts[0][0].shape[1]
    return sum(dot(ffn_parts[g][0], weights[g][:, wide:], NT) for g in range(2))


def local(n_dp, *args):
    (
        inputs,
        cotangent,
        word_lengths,
        word_count,
        attn_in,
        attn_out,
        ffn_up,
        ffn_down,
        head_bias,
        ffn_bias,
        row_params,
    ) = args[:11]
    moments, seconds = args[11:18], args[18:25]
    links = Links(n_dp)
    at_x, core = links.at_x, links.core
    seq_len = inputs.shape[0] // word_count.shape[0]
    half = seq_len // 2
    third, wide = attn_in.shape[3], ffn_up.shape[2]

    def own_rows(array):
        whole = lax.dynamic_slice_in_dim(array, at_x * 2 * seq_len, seq_len)
        return jnp.concatenate([whole, lax.dynamic_slice_in_dim(array, seq_len + at_x * half, half)])

    def all_rows(array):
        low = array.astype(BF16)
        part = low.shape[0] // 2
        piece = links.swap_x(lax.dynamic_slice_in_dim(low, core * part, part))
        twin = links.swap_core(piece)
        first = core == 0
        other = jnp.concatenate([jnp.where(first, piece, twin), jnp.where(first, twin, piece)])
        low, other = low.astype(F32), other.astype(F32)
        first = at_x == 0
        return jnp.concatenate(
            [
                jnp.where(first, low[:seq_len], other[:seq_len]),
                jnp.where(first, low[seq_len:], other[seq_len:]),
                jnp.where(first, other[seq_len:], low[seq_len:]),
                jnp.where(first, other[:seq_len], low[:seq_len]),
            ]
        )

    attn_w, ffn_w = [], []
    for layer in range(LAYERS):
        attn = [attn_in[layer, 0], attn_in[layer, 1], attn_in[layer, 2], attn_out[layer]]
        attn_w.append(jnp.concatenate(attn, axis=1).astype(BF16)[None])
        ffn_w.append(jnp.concatenate([ffn_up[layer], ffn_down[layer]], axis=1).astype(BF16)[None])
    a0 = links.gather_bit(attn_w[0], 1)
    a0, f0 = tie(a0, ffn_w[0])
    f0 = links.gather_bit(f0, 1)
    a0 = links.gather_rest(a0)
    a0, f0, a1, f1 = tie(a0, f0, attn_w[1], ffn_w[1])
    near = links.gather_near(a0)
    f0 = links.gather_rest(f0)
    a1 = links.gather_bit(a1, 1)
    a0 = links.gather_far(a0, near)

    bias_far = links.swap_x(jnp.concatenate([head_bias.reshape(-1), ffn_bias.reshape(-1)]))
    head_b = (head_bias, bias_far[: head_bias.size].reshape(head_bias.shape))
    ffn_b = (ffn_bias, bias_far[head_bias.size :].reshape(ffn_bias.shape))
    zeros = jnp.zeros((third,), F32)
    qkv_b = [[jnp.concatenate([b[layer, 0], zeros, b[layer, 1]]) for b in head_b] for layer in range(LAYERS)]
    scale = jnp.concatenate([jnp.full((third,), 0.125, F32), jnp.ones((2 * third,), F32)])

    slots = jnp.arange(word_lengths.shape[1], dtype=jnp.int32)
    used = jnp.sum(jnp.where(slots[None, :] < word_count[:, None], word_lengths, 0), axis=1)
    used_full = jnp.where(at_x == 0, used[0], used[2])
    limits = jnp.stack([used_full, used[1] - at_x * half, used[1] - (1 - at_x) * half]).astype(jnp.int32)
    places = jnp.arange(seq_len, dtype=jnp.int32)
    row_mask = jnp.concatenate([places < limits[0], places[:half] < limits[1]]).astype(F32)[:, None]

    hidden = own_rows(inputs)
    low_other = lax.dynamic_slice_in_dim(inputs, seq_len + (1 - at_x) * half, half).astype(BF16)
    in_low = [hidden.astype(BF16), None]
    qkv, far, ctx, lse = [None] * 2, [None] * 2, [None] * 2, [None] * 2
    weight_a, weight_f = [a0, None], [None, None]

    def qkv_of(layer):
        return [
            project(in_low[layer], weight_a[layer][g][:, : 3 * third], qkv_b[layer][g], scale) for g in range(2)
        ]

    def out_part(layer):
        return sum(dot(ctx[layer][g], weight_a[layer][g][:, 3 * third :], NT) for g in range(2))

    norms = [None] * 2
    ffn_parts = [None] * 2

    qkv[0] = qkv_of(0)
    far[0] = jnp.concatenate(
        [
            (dot(low_other, a0[g][:, third : 3 * third], NN) + qkv_b[0][g][third:]).astype(BF16)
            for g in range(2)
        ],
        axis=1,
    )
    ctx[0], lse[0] = attend_full(limits, qkv[0])
    ctx[0], lse[0] = attend_half(limits, qkv[0], far[0], ctx[0], lse[0], 0)
    c0, c1, f0, a1 = tie(*ctx[0], f0, a1)
    ctx[0] = (c0, c1)
    near = links.gather_near(f0)
    a1 = links.gather_rest(a1)
    f1 = links.gather_bit(f1, 1)
    attended = both_cores(links, out_part(0)) + row_params[0, 0]
    normed, scaled_one, inv_one = norm_parts(hidden + attended, row_params[0, 2], row_params[0, 3])
    normed, near, a1, f1 = tie(normed, near, a1, f1)
    f0 = links.gather_far(f0, near)
    near = links.gather_near(a1)
    f1 = links.gather_rest(f1)
    weight_f[0] = f0
    normed_low = normed.astype(BF16)
    ffn_parts[0] = up_part(normed_low, f0, [b[0] for b in ffn_b])
    act, near, f1 = tie(ffn_parts[0][0][0], near, f1)
    ffn_parts[0][0] = (act, ffn_parts[0][0][1])
    a1 = links.gather_far(a1, near)
    weight_a[1] = a1
    near = links.gather_near(f1)
    fed = both_cores(links, down_part(ffn_parts[0], f0)) + row_params[0, 1]
    hidden, scaled_two, inv_two = norm_parts(normed + fed, row_params[0, 4], row_params[0, 5])
    norms[0] = (normed_low, scaled_one, inv_one, scaled_two, inv_two)

    in_low[1] = hidden.astype(BF16)
    qkv[1] = qkv_of(1)
    q0, q1, near = tie(*qkv[1], near)
    qkv[1] = [q0, q1]
    f1 = links.gather_far(f1, near)
    weight_f[1] = f1
    far[1] = links.swap_x(jnp.concatenate([q0[seq_len:, third:], q1[seq_len:, third:]], axis=1))
    ctx[1], lse[1] = attend_full(limits, qkv[1])
    ctx[1], lse[1] = attend_half(limits, qkv[1], far[1], ctx[1], lse[1], 1)
    attended = both_cores(links, out_part(1)) + row_params[1, 0]
    normed, scaled_one, inv_one = norm_parts(hidden + attended, row_params[1, 2], row_params[1, 3])
    normed_low = normed.astype(BF16)
    ffn_parts[1] = up_part(normed_low, f1, [b[1] for b in ffn_b])
    fed = both_cores(links, down_part(ffn_parts[1], f1)) + row_params[1, 1]
    hidden, scaled_two, inv_two = norm_parts(normed + fed, row_params[1, 4], row_params[1, 5])
    norms[1] = (normed_low, scaled_one, inv_one, scaled_two, inv_two)
    encoded = all_rows(hidden)

    def ffn_back(layer, grad_output):
        normed_low, _, _, scaled_two, inv_two = norms[layer]
        upper = norm_back(grad_output, scaled_two, inv_two, row_params[layer, 4])
        upper_low = upper.astype(BF16)
        grad_pre = [
            (dot(upper_low, weight_f[layer][g][:, wide:], NN) * ffn_parts[layer][g][1]).astype(BF16) for g in range(2)
        ]
        partial = sum(dot(grad_pre[g], weight_f[layer][g][:, :wide], NT) for g in range(2))
        grad_normed = upper + both_cores(links, partial)
        pieces = weight_grads(
            links,
            (normed_low, upper_low),
            [(grad_pre[g], ffn_parts[layer][g][0]) for g in range(2)],
        )
        vectors = (
            jnp.sum(upper, axis=0),
            jnp.sum(grad_output * scaled_two, axis=0),
            jnp.sum(grad_output, axis=0),
            [jnp.sum(p.astype(F32), axis=0) for p in grad_pre],
        )
        return grad_normed, pieces, vectors

    def attn_back(layer, grad_normed, hook):
        _, scaled_one, inv_one, _, _ = norms[layer]
        lower = norm_back(grad_normed, scaled_one, inv_one, row_params[layer, 2])
        lower_low = lower.astype(BF16)
        weight = weight_a[layer]
        dctx = [dot(lower_low, weight[g][:, 3 * third :], NN).astype(BF16) for g in range(2)]
        swapped = layer
        dq, own, sent = attend_half_back(limits, qkv[layer], far[layer], dctx, lse[layer], swapped)
        came = links.swap_x(sent)
        dqkv = attend_full_back(limits, qkv[layer], dctx, lse[layer])
        dqkv = fill_half(dqkv, dq, own, came)
        dqkv = hook(dqkv)
        partial = sum(dot(dqkv[g], weight[g][:, : 3 * third], NT) for g in range(2))
        grad_hidden = lower + both_cores(links, partial)
        pieces = weight_grads(links, (in_low[layer], lower_low), [(dqkv[g], ctx[layer][g]) for g in range(2)])
        sums = [jnp.sum(d.astype(F32), axis=0) for d in dqkv]
        vectors = (
            jnp.sum(lower, axis=0),
            jnp.sum(grad_normed * scaled_one, axis=0),
            jnp.sum(grad_normed, axis=0),
            [jnp.concatenate([s[:third], s[2 * third :]]) for s in sums],
        )
        return grad_hidden, pieces, vectors

    grad_hidden = own_rows(cotangent) * row_mask
    vectors = [None, None]
    grad_normed, pieces, fvec = ffn_back(1, grad_hidden)
    state = {}

    def hook1(dqkv):
        f_keep, f_give = links.scatter_first(*pieces)
        d0, d1, f_keep, f_give = tie(*dqkv, f_keep, f_give)
        state["f1"] = links.scatter_second(f_keep, f_give)
        return [d0, d1]

    grad_hidden, a_pieces, avec = attn_back(1, grad_normed, hook1)
    vectors[1] = (fvec, avec)
    grad_hidden, f1s = tie(grad_hidden, state["f1"])
    a_keep, a_give = links.scatter_first(*a_pieces)
    grad_normed, pieces, fvec = ffn_back(0, grad_hidden)
    f1s = links.scatter_bit(f1s, links.bits - 1)
    grad_normed, a_keep, a_give, f1s = tie(grad_normed, a_keep, a_give, f1s)
    a1s = links.scatter_second(a_keep, a_give)
    f1s = links.scatter_rest_from(f1s, links.bits - 2)

    def hook0(dqkv):
        f_keep, f_give = links.scatter_first(*pieces)
        d0, d1, f_keep, f_give, a, f = tie(*dqkv, f_keep, f_give, a1s, f1s)
        state["f0"] = links.scatter_second(f_keep, f_give)
        state["a1"], state["f1"] = a, f
        return [d0, d1]

    grad_hidden, a_pieces, avec = attn_back(0, grad_normed, hook0)
    vectors[0] = (fvec, avec)
    a1s = links.scatter_rest(state["a1"])
    f1s = state["f1"]
    a_keep, a_give = links.scatter_first(*a_pieces)
    f0s = links.scatter_rest(state["f0"])
    a0s = links.scatter_rest(links.scatter_second(a_keep, a_give))
    input_grad = all_rows(grad_hidden)

    own = jnp.concatenate([v for layer in vectors for v in (layer[1][3][0], layer[0][3][0])])
    other = jnp.concatenate([v for layer in vectors for v in (layer[1][3][1], layer[0][3][1])])
    rows = jnp.concatenate(
        [
            r
            for fv, av in vectors
            for r in (av[0], fv[0], av[1], av[2], fv[1], fv[2])
        ]
    )
    came = links.swap_x(jnp.concatenate([other, rows]).reshape(-1, 128)).reshape(-1)
    sums = (jnp.concatenate([own, rows]) + came).reshape(-1, 128)
    for bit in range(links.bits):
        sums = sums + links.swap(sums, 4 << bit)
    sums = sums.reshape(-1)
    size = own.shape[0] // LAYERS
    head_grad = jnp.stack([sums[i * size : i * size + 2 * third].reshape(2, third) for i in range(LAYERS)])
    ffn_grad = jnp.stack([sums[i * size + 2 * third : (i + 1) * size] for i in range(LAYERS)])
    row_grad = sums[LAYERS * size :].reshape(row_params.shape)

    attn = jnp.stack([a0s, a1s])
    ffn = jnp.stack([f0s, f1s])
    gradients = (
        jnp.stack([attn[:, :, k * third : (k + 1) * third] for k in range(3)], axis=1),
        attn[:, :, 3 * third :],
        ffn[:, :, :wide],
        ffn[:, :, wide:],
        head_grad,
        ffn_grad,
        row_grad,
    )
    params = (attn_in, attn_out, ffn_up, ffn_down, head_bias, ffn_bias, row_params)
    stepped = [
        adam_step(
            params[i],
            moments[i],
            seconds[i],
            gradients[i],
            RATE_MATRIX if i < 4 else RATE_VECTOR,
            DECAY_MATRIX if i < 4 else 0.0,
        )
        for i in range(7)
    ]
    news, moms, vars_ = zip(*stepped)
    copies = tuple(news[i].astype(BF16) for i in range(4))
    return (encoded, input_grad) + news + moms + vars_ + copies


def solution(mesh):
    n_dp = mesh.shape["dp"]
    row = P("dp", None)
    state = (
        P(None, None, "dp", "mp"),
        P(None, "dp", "mp"),
        P(None, "dp", "mp"),
        P(None, "dp", "mp"),
        P(None, None, "mp"),
        P(None, "mp"),
        P(),
    )

    def step(*args):
        return local(n_dp, *args)

    return jax.shard_map(
        step,
        mesh=mesh,
        in_specs=(row, row, row, P("dp")) + state * 3,
        out_specs=(row, row) + state * 3 + state[:4],
        check_vma=False,
    )
```

```python
import functools

import jax
import jax.numpy as jnp
from jax import lax
from jax.experimental import pallas as pl
from jax.experimental.pallas import tpu as pltpu
from jax.sharding import PartitionSpec as P

HEAD_DIM = 64
LAYERS = 2
ADAM_STEP = 10

EPS_NORM = 1e-12
EPS_ADAM = 1e-08
RATE_MATRIX = 0.04
RATE_VECTOR = 0.3
DECAY_MATRIX = 0.01

F32 = jnp.float32
BF16 = jnp.bfloat16
AXES = ("dp", "mp")
NN = ((1,), (0,))
NT = ((1,), (1,))
TN = ((0,), (0,))


def dot(a, b, dims):
    return lax.dot_general(a, b, (dims, ((), ())), preferred_element_type=F32)


def tie(*arrays):
    return lax.optimization_barrier(arrays)


class Links:
    def __init__(self, n_dp, rows):
        self.n_dp = n_dp
        self.count = n_dp * 4
        self.z_masks = [1 << bit for bit in reversed(range(n_dp.bit_length() - 2))]
        self.order = [0]
        for mask in self.z_masks:
            self.order += [place ^ mask for place in self.order]
        self.aligned = rows % 16 == 0
        dp_at = lax.axis_index("dp")
        mp_at = lax.axis_index("mp")
        self.at_x = mp_at // 2
        self.core = mp_at % 2
        self.at_y = dp_at % 2
        self.at_z = dp_at // 2
        self.places = jnp.stack([self.core, self.at_y, self.at_z]).astype(jnp.int32)

    def swap(self, array, mask0, mask1=None):
        mask1 = mask0 if mask1 is None else mask1
        pairs = [(i, i ^ (mask1 if i & 1 else mask0)) for i in range(self.count)]
        return lax.ppermute(array, AXES, pairs)

    def swap_as(self, name, swap, *args):
        with jax.named_scope(name):
            return swap(*args)

    def swap_core(self, array):
        return self.swap(array, 1)

    def swap_x(self, array):
        return self.swap(array, 2)

    def swap_z(self, array, mask):
        return self.swap(array, 8 * mask)

    def swap_near(self, array):
        return self.swap(array, 4, 2)

    def swap_far(self, array):
        return self.swap(array, 2, 4)

    def last_z(self, block, masks):
        for mask in masks[:-1]:
            block = jnp.concatenate([block, self.swap_z(block, mask)])
        return block, self.swap_z(block, masks[-1])

    def scatter_z(self, parts, masks):
        for mask in masks[:-1]:
            half = parts.shape[0] // 2
            parts = parts[:half] + self.swap_z(parts[half:].astype(BF16), mask).astype(F32)
        half = parts.shape[0] // 2
        return parts[:half], self.swap_z(parts[half:].astype(BF16), masks[-1])

    def assemble(self, two, far):
        if self.aligned:
            shape = (far.shape[1], 2) + far.shape[2:]
            kernel = functools.partial(assemble_kernel, self.order)
            both = call(kernel, [(shape, far.dtype)] * 2, (self.places, two, far), name="assemble")
        else:
            order = jnp.array(inverse(self.order))[jnp.arange(far.shape[1]) ^ self.at_z]
            two, far = jnp.take(two, order, axis=1), jnp.take(far, order, axis=1)
            first, low = self.core == 0, self.at_y == 0
            own_far = jnp.where(first, two[1], far[0])
            other_same = jnp.where(first, far[0], two[1])
            both = [
                jnp.stack([jnp.where(low, same, other), jnp.where(low, other, same)], axis=1)
                for same, other in ((two[0], own_far), (other_same, far[1]))
            ]
        return [w.reshape(-1, w.shape[-1]) for w in both]


def inverse(order):
    return [order.index(place) for place in range(len(order))]


def assemble_kernel(order, places, two, far, own, other):
    first, at_y, at_z = places[0] == 0, places[1], places[2]
    for m, distance in enumerate(order):
        j = distance ^ at_z
        own[j, at_y] = two[0, m]
        other[j, 1 - at_y] = far[1, m]

        @pl.when(first)
        def _(j=j, m=m):
            own[j, 1 - at_y] = two[1, m]
            other[j, at_y] = far[0, m]

        @pl.when(~first)
        def _(j=j, m=m):
            own[j, 1 - at_y] = far[0, m]
            other[j, at_y] = two[1, m]


def adam_step(master, moment, second, gradient, step_rate, decay_rate):
    correction = 1.0 - 0.5**ADAM_STEP
    moment_new = 0.5 * moment + 0.5 * gradient
    second_new = 0.5 * second + 0.5 * gradient * gradient
    update = (
        moment_new / correction / (jnp.sqrt(second_new / correction) + EPS_ADAM)
        + decay_rate * master
    )
    return (master - step_rate * update, moment_new, second_new)


def key_bias(limit, count, lanes):
    places = lax.broadcasted_iota(jnp.int32, (count, lanes), 0)
    return jnp.where(places < limit, 0.0, -1000000000.0)


def head_parts(qkv, far, swapped, g, h, full):
    third = qkv[g].shape[1] // 3
    k_at, v_at = third + h * HEAD_DIM, 2 * third + h * HEAD_DIM
    f_at = (g ^ swapped) * 2 * third + h * HEAD_DIM
    keys = qkv[g][:full, k_at : k_at + HEAD_DIM]
    values = qkv[g][:full, v_at : v_at + HEAD_DIM]
    keys_half = jnp.concatenate([qkv[g][full:, k_at : k_at + HEAD_DIM], far[:, f_at : f_at + HEAD_DIM]])
    f_at += third
    values_half = jnp.concatenate([qkv[g][full:, v_at : v_at + HEAD_DIM], far[:, f_at : f_at + HEAD_DIM]])
    return keys, values, keys_half, values_half


def fill_bias(limits, bias, full, half):
    bias[0] = key_bias(limits[0], full, half)
    bias[1, :half] = key_bias(limits[1], half, half)
    bias[1, half:] = key_bias(limits[2], half, half)


def attend_unit(keys, values, queries, bias_rows):
    scores = dot(keys, queries, NT) + bias_rows
    peak = jnp.max(scores, axis=0, keepdims=True)
    shifted = jnp.exp(scores - peak)
    total = jnp.sum(shifted, axis=0, keepdims=True)
    probs = (shifted * (1.0 / total)).astype(BF16)
    return dot(values, probs, TN), peak + jnp.log(total)


def full_kernel(limits, qkv0, qkv1, ctx0, ctx1, lse, bias):
    qkv, ctx = (qkv0, qkv1), (ctx0, ctx1)
    full, half = bias.shape
    third = qkv0.shape[1] // 3
    heads = third // HEAD_DIM
    bias[...] = key_bias(limits[0], full, half)
    for g in range(2):
        outs = [[], []]
        for h in range(heads):
            columns = slice(h * HEAD_DIM, (h + 1) * HEAD_DIM)
            keys = qkv[g][:full, third + h * HEAD_DIM : third + (h + 1) * HEAD_DIM]
            values = qkv[g][:full, 2 * third + h * HEAD_DIM : 2 * third + (h + 1) * HEAD_DIM]
            for part in range(2):
                rows = slice(part * half, (part + 1) * half)
                out, log_total = attend_unit(keys, values, qkv[g][rows, columns], bias[...])
                lse[g * heads + h : g * heads + h + 1, rows] = log_total
                outs[part].append(out)
        for part in range(2):
            rows = slice(part * half, (part + 1) * half)
            ctx[g][rows, :] = jnp.concatenate(outs[part], axis=0).T.astype(BF16)


def half_kernel(swapped, limits, qkv0, qkv1, far, _a, _b, _c, ctx0, ctx1, lse, bias):
    qkv, ctx = (qkv0, qkv1), (ctx0, ctx1)
    half = far.shape[0]
    full = 2 * half
    heads = qkv0.shape[1] // 3 // HEAD_DIM
    bias[:half] = key_bias(limits[1], half, half)
    bias[half:] = key_bias(limits[2], half, half)
    for g in range(2):
        outs = []
        for h in range(heads):
            _, _, keys, values = head_parts(qkv, far, swapped, g, h, full)
            columns = slice(h * HEAD_DIM, (h + 1) * HEAD_DIM)
            out, log_total = attend_unit(keys, values, qkv[g][full:, columns], bias[...])
            lse[g * heads + h : g * heads + h + 1, :] = log_total
            outs.append(out)
        ctx[g][...] = jnp.concatenate(outs, axis=0).T.astype(BF16)


def attend_back_unit(keys, values, queries, grad_rows, log_total, bias_rows):
    probs = jnp.exp(dot(keys, queries, NT) + bias_rows - log_total)
    grad_probs = dot(values, grad_rows, NT)
    inner = jnp.sum(probs * grad_probs, axis=0, keepdims=True)
    grad_scores = (probs * (grad_probs - inner)).astype(BF16)
    grad_values = dot(probs.astype(BF16), grad_rows, NN)
    grad_keys = dot(grad_scores, queries, NN)
    grad_queries = dot(keys, grad_scores, TN)
    return grad_queries, grad_keys, grad_values


def half_back_kernel(swapped, limits, qkv0, qkv1, far, dctx0, dctx1, lse, dq0, dq1, own, sent, bias):
    qkv, dctx, dq = (qkv0, qkv1), (dctx0, dctx1), (dq0, dq1)
    half = far.shape[0]
    full = 2 * half
    third = qkv0.shape[1] // 3
    heads = third // HEAD_DIM
    fill_bias(limits, bias, full, half)
    for g in range(2):
        queries_out, keys_out, values_out = [], [], []
        for h in range(heads):
            _, _, keys, values = head_parts(qkv, far, swapped, g, h, full)
            columns = slice(h * HEAD_DIM, (h + 1) * HEAD_DIM)
            gq, gk, gv = attend_back_unit(
                keys,
                values,
                qkv[g][full:, columns],
                dctx[g][full:, columns],
                lse[g * heads + h : g * heads + h + 1, full:],
                bias[1],
            )
            queries_out.append(gq)
            keys_out.append(gk)
            values_out.append(gv)
        dq[g][...] = jnp.concatenate(queries_out, axis=0).T.astype(BF16) * 0.125
        both = jnp.concatenate(keys_out + values_out, axis=1)
        own[:, 2 * third * g : 2 * third * (g + 1)] = both[:half]
        other = 1 - g
        sent[:, 2 * third * other : 2 * third * (other + 1)] = both[half:].astype(BF16)


def full_back_kernel(limits, qkv0, qkv1, dctx0, dctx1, lse, dqkv0, dqkv1, bias):
    qkv, dctx, dqkv = (qkv0, qkv1), (dctx0, dctx1), (dqkv0, dqkv1)
    full = qkv0.shape[0] * 2 // 3
    half = full // 2
    third = qkv0.shape[1] // 3
    heads = third // HEAD_DIM
    bias[...] = key_bias(limits[0], full, half)
    for g in range(2):
        queries_out, keys_out, values_out = [[], []], [], []
        for h in range(heads):
            columns = slice(h * HEAD_DIM, (h + 1) * HEAD_DIM)
            keys = qkv[g][:full, third + h * HEAD_DIM : third + (h + 1) * HEAD_DIM]
            values = qkv[g][:full, 2 * third + h * HEAD_DIM : 2 * third + (h + 1) * HEAD_DIM]
            sums = None
            for part in range(2):
                rows = slice(part * half, (part + 1) * half)
                gq, gk, gv = attend_back_unit(
                    keys,
                    values,
                    qkv[g][rows, columns],
                    dctx[g][rows, columns],
                    lse[g * heads + h : g * heads + h + 1, rows],
                    bias[...],
                )
                queries_out[part].append(gq)
                sums = (gk, gv) if sums is None else (sums[0] + gk, sums[1] + gv)
            keys_out.append(sums[0].astype(BF16))
            values_out.append(sums[1].astype(BF16))
        for part in range(2):
            rows = slice(part * half, (part + 1) * half)
            dqkv[g][rows, :third] = jnp.concatenate(queries_out[part], axis=0).T.astype(BF16) * 0.125
        dqkv[g][:full, third:] = jnp.concatenate(keys_out + values_out, axis=1)


def half_fill_kernel(dq0, dq1, own, came, _a, _b, dqkv0, dqkv1):
    half = own.shape[0]
    full = 2 * half
    third = dq0.shape[1]
    for g, (dq, dqkv) in enumerate(((dq0, dqkv0), (dq1, dqkv1))):
        columns = slice(2 * third * g, 2 * third * (g + 1))
        both = (own[:, columns] + came[:, columns].astype(F32)).astype(BF16)
        dqkv[...] = jnp.concatenate([dq[...], both], axis=1)


VMEM = pl.BlockSpec(memory_space=pltpu.VMEM)
SMEM = pl.BlockSpec(memory_space=pltpu.SMEM)
ROOM = pltpu.CompilerParams(vmem_limit_bytes=32 * 1024 * 1024)
CHEAP = pl.CostEstimate(flops=1, bytes_accessed=1, transcendentals=0)


def call(kernel, outs, ins, scratch=(), name=None):
    specs = [SMEM if a.dtype == jnp.int32 else VMEM for a in ins]
    return pl.pallas_call(
        kernel,
        out_shape=[jax.ShapeDtypeStruct(s, d) for s, d in outs],
        in_specs=specs,
        out_specs=[VMEM] * len(outs),
        scratch_shapes=list(scratch),
        compiler_params=ROOM,
        cost_estimate=CHEAP,
        name=name,
    )(*ins)


def attend_full(limits, qkv):
    tokens, third = qkv[0].shape[0], qkv[0].shape[1] // 3
    half = tokens // 3
    ctx0, ctx1, lse = call(
        full_kernel,
        [((tokens, third), BF16)] * 2 + [((2 * third // HEAD_DIM, tokens), F32)],
        (limits, *qkv),
        [pltpu.VMEM((2 * half, half), F32)],
        name="attend_full",
    )
    return (ctx0, ctx1), lse


def attend_half(limits, qkv, far, ctx, lse, swapped):
    half, third = far.shape[0], ctx[0].shape[1]
    rows = pl.BlockSpec((half, third), lambda i: (2, 0))
    ctx0, ctx1, lse = pl.pallas_call(
        functools.partial(half_kernel, swapped),
        grid=(1,),
        out_shape=[jax.ShapeDtypeStruct(a.shape, a.dtype) for a in (*ctx, lse)],
        in_specs=[SMEM] + [VMEM] * 3 + [pl.BlockSpec(memory_space=pl.ANY)] * 3,
        out_specs=[rows, rows, pl.BlockSpec((lse.shape[0], half), lambda i: (0, 2))],
        scratch_shapes=[pltpu.VMEM((2 * half, half), F32)],
        input_output_aliases={4: 0, 5: 1, 6: 2},
        compiler_params=ROOM,
        cost_estimate=CHEAP,
        name="attend_half",
    )(limits, *qkv, far, *ctx, lse)
    return (ctx0, ctx1), lse


def attend_half_back(limits, qkv, far, dctx, lse, swapped):
    half, third = far.shape[0], qkv[0].shape[1] // 3
    dq0, dq1, own, sent = call(
        functools.partial(half_back_kernel, swapped),
        [((half, third), BF16)] * 2 + [((half, 4 * third), F32), ((half, 4 * third), BF16)],
        (limits, *qkv, far, *dctx, lse),
        [pltpu.VMEM((2, 2 * half, half), F32)],
        name="attend_half_back",
    )
    return (dq0, dq1), own, sent


def attend_full_back(limits, qkv, dctx, lse):
    half = qkv[0].shape[0] // 3
    return call(
        full_back_kernel,
        [(qkv[0].shape, BF16)] * 2,
        (limits, *qkv, *dctx, lse),
        [pltpu.VMEM((2 * half, half), F32)],
        name="attend_full_back",
    )


def fill_half(dqkv, dq, own, came):
    tokens, columns = dqkv[0].shape
    half = own.shape[0]
    rows = pl.BlockSpec((half, columns), lambda i: (2, 0))
    return pl.pallas_call(
        half_fill_kernel,
        grid=(1,),
        out_shape=[jax.ShapeDtypeStruct(d.shape, d.dtype) for d in dqkv],
        in_specs=[VMEM] * 4 + [pl.BlockSpec(memory_space=pl.ANY)] * 2,
        out_specs=[rows] * 2,
        input_output_aliases={4: 0, 5: 1},
        compiler_params=ROOM,
        cost_estimate=CHEAP,
        name="fill_half",
    )(*dq, own, came, *dqkv)

def wgrad_kernel(count, order, places, *refs):
    lefts, rights = refs[:count], (refs[count : 2 * count], refs[2 * count : 3 * count])
    keep, give, whole = refs[3 * count :]
    first, at_y, at_z = places[0] == 0, places[1], places[2]
    blocks, rows = keep.shape[1], keep.shape[2]
    turned = [left[...].T for left in lefts]
    for g in range(2):
        at = 0
        for left, right in zip(turned, rights[g]):
            wide = right.shape[1]
            whole[:, at : at + wide] = dot(left, right[...], NN).astype(BF16)
            at += wide
        for y in range(2):
            same = at_y == y
            if g == 0:
                targets = ((same, keep, 0), (~same & first, keep, 1), (~same & ~first, give, 0))
            else:
                targets = ((same & first, give, 0), (same & ~first, keep, 1), (~same, give, 1))
            for when, ref, slot in targets:

                @pl.when(when)
                def _(ref=ref, slot=slot, y=y):
                    for m, distance in enumerate(order):
                        ref[slot, m] = whole[pl.ds((2 * (distance ^ at_z) + y) * rows, rows), :]


def weight_grads(links, lefts, rights):
    features = lefts[0].shape[1]
    columns = sum(r.shape[1] for r in rights[0])
    blocks = links.n_dp // 2
    rows = features // links.n_dp
    if links.aligned:
        return call(
            functools.partial(wgrad_kernel, len(lefts), links.order),
            [((2, blocks, rows, columns), BF16)] * 2,
            (links.places, *lefts, *rights[0], *rights[1]),
            [pltpu.VMEM((features, columns), BF16)],
            name="weight_grads",
        )
    low, first = links.at_y == 0, links.core == 0
    parts = []
    for group in rights:
        grad = jnp.concatenate([dot(a, b, TN) for a, b in zip(lefts, group)], axis=1).astype(BF16)
        grad = jnp.take(grad.reshape(blocks, 2, rows, columns), jnp.array(links.order) ^ links.at_z, axis=0)
        parts += [jnp.where(low, grad[:, 0], grad[:, 1]), jnp.where(low, grad[:, 1], grad[:, 0])]
    own_same, own_far, other_same, other_far = parts
    keep = jnp.stack([own_same, jnp.where(first, own_far, other_same)])
    return keep, jnp.stack([jnp.where(first, other_same, own_far), other_far])

def both_cores(links, parts):
    return (*parts, *[links.swap_as("core", links.swap_core, part) for part in parts])


def thirds(shape):
    return [((shape[0] // 3, shape[1]), BF16)] * 3


def core_sum(parts, at, rows):
    return parts[at][rows, :].astype(F32) + parts[at + 3][rows, :].astype(F32)


def norm_kernel(step, *refs):
    parts, (residual, rows, out, low, scaled, inverse) = refs[:6], refs[6:]
    wide = out.shape[1]
    third = parts[0].shape[0]
    for part in range(3):

        @pl.loop(0, third // step)
        def _(i, part=part):
            inner = pl.ds(i * step, step)
            at = pl.ds(part * third + i * step, step)
            total = residual[at, :] + (core_sum(parts, part, inner) + rows[0:1, :])
            center = total - jnp.sum(total, axis=-1, keepdims=True) * (1.0 / wide)
            inv_std = lax.rsqrt(jnp.sum(center * center, axis=-1, keepdims=True) * (1.0 / wide) + EPS_NORM)
            normal = center * inv_std
            result = normal * rows[1:2, :] + rows[2:3, :]
            out[at, :] = result
            low[at, :] = result.astype(BF16)
            scaled[at, :] = normal
            inverse[at, :] = inv_std


def add_norm(parts, residual, rows):
    shape = residual.shape
    return call(
        functools.partial(norm_kernel, 64),
        [(shape, F32), (shape, BF16), (shape, F32), ((shape[0], 1), F32)],
        (*parts, residual, rows),
        name="add_norm",
    )


def norm_back_kernel(step, *refs):
    base, *parts, scaled, inverse, gain, out, low, sums = refs
    wide = out.shape[1]
    third = out.shape[0] // 3
    sums[...] = jnp.zeros_like(sums)
    for part in range(3):

        @pl.loop(0, third // step)
        def _(i, part=part):
            at = pl.ds(part * third + i * step, step)
            grad = base[at, :]
            if parts:
                grad = grad + core_sum(parts, part, pl.ds(i * step, step))
            normal = scaled[at, :]
            upstream = grad * gain[...]
            mean_up = jnp.sum(upstream, axis=-1, keepdims=True) * (1.0 / wide)
            mean_cross = jnp.sum(upstream * normal, axis=-1, keepdims=True) * (1.0 / wide)
            result = inverse[at, :] * (upstream - mean_up - normal * mean_cross)
            out[at, :] = result
            low[at, :] = result.astype(BF16)
            for k, term in enumerate((result, grad * normal, grad)):
                sums[8 * k : 8 * (k + 1), :] += jnp.sum(term.reshape(-1, 8, wide), axis=0)


def norm_back(parts, scaled, inverse, gain):
    shape = scaled.shape
    return call(
        functools.partial(norm_back_kernel, 64),
        [(shape, F32), (shape, BF16), ((24, shape[1]), F32)],
        (*parts, scaled, inverse, gain),
        name="norm_back",
    )


def final_sum_kernel(base, *refs):
    parts, out = refs[:6], refs[6]
    third = parts[0].shape[0]
    for part in range(3):
        at = slice(part * third, (part + 1) * third)
        out[at, :] = (base[at, :] + core_sum(parts, part, slice(None))).astype(BF16)


def chunks(count, step=256):
    return [slice(at, at + step) for at in range(0, count, step)]


def qkv_kernel(low, w0, w1, bias, *refs):
    *other, out0, out1, extra = refs
    columns = out0.shape[1]
    third = columns // 3
    half = extra.shape[0]
    scale = jnp.where(lax.broadcasted_iota(jnp.int32, (1, columns), 1) < third, 0.125, 1.0)
    for g, (weight, out) in enumerate(((w0, out0), (w1, out1))):
        at = slice(2 * third * g, 2 * third * (g + 1))
        for rows in chunks(low.shape[0]):
            out[rows, :] = ((dot(low[rows, :], weight[:, :columns], NN) + bias[g : g + 1, :]) * scale).astype(BF16)
        if other:
            more = dot(other[0][...], weight[:, :columns], NN) + bias[g : g + 1, :]
            extra[:, at] = more[:, third:].astype(BF16)
        else:
            extra[:, at] = out[2 * half :, third:]


def project(low, weights, bias, other=None):
    tokens, columns = low.shape[0], bias.shape[1]
    half = tokens // 3
    ins = (low, *weights, bias) + (() if other is None else (other,))
    q0, q1, extra = call(
        qkv_kernel,
        [((tokens, columns), BF16)] * 2 + [((half, 4 * columns // 3), BF16)],
        ins,
        name="queries_keys_values",
    )
    return [q0, q1], extra


def out_kernel(ctx0, ctx1, w0, w1, *outs):
    third = ctx0.shape[1]
    at = w0.shape[1] - third
    tails = (w0[:, at:], w1[:, at:])
    for rows, out in zip(chunks(ctx0.shape[0], outs[0].shape[0]), outs):
        out[...] = (dot(ctx0[rows, :], tails[0], NT) + dot(ctx1[rows, :], tails[1], NT)).astype(BF16)


def ffn_kernel(low, w0, w1, bias, act0, act1, slope0, slope1, *outs):
    wide = bias.shape[1]
    groups = ((w0, act0, slope0), (w1, act1, slope1))
    for at, rows in enumerate(chunks(low.shape[0], 128)):
        total = None
        for g, (weight, act, slope) in enumerate(groups):
            pre = dot(low[rows, :], weight[:, :wide], NN) + bias[g : g + 1, :]
            cdf = 0.5 * (1.0 + lax.erf(pre * 0.7071067811865476))
            slope[rows, :] = cdf + pre * (jnp.exp(-0.5 * pre * pre) * 0.3989422804014327)
            active = (pre * cdf).astype(BF16)
            act[rows, :] = active
            part = dot(active, weight[:, wide:], NT)
            total = part if total is None else total + part
        inner = slice(at % 2 * 128, (at % 2 + 1) * 128)
        outs[at // 2][inner, :] = total.astype(BF16)


def feed_forward(low, weights, bias):
    shape = (low.shape[0], bias.shape[1])
    act0, act1, slope0, slope1, *partial = call(
        ffn_kernel,
        [(shape, BF16)] * 2 + [(shape, F32)] * 2 + thirds(low.shape),
        (low, *weights, bias),
        name="feed_forward",
    )
    return [(act0, slope0), (act1, slope1)], partial


def add_rows(array):
    return jnp.sum(array.astype(F32).reshape(-1, 8, array.shape[1]), axis=0)


def ffn_back_kernel(low, w0, w1, slope0, slope1, pre0, pre1, sums):
    wide = slope0.shape[1]
    for g, (weight, slope, pre) in enumerate(((w0, slope0, pre0), (w1, slope1, pre1))):
        total = None
        for rows in chunks(low.shape[0]):
            grad = (dot(low[rows, :], weight[:, wide:], NN) * slope[rows, :]).astype(BF16)
            pre[rows, :] = grad
            part = add_rows(grad)
            total = part if total is None else total + part
        sums[8 * g : 8 * (g + 1), :] = total


def ffn_back_first(low, weights, slopes):
    shape = slopes[0].shape
    pre0, pre1, sums = call(
        ffn_back_kernel,
        [(shape, BF16)] * 2 + [((16, shape[1]), F32)],
        (low, *weights, *slopes),
        name="pre_grad",
    )
    return [pre0, pre1], sums


def back_out_kernel(d0, d1, w0, w1, *outs):
    wide = d0.shape[1]
    for rows, out in zip(chunks(d0.shape[0], outs[0].shape[0]), outs):
        out[...] = (dot(d0[rows, :], w0[:, :wide], NT) + dot(d1[rows, :], w1[:, :wide], NT)).astype(BF16)


def qkv_back_kernel(d0, d1, w0, w1, *refs):
    *outs, sums = refs
    back_out_kernel(d0, d1, w0, w1, *outs)
    for g, d in enumerate((d0, d1)):
        total = None
        for rows in chunks(d.shape[0]):
            part = add_rows(d[rows, :])
            total = part if total is None else total + part
        sums[8 * g : 8 * (g + 1), :] = total


def context_grad_kernel(low, w0, w1, out0, out1):
    third = out0.shape[1]
    at = w0.shape[1] - third
    for weight, out in ((w0, out0), (w1, out1)):
        tail = weight[:, at:]
        for rows in chunks(low.shape[0]):
            out[rows, :] = dot(low[rows, :], tail, NN).astype(BF16)


def local(n_dp, *args):
    (
        inputs,
        cotangent,
        word_lengths,
        word_count,
        attn_in,
        attn_out,
        ffn_up,
        ffn_down,
        head_bias,
        ffn_bias,
        row_params,
    ) = args[:11]
    moments, seconds = args[11:18], args[18:25]
    links = Links(n_dp, attn_out.shape[1])
    at_x, core = links.at_x, links.core
    seq_len = inputs.shape[0] // word_count.shape[0]
    half = seq_len // 2
    third, wide = attn_in.shape[3], ffn_up.shape[2]

    def own_rows(array):
        whole = lax.dynamic_slice_in_dim(array, at_x * 2 * seq_len, seq_len)
        return jnp.concatenate([whole, lax.dynamic_slice_in_dim(array, seq_len + at_x * half, half)])

    def rows_first(low):
        part = low.shape[0] // 2
        return links.swap_as("rows_x", links.swap_x, lax.dynamic_slice_in_dim(low, core * part, part))

    def rows_second(piece):
        return links.swap_as("rows_core", links.swap_core, piece)

    def all_rows(low, piece, twin):
        first = core == 0
        other = jnp.concatenate([jnp.where(first, piece, twin), jnp.where(first, twin, piece)])
        low, other = low.astype(F32), other.astype(F32)
        first = at_x == 0
        return jnp.concatenate(
            [
                jnp.where(first, low[:seq_len], other[:seq_len]),
                jnp.where(first, low[seq_len:], other[seq_len:]),
                jnp.where(first, other[seq_len:], low[seq_len:]),
                jnp.where(first, other[:seq_len], low[:seq_len]),
            ]
        )

    def packed_attn(layer):
        attn = [attn_in[layer, 0], attn_in[layer, 1], attn_in[layer, 2], attn_out[layer]]
        return jnp.concatenate([a.astype(BF16) for a in attn], axis=1)[None]

    def packed_ffn(layer):
        return jnp.concatenate([ffn_up[layer].astype(BF16), ffn_down[layer].astype(BF16)], axis=1)[None]

    z_one, z_rest = links.z_masks[:1], links.z_masks[1:]
    join = jnp.concatenate

    a0 = packed_attn(0)
    a0_in = links.swap_as("attn0_z2", links.swap_z, a0, links.z_masks[0])
    a0_in, f0, later = tie(a0_in, packed_ffn(0), join([packed_attn(1), packed_ffn(1)], axis=2))
    a0 = join([a0, a0_in])
    a0, a0_in = links.swap_as("attn0_z1", links.last_z, a0, z_rest)
    f0_in = links.swap_as("ffn0_z2", links.swap_z, f0, links.z_masks[0])
    a0_in, f0_in, later = tie(a0_in, f0_in, later)
    a0, f0 = join([a0, a0_in]), join([f0, f0_in])
    near = links.swap_as("attn0_near", links.swap_near, a0)
    f0, f0_in = links.swap_as("ffn0_z1", links.last_z, f0, z_rest)
    later_in = links.swap_as("layer1_z2", links.swap_z, later, links.z_masks[0])
    biases = jnp.concatenate([head_bias.reshape(-1), ffn_bias.reshape(-1)])
    near, biases = tie(near, biases)
    two = jnp.stack([a0, near])
    far_part = links.swap_as("attn0_far", links.swap_far, two)
    bias_far = links.swap_as("biases", links.swap_x, biases)
    far_part, bias_far, later_in = tie(far_part, bias_far, later_in)
    later = join([later, later_in])
    a0 = links.assemble(two, far_part)
    head_b = (head_bias, bias_far[: head_bias.size].reshape(head_bias.shape))
    ffn_b = (ffn_bias, bias_far[head_bias.size :].reshape(ffn_bias.shape))
    zeros = jnp.zeros((third,), F32)
    qkv_b = [
        jnp.stack([jnp.concatenate([b[layer, 0], zeros, b[layer, 1]]) for b in head_b]) for layer in range(LAYERS)
    ]
    ffn_b = [jnp.stack([b[layer] for b in ffn_b]) for layer in range(LAYERS)]

    slots = jnp.arange(word_lengths.shape[1], dtype=jnp.int32)
    used = jnp.sum(jnp.where(slots[None, :] < word_count[:, None], word_lengths, 0), axis=1)
    used_full = jnp.where(at_x == 0, used[0], used[2])
    limits = jnp.stack([used_full, used[1] - at_x * half, used[1] - (1 - at_x) * half]).astype(jnp.int32)
    places = jnp.arange(seq_len, dtype=jnp.int32)
    row_mask = jnp.concatenate([places < limits[0], places[:half] < limits[1]]).astype(F32)[:, None]

    hidden = own_rows(inputs)
    low_other = lax.dynamic_slice_in_dim(inputs, seq_len + (1 - at_x) * half, half).astype(BF16)
    in_low = [hidden.astype(BF16), None]
    qkv, far, ctx, lse = [None] * 2, [None] * 2, [None] * 2, [None] * 2
    weight_a, weight_f = [a0, None], [None, None]

    def out_part(layer):
        return call(out_kernel, thirds(hidden.shape), (*ctx[layer], *weight_a[layer]), name="attention_out")

    norms = [None] * 2
    ffn_parts = [None] * 2

    row_parts = [
        [jnp.stack([row_params[i, k] for k in ks]) for ks in ((0, 2, 3), (1, 4, 5))] for i in range(LAYERS)
    ]
    row_parts = [
        [jnp.stack([row_params[i, k] for k in ks]) for ks in ((0, 2, 3), (1, 4, 5))] for i in range(LAYERS)
    ]
    qkv[0], far[0] = project(in_low[0], a0, qkv_b[0], low_other)
    q0, q1, far[0], f0_in, later = tie(*qkv[0], far[0], f0_in, later)
    f0 = join([f0, f0_in])
    near = links.swap_as("ffn0_near", links.swap_near, f0)
    later, later_in = links.swap_as("layer1_z1", links.last_z, later, z_rest)
    qkv[0] = [q0, q1]
    ctx[0], lse[0] = attend_full(limits, qkv[0])
    ctx[0], lse[0] = attend_half(limits, qkv[0], far[0], ctx[0], lse[0], 0)
    c0, c1, near = tie(*ctx[0], near)
    ctx[0] = (c0, c1)
    f0two = jnp.stack([f0, near])
    f0far = links.swap_as("ffn0_far", links.swap_far, f0two)
    normed, normed_low, scaled_one, inv_one = add_norm(both_cores(links, out_part(0)), hidden, row_parts[0][0])
    normed_low, later_in = tie(normed_low, later_in)
    later = join([later, later_in])
    a1, f1 = later[:, :, : 4 * third], later[:, :, 4 * third :]
    near = links.swap_as("attn1_near", links.swap_near, a1)
    normed_low, f0far = tie(normed_low, f0far)
    f0 = links.assemble(f0two, f0far)
    weight_f[0] = f0
    ffn_parts[0], partial = feed_forward(normed_low, f0, ffn_b[0])
    *partial, near, f1 = tie(*partial, near, f1)
    a1two = jnp.stack([a1, near])
    a1far = links.swap_as("attn1_far", links.swap_far, a1two)
    near = links.swap_as("ffn1_near", links.swap_near, f1)
    fed = both_cores(links, partial)
    hidden, low, scaled_two, inv_two = add_norm(fed, normed, row_parts[0][1])
    norms[0] = (normed_low, scaled_one, inv_one, scaled_two, inv_two)

    low, a1far = tie(low, a1far)
    a1 = links.assemble(a1two, a1far)
    weight_a[1] = a1
    in_low[1] = low
    qkv[1], sent = project(low, a1, qkv_b[1])
    far[1] = links.swap_as("keys_values", links.swap_x, sent)
    ctx[1], lse[1] = attend_full(limits, qkv[1])
    c0, c1, near, far[1] = tie(*ctx[1], near, far[1])
    f1two = jnp.stack([f1, near])
    f1far = links.swap_as("ffn1_far", links.swap_far, f1two)
    ctx[1], lse[1] = attend_half(limits, qkv[1], far[1], (c0, c1), lse[1], 1)
    fed = both_cores(links, out_part(1))
    normed, normed_low, scaled_one, inv_one = add_norm(fed, hidden, row_parts[1][0])
    normed_low, f1far = tie(normed_low, f1far)
    f1 = links.assemble(f1two, f1far)
    weight_f[1] = f1
    ffn_parts[1], partial = feed_forward(normed_low, f1, ffn_b[1])
    fed = both_cores(links, partial)
    hidden, low, scaled_two, inv_two = add_norm(fed, normed, row_parts[1][1])
    norms[1] = (normed_low, scaled_one, inv_one, scaled_two, inv_two)
    state = {}

    def ffn_back(layer, grad_parts, middle):
        normed_low, _, _, scaled_two, inv_two = norms[layer]
        upper, upper_low, row_sums = norm_back(grad_parts, scaled_two, inv_two, row_params[layer, 4:5])
        slopes = [part[1] for part in ffn_parts[layer]]
        grad_pre, pre_sums = ffn_back_first(upper_low, weight_f[layer], slopes)
        grad_pre = middle(grad_pre)
        keep, give = weight_grads(
            links,
            (normed_low, upper_low),
            [(grad_pre[g], ffn_parts[layer][g][0]) for g in range(2)],
        )
        g0, g1, give = tie(*grad_pre, give)
        grad_pre = [g0, g1]
        came = links.swap_as("ffn%d_grad_far" % layer, links.swap_far, give)
        partial = call(back_out_kernel, thirds(upper.shape), (*grad_pre, *weight_f[layer]), name="up_back")
        vectors = (row_sums, pre_sums)
        return upper, partial, (keep, came), vectors

    def attn_back(layer, grad_parts, during):
        _, scaled_one, inv_one, _, _ = norms[layer]
        lower, lower_low, row_sums = norm_back(grad_parts, scaled_one, inv_one, row_params[layer, 2:3])
        weight = weight_a[layer]
        shape = (lower.shape[0], third)
        dctx = call(context_grad_kernel, [(shape, BF16)] * 2, (lower_low, *weight), name="context_grad")
        dq, own, sent = attend_half_back(limits, qkv[layer], far[layer], dctx, lse[layer], layer)
        d0, d1, sent = tie(*dctx, sent)
        came = links.swap_as("keys_values_grad", links.swap_x, sent)
        dqkv = attend_full_back(limits, qkv[layer], (d0, d1), lse[layer])
        dqkv, came = during(dqkv, came)
        dqkv = fill_half(dqkv, dq, own, came)
        keep, give = weight_grads(links, (in_low[layer], lower_low), [(dqkv[g], ctx[layer][g]) for g in range(2)])
        d0, d1, give = tie(*dqkv, give)
        dqkv = [d0, d1]
        came = links.swap_as("attn%d_grad_far" % layer, links.swap_far, give)
        *partial, sums = call(
            qkv_back_kernel,
            thirds(lower.shape) + [((16, 3 * third), F32)],
            (*dqkv, *weight),
            name="qkv_back",
        )
        vectors = (row_sums, sums)
        return lower, partial, (keep, came), vectors

    def first_sum(keep, came):
        return keep.astype(F32) + came.astype(F32)

    def near_swap(name, parts):
        return parts[0], links.swap_as(name, links.swap_near, parts[1].astype(BF16))

    def add(keep, came):
        return keep + came.astype(F32)

    z_top, z_last = links.z_masks[:0:-1], z_one
    vectors = [None, None]
    grad_top = own_rows(cotangent) * row_mask
    upper, partial, (f1k, f1c), fvec = ffn_back(1, (grad_top,), lambda g: g)
    fed = both_cores(links, partial)

    def during1(dqkv, kv):
        d0, d1, kv, came = tie(*dqkv, kv, f1c)
        state["f1"] = near_swap("ffn1_grad_near", first_sum(f1k, came))
        return [d0, d1], kv

    lower, partial, (a1k, a1c), avec = attn_back(1, (upper, *fed), during1)
    vectors[1] = (fvec, avec)
    fed = both_cores(links, partial)

    def middle0(grad_pre):
        g0, g1, came = tie(*grad_pre, state["f1"][1])
        state["f1"] = links.swap_as("ffn1_grad_z1", links.scatter_z, add(state["f1"][0], came), z_top)
        return [g0, g1]

    upper, partial, (f0k, f0c), fvec = ffn_back(0, (lower, *fed), middle0)
    fed = both_cores(links, partial)

    def during0(dqkv, kv):
        d0, d1, came = tie(*dqkv, a1c)
        state["a1"] = near_swap("attn1_grad_near", first_sum(a1k, came))
        d0, d1, f1_in, kv, came = tie(d0, d1, state["f1"][1], kv, f0c)
        state["f1"] = links.swap_as("ffn1_grad_z2", links.scatter_z, add(state["f1"][0], f1_in), z_last)
        state["f0"] = near_swap("ffn0_grad_near", first_sum(f0k, came))
        return [d0, d1], kv

    lower, partial, (a0k, a0c), avec = attn_back(0, (upper, *fed), during0)
    vectors[0] = (fvec, avec)
    *partial, came = tie(*partial, state["a1"][1])
    a1s = links.swap_as("attn1_grad_z1", links.scatter_z, add(state["a1"][0], came), z_top)
    fed = both_cores(links, partial)
    grad_hidden = call(final_sum_kernel, [(lower.shape, BF16)], (lower, *fed), name="input_grad")[0]

    own, other = [], []
    for f, a in vectors:
        for g, into in enumerate((own, other)):
            heads = jnp.sum(a[1][8 * g : 8 * (g + 1)], axis=0)
            into += [heads[:third], heads[2 * third :], jnp.sum(f[1][8 * g : 8 * (g + 1)], axis=0)]
    own, other = jnp.concatenate(own), jnp.concatenate(other)
    rows = []
    for f, a in vectors:
        upper_sums = jnp.sum(f[0].reshape(3, 8, -1), axis=1)
        lower_sums = jnp.sum(a[0].reshape(3, 8, -1), axis=1)
        rows += [lower_sums[0], upper_sums[0], lower_sums[1], lower_sums[2], upper_sums[1], upper_sums[2]]
    rows = jnp.concatenate(rows)
    vector, given = (jnp.concatenate([part, rows]).reshape(-1, 128) for part in (own, other))

    grad_hidden, given, f1_in, f0_in = tie(grad_hidden, given, state["f1"][1], state["f0"][1])
    f1s = add(state["f1"][0], f1_in)[0]
    f0s = links.swap_as("ffn0_grad_z1", links.scatter_z, add(state["f0"][0], f0_in), z_top)
    v_in = links.swap_as("vectors_x", links.swap_x, given)
    came, v_in, grad_hidden, low = tie(a0c, v_in, grad_hidden, low)
    a0s = near_swap("attn0_grad_near", first_sum(a0k, came))
    vector = vector + v_in
    v_in = links.swap_as("vectors_y", links.swap, vector, 4)
    piece = rows_first(jnp.stack([grad_hidden, low], axis=1))
    came, v_in, a1_in = tie(a0s[1], v_in, a1s[1])
    a0s = links.swap_as("attn0_grad_z1", links.scatter_z, add(a0s[0], came), z_top)
    a1s = links.swap_as("attn1_grad_z2", links.scatter_z, add(a1s[0], a1_in), z_last)
    vector = vector + v_in
    v_in = links.swap_as("vectors_z", links.swap_z, vector, links.z_masks[0])
    piece, v_in, f0_in = tie(piece, v_in, f0s[1])
    twin = rows_second(piece)
    vector = vector + v_in
    f0s = links.swap_as("ffn0_grad_z2", links.scatter_z, add(f0s[0], f0_in), z_last)
    for mask in links.z_masks[1:]:
        vector = vector + links.swap_as("vectors_z", links.swap_z, vector, mask)
    twin, came, a1_in = tie(twin, a0s[1], a1s[1])
    a0s = links.swap_as("attn0_grad_z2", links.scatter_z, add(a0s[0], came), z_last)
    a1s = add(a1s[0], a1_in)[0]
    input_grad = all_rows(grad_hidden, piece[:, 0], twin[:, 0])
    encoded = all_rows(low, piece[:, 1], twin[:, 1])
    f0s = add(*f0s)[0]
    a0s = add(*a0s)[0]

    sums = vector.reshape(-1)
    size = own.shape[0] // LAYERS
    head_grad = jnp.stack([sums[i * size : i * size + 2 * third].reshape(2, third) for i in range(LAYERS)])
    ffn_grad = jnp.stack([sums[i * size + 2 * third : (i + 1) * size] for i in range(LAYERS)])
    row_grad = sums[LAYERS * size :].reshape(row_params.shape)

    attn = jnp.stack([a0s, a1s])
    ffn = jnp.stack([f0s, f1s])
    gradients = (
        jnp.stack([attn[:, :, k * third : (k + 1) * third] for k in range(3)], axis=1),
        attn[:, :, 3 * third :],
        ffn[:, :, :wide],
        ffn[:, :, wide:],
        head_grad,
        ffn_grad,
        row_grad,
    )
    params = (attn_in, attn_out, ffn_up, ffn_down, head_bias, ffn_bias, row_params)
    stepped = [
        adam_step(
            params[i],
            moments[i],
            seconds[i],
            gradients[i],
            RATE_MATRIX if i < 4 else RATE_VECTOR,
            DECAY_MATRIX if i < 4 else 0.0,
        )
        for i in range(7)
    ]
    news, moms, vars_ = zip(*stepped)
    copies = tuple(news[i].astype(BF16) for i in range(4))
    return (encoded, input_grad) + news + moms + vars_ + copies


def solution(mesh):
    n_dp = mesh.shape["dp"]
    row = P("dp", None)
    state = (
        P(None, None, "dp", "mp"),
        P(None, "dp", "mp"),
        P(None, "dp", "mp"),
        P(None, "dp", "mp"),
        P(None, None, "mp"),
        P(None, "mp"),
        P(),
    )

    def step(*args):
        return local(n_dp, *args)

    return jax.shard_map(
        step,
        mesh=mesh,
        in_specs=(row, row, row, P("dp")) + state * 3,
        out_specs=(row, row) + state * 3 + state[:4],
        check_vma=False,
    )
```

```python
import functools

import jax
import jax.numpy as jnp
from jax import lax
from jax.experimental import pallas as pl
from jax.experimental.pallas import tpu as pltpu
from jax.sharding import PartitionSpec as P

HEAD_DIM = 64
LAYERS = 2
ADAM_STEP = 10

EPS_NORM = 1e-12
EPS_ADAM = 1e-08
RATE_MATRIX = 0.04
RATE_VECTOR = 0.3
DECAY_MATRIX = 0.01

F32 = jnp.float32
BF16 = jnp.bfloat16
AXES = ("dp", "mp")
NN = ((1,), (0,))
NT = ((1,), (1,))
TN = ((0,), (0,))


def dot(a, b, dims):
    return lax.dot_general(a, b, (dims, ((), ())), preferred_element_type=F32)


def tie(*arrays):
    return lax.optimization_barrier(arrays)


class Links:
    def __init__(self, n_dp, rows):
        self.n_dp = n_dp
        self.count = n_dp * 4
        self.z_masks = [1 << bit for bit in reversed(range(n_dp.bit_length() - 2))]
        self.order = [0]
        for mask in self.z_masks:
            self.order += [place ^ mask for place in self.order]
        self.aligned = rows % 16 == 0
        dp_at = lax.axis_index("dp")
        mp_at = lax.axis_index("mp")
        self.at_x = mp_at // 2
        self.core = mp_at % 2
        self.at_y = dp_at % 2
        self.at_z = dp_at // 2
        self.places = jnp.stack([self.core, self.at_y, self.at_z, self.at_x]).astype(jnp.int32)

    def swap(self, array, mask0, mask1=None):
        mask1 = mask0 if mask1 is None else mask1
        pairs = [(i, i ^ (mask1 if i & 1 else mask0)) for i in range(self.count)]
        return lax.ppermute(array, AXES, pairs)

    def swap_as(self, name, swap, *args):
        with jax.named_scope(name):
            return swap(*args)

    def swap_core(self, array):
        return self.swap(array, 1)

    def swap_x(self, array):
        return self.swap(array, 2)

    def swap_z(self, array, mask):
        return self.swap(array, 8 * mask)

    def swap_near(self, array):
        return self.swap(array, 4, 2)

    def swap_far(self, array):
        return self.swap(array, 2, 4)

    def last_z(self, block, masks):
        for mask in masks[:-1]:
            block = jnp.concatenate([block, self.swap_z(block, mask)])
        return block, self.swap_z(block, masks[-1])

    def scatter_z(self, parts, masks):
        for mask in masks[:-1]:
            half = parts.shape[0] // 2
            parts = parts[:half] + self.swap_z(parts[half:].astype(BF16), mask).astype(F32)
        half = parts.shape[0] // 2
        return parts[:half], self.swap_z(parts[half:].astype(BF16), masks[-1])

    def assemble(self, block, near, far_block, far_near):
        parts = (block, near, far_block, far_near)
        if self.aligned:
            shape = (block.shape[0], 2) + block.shape[1:]
            kernel = functools.partial(assemble_kernel, self.order)
            both = call(kernel, [(shape, block.dtype)] * 2, (self.places, *parts), name="assemble")
        else:
            order = jnp.array(inverse(self.order))[jnp.arange(block.shape[0]) ^ self.at_z]
            block, near, far_block, far_near = (jnp.take(part, order, axis=0) for part in parts)
            first, low = self.core == 0, self.at_y == 0
            own_far = jnp.where(first, near, far_block)
            other_same = jnp.where(first, far_block, near)
            both = [
                jnp.stack([jnp.where(low, same, other), jnp.where(low, other, same)], axis=1)
                for same, other in ((block, own_far), (other_same, far_near))
            ]
        return [w.reshape(-1, w.shape[-1]) for w in both]


def inverse(order):
    return [order.index(place) for place in range(len(order))]


def assemble_kernel(order, places, block, near, far_block, far_near, own, other):
    first, at_y, at_z = places[0] == 0, places[1], places[2]
    for m, distance in enumerate(order):
        j = distance ^ at_z
        own[j, at_y] = block[m]
        other[j, 1 - at_y] = far_near[m]

        @pl.when(first)
        def _(j=j, m=m):
            own[j, 1 - at_y] = near[m]
            other[j, at_y] = far_block[m]

        @pl.when(~first)
        def _(j=j, m=m):
            own[j, 1 - at_y] = far_block[m]
            other[j, at_y] = near[m]


def adam_step(master, moment, second, gradient, step_rate, decay_rate):
    correction = 1.0 - 0.5**ADAM_STEP
    moment_new = 0.5 * moment + 0.5 * gradient
    second_new = 0.5 * second + 0.5 * gradient * gradient
    update = (
        moment_new / correction / (jnp.sqrt(second_new / correction) + EPS_ADAM)
        + decay_rate * master
    )
    return (master - step_rate * update, moment_new, second_new)


def key_bias(limit, count, lanes):
    places = lax.broadcasted_iota(jnp.int32, (count, lanes), 0)
    return jnp.where(places < limit, 0.0, -1000000000.0)


def head_parts(qkv, far, swapped, g, h, full):
    third = qkv[g].shape[1] // 3
    k_at, v_at = third + h * HEAD_DIM, 2 * third + h * HEAD_DIM
    f_at = (g ^ swapped) * 2 * third + h * HEAD_DIM
    keys = qkv[g][:full, k_at : k_at + HEAD_DIM]
    values = qkv[g][:full, v_at : v_at + HEAD_DIM]
    keys_half = jnp.concatenate([qkv[g][full:, k_at : k_at + HEAD_DIM], far[:, f_at : f_at + HEAD_DIM]])
    f_at += third
    values_half = jnp.concatenate([qkv[g][full:, v_at : v_at + HEAD_DIM], far[:, f_at : f_at + HEAD_DIM]])
    return keys, values, keys_half, values_half


def attend_unit(keys, values, queries, bias_rows):
    scores = dot(keys, queries, NT) + bias_rows
    peak = jnp.max(scores, axis=0, keepdims=True)
    shifted = jnp.exp(scores - peak)
    total = jnp.sum(shifted, axis=0, keepdims=True)
    probs = (shifted * (1.0 / total)).astype(BF16)
    return dot(values, probs, TN), peak + jnp.log(total)


def full_kernel(limits, qkv0, qkv1, ctx0, ctx1, lse, bias):
    qkv, ctx = (qkv0, qkv1), (ctx0, ctx1)
    full, half = bias.shape
    third = qkv0.shape[1] // 3
    heads = third // HEAD_DIM
    bias[...] = key_bias(limits[0], full, half)
    for g in range(2):
        outs = [[], []]
        for h in range(heads):
            columns = slice(h * HEAD_DIM, (h + 1) * HEAD_DIM)
            keys = qkv[g][:full, third + h * HEAD_DIM : third + (h + 1) * HEAD_DIM]
            values = qkv[g][:full, 2 * third + h * HEAD_DIM : 2 * third + (h + 1) * HEAD_DIM]
            for part in range(2):
                rows = slice(part * half, (part + 1) * half)
                out, log_total = attend_unit(keys, values, qkv[g][rows, columns], bias[...])
                lse[g * heads + h : g * heads + h + 1, rows] = log_total
                outs[part].append(out)
        for part in range(2):
            rows = slice(part * half, (part + 1) * half)
            ctx[g][rows, :] = jnp.concatenate(outs[part], axis=0).T.astype(BF16)


def half_kernel(swapped, limits, qkv0, qkv1, far, ctx0, ctx1, lse, bias):
    qkv, ctx = (qkv0, qkv1), (ctx0, ctx1)
    half = far.shape[0]
    full = 2 * half
    heads = qkv0.shape[1] // 3 // HEAD_DIM
    bias[:half] = key_bias(limits[1], half, half)
    bias[half:] = key_bias(limits[2], half, half)
    for g in range(2):
        outs = []
        for h in range(heads):
            _, _, keys, values = head_parts(qkv, far, swapped, g, h, full)
            columns = slice(h * HEAD_DIM, (h + 1) * HEAD_DIM)
            out, log_total = attend_unit(keys, values, qkv[g][full:, columns], bias[...])
            lse[g * heads + h : g * heads + h + 1, :] = log_total
            outs.append(out)
        ctx[g][...] = jnp.concatenate(outs, axis=0).T.astype(BF16)


def attend_back_unit(keys, values, queries, grad_rows, log_total, bias_rows):
    probs = jnp.exp(dot(keys, queries, NT) + bias_rows - log_total)
    grad_probs = dot(values, grad_rows, NT)
    inner = jnp.sum(probs * grad_probs, axis=0, keepdims=True)
    grad_scores = (probs * (grad_probs - inner)).astype(BF16)
    grad_values = dot(probs.astype(BF16), grad_rows, NN)
    grad_keys = dot(grad_scores, queries, NN)
    grad_queries = dot(keys, grad_scores, TN)
    return grad_queries, grad_keys, grad_values


def half_back_kernel(swapped, limits, qkv0, qkv1, far, dctx0, dctx1, lse, dq0, dq1, own, sent, bias):
    qkv, dctx, dq = (qkv0, qkv1), (dctx0, dctx1), (dq0, dq1)
    half = far.shape[0]
    full = 2 * half
    third = qkv0.shape[1] // 3
    heads = third // HEAD_DIM
    bias[:half] = key_bias(limits[1], half, half)
    bias[half:] = key_bias(limits[2], half, half)
    for g in range(2):
        queries_out, keys_out, values_out = [], [], []
        for h in range(heads):
            _, _, keys, values = head_parts(qkv, far, swapped, g, h, full)
            columns = slice(h * HEAD_DIM, (h + 1) * HEAD_DIM)
            gq, gk, gv = attend_back_unit(
                keys,
                values,
                qkv[g][full:, columns],
                dctx[g][full:, columns],
                lse[g * heads + h : g * heads + h + 1, :],
                bias[...],
            )
            queries_out.append(gq)
            keys_out.append(gk)
            values_out.append(gv)
        dq[g][...] = jnp.concatenate(queries_out, axis=0).T.astype(BF16) * 0.125
        both = jnp.concatenate(keys_out + values_out, axis=1)
        own[:, 2 * third * g : 2 * third * (g + 1)] = both[:half]
        other = 1 - g
        sent[:, 2 * third * other : 2 * third * (other + 1)] = both[half:].astype(BF16)


def full_back_kernel(limits, qkv0, qkv1, dctx0, dctx1, lse, dqkv0, dqkv1, bias):
    qkv, dctx, dqkv = (qkv0, qkv1), (dctx0, dctx1), (dqkv0, dqkv1)
    full, half = bias.shape
    third = qkv0.shape[1] // 3
    heads = third // HEAD_DIM
    bias[...] = key_bias(limits[0], full, half)
    for g in range(2):
        queries_out, keys_out, values_out = [[], []], [], []
        for h in range(heads):
            columns = slice(h * HEAD_DIM, (h + 1) * HEAD_DIM)
            keys = qkv[g][:full, third + h * HEAD_DIM : third + (h + 1) * HEAD_DIM]
            values = qkv[g][:full, 2 * third + h * HEAD_DIM : 2 * third + (h + 1) * HEAD_DIM]
            sums = None
            for part in range(2):
                rows = slice(part * half, (part + 1) * half)
                gq, gk, gv = attend_back_unit(
                    keys,
                    values,
                    qkv[g][rows, columns],
                    dctx[g][rows, columns],
                    lse[g * heads + h : g * heads + h + 1, rows],
                    bias[...],
                )
                queries_out[part].append(gq)
                sums = (gk, gv) if sums is None else (sums[0] + gk, sums[1] + gv)
            keys_out.append(sums[0].astype(BF16))
            values_out.append(sums[1].astype(BF16))
        for part in range(2):
            rows = slice(part * half, (part + 1) * half)
            dqkv[g][rows, :third] = jnp.concatenate(queries_out[part], axis=0).T.astype(BF16) * 0.125
        dqkv[g][:, third:] = jnp.concatenate(keys_out + values_out, axis=1)


def half_fill_kernel(dq0, dq1, own, came, dqkv0, dqkv1):
    third = dq0.shape[1]
    for g, (dq, dqkv) in enumerate(((dq0, dqkv0), (dq1, dqkv1))):
        columns = slice(2 * third * g, 2 * third * (g + 1))
        both = (own[:, columns] + came[:, columns].astype(F32)).astype(BF16)
        dqkv[...] = jnp.concatenate([dq[...], both], axis=1)


VMEM = pl.BlockSpec(memory_space=pltpu.VMEM)
SMEM = pl.BlockSpec(memory_space=pltpu.SMEM)
ROOM = pltpu.CompilerParams(vmem_limit_bytes=16 * 1024 * 1024)
CHEAP = pl.CostEstimate(flops=1, bytes_accessed=1, transcendentals=0)


def call(kernel, outs, ins, scratch=(), name=None):
    specs = [SMEM if a.dtype == jnp.int32 else VMEM for a in ins]
    return pl.pallas_call(
        kernel,
        out_shape=[jax.ShapeDtypeStruct(s, d) for s, d in outs],
        in_specs=specs,
        out_specs=[VMEM] * len(outs),
        scratch_shapes=list(scratch),
        compiler_params=ROOM,
        cost_estimate=CHEAP,
        name=name,
    )(*ins)


def attend_full(limits, qkv):
    tokens, third = qkv[0].shape[0], qkv[0].shape[1] // 3
    half = tokens // 3
    ctx0, ctx1, lse = call(
        full_kernel,
        [((2 * half, third), BF16)] * 2 + [((2 * third // HEAD_DIM, 2 * half), F32)],
        (limits, *qkv),
        [pltpu.VMEM((2 * half, half), F32)],
        name="attend_full",
    )
    return [ctx0, ctx1], lse


def attend_half(limits, qkv, far, swapped):
    half, third = far.shape[0], qkv[0].shape[1] // 3
    ctx0, ctx1, lse = call(
        functools.partial(half_kernel, swapped),
        [((half, third), BF16)] * 2 + [((2 * third // HEAD_DIM, half), F32)],
        (limits, *qkv, far),
        [pltpu.VMEM((2 * half, half), F32)],
        name="attend_half",
    )
    return [ctx0, ctx1], lse


def attend_half_back(limits, qkv, far, dctx, lse, swapped):
    half, third = far.shape[0], qkv[0].shape[1] // 3
    dq0, dq1, own, sent = call(
        functools.partial(half_back_kernel, swapped),
        [((half, third), BF16)] * 2 + [((half, 4 * third), F32), ((half, 4 * third), BF16)],
        (limits, *qkv, far, *dctx, lse),
        [pltpu.VMEM((2 * half, half), F32)],
        name="attend_half_back",
    )
    return (dq0, dq1), own, sent


def attend_full_back(limits, qkv, dctx, lse):
    half = qkv[0].shape[0] // 3
    return call(
        full_back_kernel,
        [((2 * half, qkv[0].shape[1]), BF16)] * 2,
        (limits, *qkv, *dctx, lse),
        [pltpu.VMEM((2 * half, half), F32)],
        name="attend_full_back",
    )


def fill_half(dq, own, came):
    shape = (own.shape[0], 3 * dq[0].shape[1])
    return call(half_fill_kernel, [(shape, BF16)] * 2, (*dq, own, came), name="fill_half")


def wgrad_kernel(count, pieces, order, places, *refs):
    step = count * pieces
    lefts, rights = refs[:count], (refs[count : count + step], refs[count + step : count + 2 * step])
    keep0, keep1, give0, give1, whole = refs[count + 2 * step :]
    first, at_y, at_z = places[0] == 0, places[1], places[2]
    rows = keep0.shape[1]
    turned = [left[...].T for left in lefts]
    for g in range(2):
        at = 0
        for k, left in enumerate(turned):
            right = [ref[...] for ref in rights[g][k * pieces : (k + 1) * pieces]]
            right = right[0] if pieces == 1 else jnp.concatenate(right)
            wide = right.shape[1]
            whole[:, at : at + wide] = dot(left, right, NN).astype(BF16)
            at += wide
        for y in range(2):
            same = at_y == y
            if g == 0:
                targets = ((same, keep0), (~same & first, keep1), (~same & ~first, give0))
            else:
                targets = ((same & first, give0), (same & ~first, keep1), (~same, give1))
            for when, ref in targets:

                @pl.when(when)
                def _(ref=ref, y=y):
                    for m, distance in enumerate(order):
                        from_row = pl.ds(pl.multiple_of((2 * (distance ^ at_z) + y) * rows, 16), rows)
                        ref[m] = whole[from_row, :]


def weight_grads(links, lefts, rights):
    features = lefts[0].shape[1]
    columns = sum(r[0].shape[1] for r in rights[0])
    blocks = links.n_dp // 2
    rows = features // links.n_dp
    if links.aligned:
        return call(
            functools.partial(wgrad_kernel, len(lefts), len(rights[0][0]), links.order),
            [((blocks, rows, columns), BF16)] * 4,
            (links.places, *lefts, *[piece for group in rights for right in group for piece in right]),
            [pltpu.VMEM((features, columns), BF16)],
            name="weight_grads",
        )
    low, first = links.at_y == 0, links.core == 0
    parts = []
    for group in rights:
        grad = jnp.concatenate([dot(a, jnp.concatenate(b), TN) for a, b in zip(lefts, group)], axis=1).astype(BF16)
        grad = jnp.take(grad.reshape(blocks, 2, rows, columns), jnp.array(links.order) ^ links.at_z, axis=0)
        parts += [jnp.where(low, grad[:, 0], grad[:, 1]), jnp.where(low, grad[:, 1], grad[:, 0])]
    own_same, own_far, other_same, other_far = parts
    return own_same, jnp.where(first, own_far, other_same), jnp.where(first, other_same, own_far), other_far


def both_cores(links, parts):
    return (*parts, *[links.swap_as("core", links.swap_core, part) for part in parts])


def thirds(shape):
    return [((shape[0] // 3, shape[1]), BF16)] * 3


def core_sum(parts, at, rows):
    return parts[at][rows, :].astype(F32) + parts[at + 3][rows, :].astype(F32)


def norm_kernel(step, *refs):
    parts, (residual, rows, out, low, scaled, inverse) = refs[:6], refs[6:]
    wide = out.shape[1]
    third = parts[0].shape[0]
    for part in range(3):

        @pl.loop(0, third // step)
        def _(i, part=part):
            inner = pl.ds(i * step, step)
            at = pl.ds(part * third + i * step, step)
            total = residual[at, :] + (core_sum(parts, part, inner) + rows[0:1, :])
            center = total - jnp.sum(total, axis=-1, keepdims=True) * (1.0 / wide)
            inv_std = lax.rsqrt(jnp.sum(center * center, axis=-1, keepdims=True) * (1.0 / wide) + EPS_NORM)
            normal = center * inv_std
            result = normal * rows[1:2, :] + rows[2:3, :]
            out[at, :] = result
            low[at, :] = result.astype(BF16)
            scaled[at, :] = normal
            inverse[at, :] = inv_std


def add_norm(parts, residual, rows):
    shape = residual.shape
    return call(
        functools.partial(norm_kernel, 64),
        [(shape, F32), (shape, BF16), (shape, F32), ((shape[0], 1), F32)],
        (*parts, residual, rows),
        name="add_norm",
    )


def norm_back_kernel(step, *refs):
    base, *parts, scaled, inverse, gain, out, low, sums = refs
    wide = out.shape[1]
    third = out.shape[0] // 3
    sums[...] = jnp.zeros_like(sums)
    for part in range(3):

        @pl.loop(0, third // step)
        def _(i, part=part):
            at = pl.ds(part * third + i * step, step)
            grad = base[at, :]
            if parts:
                grad = grad + core_sum(parts, part, pl.ds(i * step, step))
            normal = scaled[at, :]
            upstream = grad * gain[...]
            mean_up = jnp.sum(upstream, axis=-1, keepdims=True) * (1.0 / wide)
            mean_cross = jnp.sum(upstream * normal, axis=-1, keepdims=True) * (1.0 / wide)
            result = inverse[at, :] * (upstream - mean_up - normal * mean_cross)
            out[at, :] = result
            low[at, :] = result.astype(BF16)
            for k, term in enumerate((result, grad * normal, grad)):
                sums[8 * k : 8 * (k + 1), :] += jnp.sum(term.reshape(-1, 8, wide), axis=0)


def norm_back(parts, scaled, inverse, gain):
    shape = scaled.shape
    return call(
        functools.partial(norm_back_kernel, 64),
        [(shape, F32), (shape, BF16), ((24, shape[1]), F32)],
        (*parts, scaled, inverse, gain),
        name="norm_back",
    )


def final_sum_kernel(base, *refs):
    parts, out = refs[:6], refs[6]
    third = parts[0].shape[0]
    for part in range(3):
        at = slice(part * third, (part + 1) * third)
        out[at, :] = (base[at, :] + core_sum(parts, part, slice(None))).astype(BF16)


def chunks(count, step=256):
    return [slice(at, at + step) for at in range(0, count, step)]


def qkv_kernel(low, w0, w1, bias, *refs):
    *other, out0, out1, extra = refs
    columns = out0.shape[1]
    third = columns // 3
    half = extra.shape[0]
    scale = jnp.where(lax.broadcasted_iota(jnp.int32, (1, columns), 1) < third, 0.125, 1.0)
    for g, (weight, out) in enumerate(((w0, out0), (w1, out1))):
        at = slice(2 * third * g, 2 * third * (g + 1))
        for rows in chunks(low.shape[0]):
            out[rows, :] = ((dot(low[rows, :], weight[:, :columns], NN) + bias[g : g + 1, :]) * scale).astype(BF16)
        if other:
            more = dot(other[0][...], weight[:, :columns], NN) + bias[g : g + 1, :]
            extra[:, at] = more[:, third:].astype(BF16)
        else:
            extra[:, at] = out[2 * half :, third:]


def project(low, weights, bias, other=None):
    tokens, columns = low.shape[0], bias.shape[1]
    half = tokens // 3
    ins = (low, *weights, bias) + (() if other is None else (other,))
    q0, q1, extra = call(
        qkv_kernel,
        [((tokens, columns), BF16)] * 2 + [((half, 4 * columns // 3), BF16)],
        ins,
        name="queries_keys_values",
    )
    return [q0, q1], extra


def row_thirds(full0, full1, half0, half1):
    half = half0.shape[0]
    rows = [slice(0, half), slice(half, 2 * half), slice(0, half)]
    return [((full0, full1) if k < 2 else (half0, half1), rows[k]) for k in range(3)]


def out_kernel(full0, full1, half0, half1, w0, w1, *outs):
    third = full0.shape[1]
    at = w0.shape[1] - third
    tails = (w0[:, at:], w1[:, at:])
    for (pair, rows), out in zip(row_thirds(full0, full1, half0, half1), outs):
        out[...] = (dot(pair[0][rows, :], tails[0], NT) + dot(pair[1][rows, :], tails[1], NT)).astype(BF16)


def ffn_kernel(low, w0, w1, bias, act0, act1, slope0, slope1, *outs):
    wide = bias.shape[1]
    groups = ((w0, act0, slope0), (w1, act1, slope1))
    for at, rows in enumerate(chunks(low.shape[0], 128)):
        total = None
        for g, (weight, act, slope) in enumerate(groups):
            pre = dot(low[rows, :], weight[:, :wide], NN) + bias[g : g + 1, :]
            cdf = 0.5 * (1.0 + lax.erf(pre * 0.7071067811865476))
            slope[rows, :] = cdf + pre * (jnp.exp(-0.5 * pre * pre) * 0.3989422804014327)
            active = (pre * cdf).astype(BF16)
            act[rows, :] = active
            part = dot(active, weight[:, wide:], NT)
            total = part if total is None else total + part
        inner = slice(at % 2 * 128, (at % 2 + 1) * 128)
        outs[at // 2][inner, :] = total.astype(BF16)


def feed_forward(low, weights, bias):
    shape = (low.shape[0], bias.shape[1])
    act0, act1, slope0, slope1, *partial = call(
        ffn_kernel,
        [(shape, BF16)] * 2 + [(shape, F32)] * 2 + thirds(low.shape),
        (low, *weights, bias),
        name="feed_forward",
    )
    return [(act0, slope0), (act1, slope1)], partial


def add_rows(array):
    return jnp.sum(array.astype(F32).reshape(-1, 8, array.shape[1]), axis=0)


def ffn_back_kernel(low, w0, w1, slope0, slope1, pre0, pre1, sums):
    wide = slope0.shape[1]
    for g, (weight, slope, pre) in enumerate(((w0, slope0, pre0), (w1, slope1, pre1))):
        total = None
        for rows in chunks(low.shape[0]):
            grad = (dot(low[rows, :], weight[:, wide:], NN) * slope[rows, :]).astype(BF16)
            pre[rows, :] = grad
            part = add_rows(grad)
            total = part if total is None else total + part
        sums[8 * g : 8 * (g + 1), :] = total


def ffn_back_first(low, weights, slopes):
    shape = slopes[0].shape
    pre0, pre1, sums = call(
        ffn_back_kernel,
        [(shape, BF16)] * 2 + [((16, shape[1]), F32)],
        (low, *weights, *slopes),
        name="pre_grad",
    )
    return [pre0, pre1], sums


def back_out_kernel(d0, d1, w0, w1, *outs):
    wide = d0.shape[1]
    for rows, out in zip(chunks(d0.shape[0], outs[0].shape[0]), outs):
        out[...] = (dot(d0[rows, :], w0[:, :wide], NT) + dot(d1[rows, :], w1[:, :wide], NT)).astype(BF16)


def qkv_back_kernel(full0, full1, half0, half1, w0, w1, *refs):
    *outs, sums = refs
    wide = full0.shape[1]
    totals = [None, None]
    for (pair, rows), out in zip(row_thirds(full0, full1, half0, half1), outs):
        parts = [ref[rows, :] for ref in pair]
        out[...] = (dot(parts[0], w0[:, :wide], NT) + dot(parts[1], w1[:, :wide], NT)).astype(BF16)
        for g in range(2):
            part = add_rows(parts[g])
            totals[g] = part if totals[g] is None else totals[g] + part
    for g in range(2):
        sums[8 * g : 8 * (g + 1), :] = totals[g]


def context_grad_kernel(low, w0, w1, out0, out1):
    third = out0.shape[1]
    at = w0.shape[1] - third
    for weight, out in ((w0, out0), (w1, out1)):
        tail = weight[:, at:]
        for rows in chunks(low.shape[0]):
            out[rows, :] = dot(low[rows, :], tail, NN).astype(BF16)


def adam_kernel(splits, count, *refs):
    keep, came, *refs = refs
    ins, outs = refs[: 3 * len(splits)], refs[3 * len(splits) + count :]
    for i, ranges in enumerate(splits):
        master, moment, second = ins[3 * i : 3 * i + 3]
        results = outs[4 * i : 4 * i + 4]
        for k, (low, high) in enumerate(ranges):
            at = (0, k) if len(ranges) > 1 else (0,)
            grad = keep[0, :, low:high] + came[0, :, low:high].astype(F32)
            new = adam_step(master[at], moment[at], second[at], grad, RATE_MATRIX, DECAY_MATRIX)
            for ref, value in zip(results, (*new, new[0].astype(BF16))):
                ref[at] = value


def adam_layer(layer, splits, keep, came, states, before):
    def block(array):
        rest = array.shape[1:]
        return pl.BlockSpec((1,) + rest, lambda i, n=len(rest): (layer,) + (0,) * n)

    flat = [a for state in states for a in state]
    outs, specs = [], []
    for state in states:
        outs += [jax.ShapeDtypeStruct(state[0].shape, d) for d in (F32, F32, F32, BF16)]
        specs += [block(state[0])] * 4
    before = [] if before is None else before
    results = pl.pallas_call(
        functools.partial(adam_kernel, splits, len(before)),
        grid=(1,),
        out_shape=outs,
        in_specs=[VMEM] * 2 + [block(a) for a in flat] + [pl.BlockSpec(memory_space=pl.ANY)] * len(before),
        out_specs=specs,
        input_output_aliases={2 + len(flat) + i: i for i in range(len(before))},
        compiler_params=ROOM,
        cost_estimate=CHEAP,
        name="adam",
    )(keep, came, *flat, *before)
    return list(results)


def pack_kernel(*refs):
    *parts, own, other = refs
    own[...] = jnp.zeros_like(own)
    other[...] = jnp.zeros_like(other)
    for layer in range(LAYERS):
        upper, pre, lower, heads = parts[4 * layer : 4 * layer + 4]
        third = heads.shape[1] // 3

        def total(ref, k):
            return jnp.sum(ref[8 * k : 8 * (k + 1), :], axis=0, keepdims=True)

        rows = [(lower, 0), (upper, 0), (lower, 1), (lower, 2), (upper, 1), (upper, 2)]
        for k, row in enumerate(rows):
            value = total(*row)
            own[6 * layer + k : 6 * layer + k + 1, :] = value
            other[6 * layer + k : 6 * layer + k + 1, :] = value
        for g, ref in enumerate((own, other)):
            at = 6 * LAYERS + layer
            ref[at : at + 1, :] = total(pre, g)
            head = total(heads, g)
            at += LAYERS
            ref[at : at + 1, : 2 * third] = jnp.concatenate([head[:, :third], head[:, 2 * third :]], axis=1)


def vector_adam_kernel(grads, *refs):
    ins, outs = refs[:9], refs[9:]
    third = ins[0].shape[2]

    def update(i, at, grad):
        new = adam_step(ins[3 * i][at], ins[3 * i + 1][at], ins[3 * i + 2][at], grad, RATE_VECTOR, 0.0)
        for k, value in enumerate(new):
            outs[3 * i + k][at] = value

    for layer in range(LAYERS):
        at = 7 * LAYERS + layer
        for k in range(2):
            grad = grads[at : at + 1, k * third : (k + 1) * third]
            update(0, (layer, slice(k, k + 1)), grad)
        update(1, (slice(layer, layer + 1),), grads[at - LAYERS : at - LAYERS + 1, :])
        update(2, (layer,), grads[6 * layer : 6 * layer + 6, :])


def rows_kernel(places, low, piece, twin, out):
    first, at_x = places[0] == 0, places[3]
    half = low.shape[0] // 3
    part = piece.shape[0]

    def put(start, rows):
        out[pl.ds(pl.multiple_of(start, 8), rows.shape[0]), :] = rows.astype(F32)

    def put_other(upper, lower):
        put((1 - at_x) * 4 * half, upper[...])
        put((1 - at_x) * 4 * half + part, lower[: 2 * half - part, :])
        put(2 * half + (1 - at_x) * half, lower[2 * half - part :, :])

    put(at_x * 4 * half, low[: 2 * half, :])
    put(2 * half + at_x * half, low[2 * half :, :])

    @pl.when(first)
    def _():
        put_other(piece, twin)

    @pl.when(~first)
    def _():
        put_other(twin, piece)


def local(n_dp, *args):
    (
        inputs,
        cotangent,
        word_lengths,
        word_count,
        attn_in,
        attn_out,
        ffn_up,
        ffn_down,
        head_bias,
        ffn_bias,
        row_params,
    ) = args[:11]
    moments, seconds = args[11:18], args[18:25]
    links = Links(n_dp, attn_out.shape[1])
    at_x, core = links.at_x, links.core
    seq_len = inputs.shape[0] // word_count.shape[0]
    half = seq_len // 2
    third, wide = attn_in.shape[3], ffn_up.shape[2]

    def own_rows(array):
        whole = lax.dynamic_slice_in_dim(array, at_x * 2 * seq_len, seq_len)
        return jnp.concatenate([whole, lax.dynamic_slice_in_dim(array, seq_len + at_x * half, half)])

    def rows_first(low):
        part = low.shape[0] // 2
        return links.swap_as("rows_x", links.swap_x, lax.dynamic_slice_in_dim(low, core * part, part))

    def rows_second(piece):
        return links.swap_as("rows_core", links.swap_core, piece)

    def all_rows(low, piece, twin):
        return call(rows_kernel, [(inputs.shape, F32)], (links.places, low, piece, twin), name="all_rows")[0]

    def packed_attn(layer):
        attn = [attn_in[layer, 0], attn_in[layer, 1], attn_in[layer, 2], attn_out[layer]]
        return jnp.concatenate([a.astype(BF16) for a in attn], axis=1)[None]

    def packed_ffn(layer):
        return jnp.concatenate([ffn_up[layer].astype(BF16), ffn_down[layer].astype(BF16)], axis=1)[None]

    z_one, z_rest = links.z_masks[:1], links.z_masks[1:]
    join = jnp.concatenate

    a0 = packed_attn(0)
    a0_in = links.swap_as("attn0_z2", links.swap_z, a0, links.z_masks[0])
    a0_in, f0, later = tie(a0_in, packed_ffn(0), join([packed_attn(1), packed_ffn(1)], axis=2))
    a0 = join([a0, a0_in])
    a0, a0_in = links.swap_as("attn0_z1", links.last_z, a0, z_rest)
    f0_in = links.swap_as("ffn0_z2", links.swap_z, f0, links.z_masks[0])
    biases = jnp.concatenate([head_bias.reshape(-1), ffn_bias.reshape(-1)])
    a0_in, f0_in, later, biases = tie(a0_in, f0_in, later, biases)
    a0, f0 = join([a0, a0_in]), join([f0, f0_in])
    bias_far = links.swap_as("biases", links.swap_x, biases)
    near = links.swap_as("attn0_near", links.swap_near, a0)
    a0far = links.swap_as("attn0_far", links.swap_far, a0)
    f0, f0_in = links.swap_as("ffn0_z1", links.last_z, f0, z_rest)
    later_in = links.swap_as("layer1_z2", links.swap_z, later, links.z_masks[0])
    near, bias_far = tie(near, bias_far)
    a0last = links.swap_as("attn0_far_near", links.swap_far, near)
    a0far, a0last, f0_in = tie(a0far, a0last, f0_in)
    f0 = join([f0, f0_in])
    f0near = links.swap_as("ffn0_near", links.swap_near, f0)
    f0far = links.swap_as("ffn0_far", links.swap_far, f0)
    a0 = links.assemble(a0, near, a0far, a0last)
    head_b = (head_bias, bias_far[: head_bias.size].reshape(head_bias.shape))
    ffn_b = (ffn_bias, bias_far[head_bias.size :].reshape(ffn_bias.shape))
    zeros = jnp.zeros((third,), F32)
    qkv_b = [
        jnp.stack([jnp.concatenate([b[layer, 0], zeros, b[layer, 1]]) for b in head_b]) for layer in range(LAYERS)
    ]
    ffn_b = [jnp.stack([b[layer] for b in ffn_b]) for layer in range(LAYERS)]

    slots = jnp.arange(word_lengths.shape[1], dtype=jnp.int32)
    used = jnp.sum(jnp.where(slots[None, :] < word_count[:, None], word_lengths, 0), axis=1)
    used_full = jnp.where(at_x == 0, used[0], used[2])
    limits = jnp.stack([used_full, used[1] - at_x * half, used[1] - (1 - at_x) * half]).astype(jnp.int32)
    places = jnp.arange(seq_len, dtype=jnp.int32)
    row_mask = jnp.concatenate([places < limits[0], places[:half] < limits[1]]).astype(F32)[:, None]

    hidden = own_rows(inputs)
    low_other = lax.dynamic_slice_in_dim(inputs, seq_len + (1 - at_x) * half, half).astype(BF16)
    in_low = [hidden.astype(BF16), None]
    qkv, far, ctx, lse = [None] * 2, [None] * 2, [None] * 2, [None] * 2
    weight_a, weight_f = [a0, None], [None, None]

    def out_part(layer):
        return call(
            out_kernel, thirds(hidden.shape), (*ctx[layer][0], *ctx[layer][1], *weight_a[layer]), name="attention_out"
        )

    norms = [None] * 2
    ffn_parts = [None] * 2

    row_parts = [
        [jnp.stack([row_params[i, k] for k in ks]) for ks in ((0, 2, 3), (1, 4, 5))] for i in range(LAYERS)
    ]
    row_parts = [
        [jnp.stack([row_params[i, k] for k in ks]) for ks in ((0, 2, 3), (1, 4, 5))] for i in range(LAYERS)
    ]
    qkv[0], far[0] = project(in_low[0], a0, qkv_b[0], low_other)
    whole, whole_lse = attend_full(limits, qkv[0])
    *whole, f0near, later_in = tie(*whole, f0near, later_in)
    f0last = links.swap_as("ffn0_far_near", links.swap_far, f0near)
    later = join([later, later_in])
    later, later_in = links.swap_as("layer1_z1", links.last_z, later, z_rest)
    split, split_lse = attend_half(limits, qkv[0], far[0], 0)
    *split, f0far = tie(*split, f0far)
    ctx[0], lse[0] = (whole, split), (whole_lse, split_lse)
    normed, normed_low, scaled_one, inv_one = add_norm(both_cores(links, out_part(0)), hidden, row_parts[0][0])
    normed_low, later_in, f0last = tie(normed_low, later_in, f0last)
    later = join([later, later_in])
    a1, f1 = later[:, :, : 4 * third], later[:, :, 4 * third :]
    a1near = links.swap_as("attn1_near", links.swap_near, a1)
    a1far = links.swap_as("attn1_far", links.swap_far, a1)
    f0 = links.assemble(f0, f0near, f0far, f0last)
    weight_f[0] = f0
    ffn_parts[0], partial = feed_forward(normed_low, f0, ffn_b[0])
    fed = both_cores(links, partial)
    hidden, low, scaled_two, inv_two = add_norm(fed, normed, row_parts[0][1])
    norms[0] = (normed_low, scaled_one, inv_one, scaled_two, inv_two)

    low, a1near, a1far = tie(low, a1near, a1far)
    a1last = links.swap_as("attn1_far_near", links.swap_far, a1near)
    low, a1last, f1 = tie(low, a1last, f1)
    f1near = links.swap_as("ffn1_near", links.swap_near, f1)
    f1far = links.swap_as("ffn1_far", links.swap_far, f1)
    a1 = links.assemble(a1, a1near, a1far, a1last)
    weight_a[1] = a1
    in_low[1] = low
    qkv[1], sent = project(low, a1, qkv_b[1])
    far[1] = links.swap_as("keys_values", links.swap_x, sent)
    whole, whole_lse = attend_full(limits, qkv[1])
    *whole, far[1], f1near, f1far = tie(*whole, far[1], f1near, f1far)
    f1last = links.swap_as("ffn1_far_near", links.swap_far, f1near)
    split, split_lse = attend_half(limits, qkv[1], far[1], 1)
    ctx[1], lse[1] = (whole, split), (whole_lse, split_lse)
    fed = both_cores(links, out_part(1))
    normed, normed_low, scaled_one, inv_one = add_norm(fed, hidden, row_parts[1][0])
    normed_low, f1last = tie(normed_low, f1last)
    f1 = links.assemble(f1, f1near, f1far, f1last)
    weight_f[1] = f1
    ffn_parts[1], partial = feed_forward(normed_low, f1, ffn_b[1])
    fed = both_cores(links, partial)
    hidden, low, scaled_two, inv_two = add_norm(fed, normed, row_parts[1][1])
    norms[1] = (normed_low, scaled_one, inv_one, scaled_two, inv_two)
    state = {}

    def ffn_back(layer, grad_parts, middle):
        normed_low, _, _, scaled_two, inv_two = norms[layer]
        upper, upper_low, row_sums = norm_back(grad_parts, scaled_two, inv_two, row_params[layer, 4:5])
        slopes = [part[1] for part in ffn_parts[layer]]
        grad_pre, pre_sums = ffn_back_first(upper_low, weight_f[layer], slopes)
        grad_pre = middle(grad_pre)
        partial = call(back_out_kernel, thirds(upper.shape), (*grad_pre, *weight_f[layer]), name="up_back")
        fed = both_cores(links, partial)
        g0, g1, *_ = tie(*grad_pre, *partial)
        grad_pre = [g0, g1]
        grads = weight_grads(
            links,
            (normed_low, upper_low),
            [((grad_pre[g],), (ffn_parts[layer][g][0],)) for g in range(2)],
        )
        return upper, fed, grads, (row_sums, pre_sums)

    def attn_back(layer, grad_parts, during):
        _, scaled_one, inv_one, _, _ = norms[layer]
        lower, lower_low, row_sums = norm_back(grad_parts, scaled_one, inv_one, row_params[layer, 2:3])
        weight = weight_a[layer]
        shape = (lower.shape[0], third)
        dctx = call(context_grad_kernel, [(shape, BF16)] * 2, (lower_low, *weight), name="context_grad")
        dq, own, sent = attend_half_back(limits, qkv[layer], far[layer], dctx, lse[layer][1], layer)
        d0, d1, sent = tie(*dctx, sent)
        came = links.swap_as("keys_values_grad", links.swap_x, sent)
        dqkv = attend_full_back(limits, qkv[layer], (d0, d1), lse[layer][0])
        dqkv, came = during(dqkv, came)
        dqkv = (dqkv, fill_half(dq, own, came))
        *partial, sums = call(
            qkv_back_kernel,
            thirds(lower.shape) + [((16, 3 * third), F32)],
            (*dqkv[0], *dqkv[1], *weight),
            name="qkv_back",
        )
        fed = both_cores(links, partial)
        d0, d1, *_ = tie(*dqkv[0], *partial)
        dqkv = ([d0, d1], dqkv[1])
        rights = [((dqkv[0][g], dqkv[1][g]), (ctx[layer][0][g], ctx[layer][1][g])) for g in range(2)]
        grads = weight_grads(links, (in_low[layer], lower_low), rights)
        return lower, fed, grads, (row_sums, sums)

    def add(keep, *came):
        total = keep.astype(F32)
        for part in came:
            total = total + part.astype(F32)
        return total

    def swap_far(name, give):
        return links.swap_as(name + "_far", links.swap_far, give)

    def swap_near(name, keep, came):
        return links.swap_as(name + "_near", links.swap_near, add(keep, came).astype(BF16))

    def scatter_z(name, parts, masks):
        return links.swap_as(name, links.scatter_z, parts, masks)

    z_top, z_last = links.z_masks[:0:-1], z_one
    state = {}
    vectors = [None, None]

    grad_top = own_rows(cotangent) * row_mask
    encoded_low = low
    piece = rows_first(low)
    upper, fed, (f1k0, f1k1, f1g0, f1g1), fvec = ffn_back(1, (grad_top,), lambda g: g)
    *fed, f1g0, f1g1, piece = tie(*fed, f1g0, f1g1, piece)
    f1c1 = swap_far("ffn1_grad_1", f1g1)
    f1c0 = swap_far("ffn1_grad_0", f1g0)
    twin = rows_second(piece)

    def during1(dqkv, kv):
        d0, d1, kv, came = tie(*dqkv, kv, f1c1)
        state["f1"] = swap_near("ffn1_grad", f1k1, came)
        return [d0, d1], kv

    lower, fed, (a1k0, a1k1, a1g0, a1g1), avec = attn_back(1, (upper, *fed), during1)
    vectors[1] = (fvec, avec)
    *fed, a1g0, a1g1 = tie(*fed, a1g0, a1g1)
    a1c1 = swap_far("attn1_grad_1", a1g1)
    a1c0 = swap_far("attn1_grad_0", a1g0)

    upper, fed, (f0k0, f0k1, f0g0, f0g1), fvec = ffn_back(0, (lower, *fed), lambda g: g)
    *fed, f0g0, f0g1, a1c1, f1c0, f1near, twin = tie(*fed, f0g0, f0g1, a1c1, f1c0, state["f1"], twin)
    state["a1"] = swap_near("attn1_grad", a1k1, a1c1)
    state["f1"] = scatter_z("ffn1_grad_z1", add(f1k0, f1c0, f1near), z_top)
    encoded = all_rows(encoded_low, piece, twin)
    f0c1 = swap_far("ffn0_grad_1", f0g1)
    f0c0 = swap_far("ffn0_grad_0", f0g0)

    def during0(dqkv, kv):
        d0, d1, kv, f1_in, came, far, near = tie(*dqkv, kv, state["f1"][1], f0c1, a1c0, state["a1"])
        state["f0"] = swap_near("ffn0_grad", f0k1, came)
        state["a1"] = scatter_z("attn1_grad_z1", add(a1k0, far, near), z_top)
        state["f1"] = scatter_z("ffn1_grad_z2", add(state["f1"][0], f1_in), z_last)
        return [d0, d1], kv

    lower, fed, (a0k0, a0k1, a0g0, a0g1), avec = attn_back(0, (upper, *fed), during0)
    vectors[0] = (fvec, avec)
    *fed, a0g0, a0g1, a1_in = tie(*fed, a0g0, a0g1, state["a1"][1])
    a1s = scatter_z("attn1_grad_z2", add(state["a1"][0], a1_in), z_last)
    a0c1 = swap_far("attn0_grad_1", a0g1)
    a0c0 = swap_far("attn0_grad_0", a0g0)
    grad_hidden = call(final_sum_kernel, [(lower.shape, BF16)], (lower, *fed), name="input_grad")[0]
    sums = [part for f, a in vectors for part in (*f, *a)]
    vector, given = call(pack_kernel, [((8 * LAYERS, inputs.shape[1]), F32)] * 2, sums, name="vector_grads")

    attn_splits = ([(k * third, (k + 1) * third) for k in range(3)], [(3 * third, 4 * third)])
    ffn_splits = ([(0, wide)], [(wide, 2 * wide)])
    params = (attn_in, attn_out, ffn_up, ffn_down, head_bias, ffn_bias, row_params)
    states = [(params[i], moments[i], seconds[i]) for i in range(7)]

    attn_splits = ([(k * third, (k + 1) * third) for k in range(3)], [(3 * third, 4 * third)])
    ffn_splits = ([(0, wide)], [(wide, 2 * wide)])
    params = (attn_in, attn_out, ffn_up, ffn_down, head_bias, ffn_bias, row_params)
    states = [(params[i], moments[i], seconds[i]) for i in range(7)]

    grad_hidden, given, f0c0, f0near, f1_in = tie(grad_hidden, given, f0c0, state["f0"], state["f1"][1])
    f0s = scatter_z("ffn0_grad_z1", add(f0k0, f0c0, f0near), z_top)
    v_in = links.swap_as("vectors_x", links.swap_x, given)
    came, a0c0, v_in, a1_in = tie(a0c1, a0c0, v_in, a1s[1])
    a0near = swap_near("attn0_grad", a0k1, came)
    vector = vector + v_in
    grad_hidden, vector, f1s, a1s0 = tie(grad_hidden, vector, state["f1"][0], a1s[0])
    piece = rows_first(grad_hidden)
    ffn_new = adam_layer(1, ffn_splits, f1s, f1_in, states[2:4], None)
    attn_new = adam_layer(1, attn_splits, a1s0, a1_in, states[:2], None)
    a0near, vector, ffn_new[0], attn_new[0] = tie(a0near, vector, ffn_new[0], attn_new[0])
    a0s = scatter_z("attn0_grad_z1", add(a0k0, a0c0, a0near), z_top)
    v_in = links.swap_as("vectors_y", links.swap, vector, 4)
    f0_in, v_in, encoded = tie(f0s[1], v_in, encoded)
    f0s = scatter_z("ffn0_grad_z2", add(f0s[0], f0_in), z_last)
    vector = vector + v_in
    v_in = links.swap_as("vectors_z", links.swap_z, vector, links.z_masks[0])
    came, piece, v_in = tie(a0s[1], piece, v_in)
    a0s = scatter_z("attn0_grad_z2", add(a0s[0], came), z_last)
    twin = rows_second(piece)
    vector = vector + v_in
    for mask in links.z_masks[1:]:
        vector = vector + links.swap_as("vectors_z", links.swap_z, vector, mask)
    ffn_new = adam_layer(0, ffn_splits, f0s[0], f0s[1], states[2:4], ffn_new)
    input_grad = all_rows(grad_hidden, piece, twin)
    flat = [a for state in states[4:] for a in state]
    vector_new = call(vector_adam_kernel, [(a.shape, F32) for a in flat], (vector, *flat), name="vector_adam")
    a0_in, input_grad = tie(a0s[1], input_grad)
    attn_new = adam_layer(0, attn_splits, a0s[0], a0_in, states[:2], attn_new)

    new = [attn_new[:4], attn_new[4:], ffn_new[:4], ffn_new[4:]] + [vector_new[3 * i : 3 * i + 3] for i in range(3)]
    return (encoded, input_grad) + tuple(new[i][k] for k in range(3) for i in range(7)) + tuple(n[3] for n in new[:4])


def solution(mesh):
    n_dp = mesh.shape["dp"]
    row = P("dp", None)
    state = (
        P(None, None, "dp", "mp"),
        P(None, "dp", "mp"),
        P(None, "dp", "mp"),
        P(None, "dp", "mp"),
        P(None, None, "mp"),
        P(None, "mp"),
        P(),
    )

    def step(*args):
        return local(n_dp, *args)

    return jax.shard_map(
        step,
        mesh=mesh,
        in_specs=(row, row, row, P("dp")) + state * 3,
        out_specs=(row, row) + state * 3 + state[:4],
        check_vma=False,
    )
```

```python
import functools

import jax
import jax.numpy as jnp
from jax import lax
from jax.experimental import pallas as pl
from jax.experimental.pallas import tpu as pltpu
from jax.sharding import PartitionSpec as P

HEAD_DIM = 64
LAYERS = 2
ADAM_STEP = 10

EPS_NORM = 1e-12
EPS_ADAM = 1e-08
RATE_MATRIX = 0.04
RATE_VECTOR = 0.3
DECAY_MATRIX = 0.01

F32 = jnp.float32
BF16 = jnp.bfloat16
AXES = ("dp", "mp")
NN = ((1,), (0,))
NT = ((1,), (1,))
TN = ((0,), (0,))
PARTS = 3


def dot(a, b, dims):
    return lax.dot_general(a, b, (dims, ((), ())), preferred_element_type=F32)


def tie(*arrays):
    return lax.optimization_barrier(arrays)


class Links:
    def __init__(self, n_dp, rows):
        self.n_dp = n_dp
        self.count = n_dp * 4
        self.z_masks = [1 << bit for bit in reversed(range(n_dp.bit_length() - 2))]
        self.order = [0]
        for mask in self.z_masks:
            self.order += [place ^ mask for place in self.order]
        self.aligned = rows % 16 == 0
        dp_at = lax.axis_index("dp")
        mp_at = lax.axis_index("mp")
        self.at_x = mp_at // 2
        self.core = mp_at % 2
        self.at_y = dp_at % 2
        self.at_z = dp_at // 2
        self.places = jnp.stack([self.core, self.at_y, self.at_z, self.at_x]).astype(jnp.int32)

    def swap(self, array, mask0, mask1=None):
        mask1 = mask0 if mask1 is None else mask1
        pairs = [(i, i ^ (mask1 if i & 1 else mask0)) for i in range(self.count)]
        return lax.ppermute(array, AXES, pairs)

    def swap_as(self, name, swap, *args):
        with jax.named_scope(name):
            return swap(*args)

    def swap_core(self, array):
        return self.swap(array, 1)

    def swap_x(self, array):
        return self.swap(array, 2)

    def swap_z(self, array, mask):
        return self.swap(array, 8 * mask)

    def swap_near(self, array):
        return self.swap(array, 4, 2)

    def swap_far(self, array):
        return self.swap(array, 2, 4)

    def last_z(self, block, masks):
        for mask in masks[:-1]:
            block = jnp.concatenate([block, self.swap_z(block, mask)], axis=-3)
        return block, self.swap_z(block, masks[-1])

    def scatter_z(self, parts, masks):
        for mask in masks[:-1]:
            half = parts.shape[-3] // 2
            parts = parts[..., :half, :, :] + self.swap_z(parts[..., half:, :, :].astype(BF16), mask).astype(F32)
        half = parts.shape[-3] // 2
        return parts[..., :half, :, :], self.swap_z(parts[..., half:, :, :].astype(BF16), masks[-1])

    def assemble(self, *parts):
        if self.aligned:
            shape = parts[0].shape[-3:]
            kernel = functools.partial(assemble_kernel, self.order)
            outs = [((shape[0], 2) + shape[1:], parts[0].dtype)] * 2
            both = call(kernel, outs, (self.places, *parts), name="assemble")
        else:
            if len(parts) == 2:
                parts = [part[k] for part in parts for k in range(2)]
            order = jnp.array(inverse(self.order))[jnp.arange(parts[0].shape[0]) ^ self.at_z]
            block, near, far_block, far_near = (jnp.take(part, order, axis=0) for part in parts)
            first, low = self.core == 0, self.at_y == 0
            own_far = jnp.where(first, near, far_block)
            other_same = jnp.where(first, far_block, near)
            both = [
                jnp.stack([jnp.where(low, same, other), jnp.where(low, other, same)], axis=1)
                for same, other in ((block, own_far), (other_same, far_near))
            ]
        return [w.reshape(-1, w.shape[-1]) for w in both]


def inverse(order):
    return [order.index(place) for place in range(len(order))]


def assemble_kernel(order, places, *refs):
    *parts, own, other = refs
    if len(parts) == 2:
        parts = [part.at[k] for part in parts for k in range(2)]
    block, near, far_block, far_near = parts
    first, at_y, at_z = places[0] == 0, places[1], places[2]
    for m, distance in enumerate(order):
        j = distance ^ at_z
        own[j, at_y] = block[m]
        other[j, 1 - at_y] = far_near[m]

        @pl.when(first)
        def _(j=j, m=m):
            own[j, 1 - at_y] = near[m]
            other[j, at_y] = far_block[m]

        @pl.when(~first)
        def _(j=j, m=m):
            own[j, 1 - at_y] = far_block[m]
            other[j, at_y] = near[m]


def adam_step(master, moment, second, gradient, step_rate, decay_rate):
    correction = 1.0 - 0.5**ADAM_STEP
    moment_new = 0.5 * moment + 0.5 * gradient
    second_new = 0.5 * second + 0.5 * gradient * gradient
    update = (
        moment_new / correction / (jnp.sqrt(second_new / correction) + EPS_ADAM)
        + decay_rate * master
    )
    return (master - step_rate * update, moment_new, second_new)


def key_bias(limit, count, lanes):
    places = lax.broadcasted_iota(jnp.int32, (count, lanes), 0)
    return jnp.where(places < limit, 0.0, -1000000000.0)


def head_parts(qkv, far, swapped, g, h, full):
    third = qkv[g].shape[1] // 3
    k_at, v_at = third + h * HEAD_DIM, 2 * third + h * HEAD_DIM
    f_at = (g ^ swapped) * 2 * third + h * HEAD_DIM
    keys = qkv[g][:full, k_at : k_at + HEAD_DIM]
    values = qkv[g][:full, v_at : v_at + HEAD_DIM]
    keys_half = jnp.concatenate([qkv[g][full:, k_at : k_at + HEAD_DIM], far[:, f_at : f_at + HEAD_DIM]])
    f_at += third
    values_half = jnp.concatenate([qkv[g][full:, v_at : v_at + HEAD_DIM], far[:, f_at : f_at + HEAD_DIM]])
    return keys, values, keys_half, values_half


def attend_unit(keys, values, queries, bias_rows):
    scores = dot(keys, queries, NT) + bias_rows
    peak = jnp.max(scores, axis=0, keepdims=True)
    shifted = jnp.exp(scores - peak)
    total = jnp.sum(shifted, axis=0, keepdims=True)
    probs = (shifted * (1.0 / total)).astype(BF16)
    return dot(values, probs, TN), peak + jnp.log(total)


def full_kernel(limits, qkv0, qkv1, ctx0, ctx1, lse, bias):
    qkv, ctx = (qkv0, qkv1), (ctx0, ctx1)
    full, half = bias.shape
    third = qkv0.shape[1] // 3
    heads = third // HEAD_DIM
    bias[...] = key_bias(limits[0], full, half)
    for g in range(2):
        outs = [[], []]
        for h in range(heads):
            columns = slice(h * HEAD_DIM, (h + 1) * HEAD_DIM)
            keys = qkv[g][:full, third + h * HEAD_DIM : third + (h + 1) * HEAD_DIM]
            values = qkv[g][:full, 2 * third + h * HEAD_DIM : 2 * third + (h + 1) * HEAD_DIM]
            for part in range(2):
                rows = slice(part * half, (part + 1) * half)
                out, log_total = attend_unit(keys, values, qkv[g][rows, columns], bias[...])
                lse[g * heads + h : g * heads + h + 1, rows] = log_total
                outs[part].append(out)
        for part in range(2):
            rows = slice(part * half, (part + 1) * half)
            ctx[g][rows, :] = jnp.concatenate(outs[part], axis=0).T.astype(BF16)


def half_kernel(swapped, limits, qkv0, qkv1, far, ctx0, ctx1, lse, bias):
    qkv, ctx = (qkv0, qkv1), (ctx0, ctx1)
    half = far.shape[0]
    full = 2 * half
    heads = qkv0.shape[1] // 3 // HEAD_DIM
    bias[:half] = key_bias(limits[1], half, half)
    bias[half:] = key_bias(limits[2], half, half)
    for g in range(2):
        outs = []
        for h in range(heads):
            _, _, keys, values = head_parts(qkv, far, swapped, g, h, full)
            columns = slice(h * HEAD_DIM, (h + 1) * HEAD_DIM)
            out, log_total = attend_unit(keys, values, qkv[g][full:, columns], bias[...])
            lse[g * heads + h : g * heads + h + 1, :] = log_total
            outs.append(out)
        ctx[g][...] = jnp.concatenate(outs, axis=0).T.astype(BF16)


def attend_back_unit(keys, values, queries, grad_rows, log_total, bias_rows):
    probs = jnp.exp(dot(keys, queries, NT) + bias_rows - log_total)
    grad_probs = dot(values, grad_rows, NT)
    inner = jnp.sum(probs * grad_probs, axis=0, keepdims=True)
    grad_scores = (probs * (grad_probs - inner)).astype(BF16)
    grad_values = dot(probs.astype(BF16), grad_rows, NN)
    grad_keys = dot(grad_scores, queries, NN)
    grad_queries = dot(keys, grad_scores, TN)
    return grad_queries, grad_keys, grad_values


def half_back_kernel(swapped, limits, qkv0, qkv1, far, dctx0, dctx1, lse, dq0, dq1, own, sent, bias):
    qkv, dctx, dq = (qkv0, qkv1), (dctx0, dctx1), (dq0, dq1)
    half = far.shape[0]
    full = 2 * half
    third = qkv0.shape[1] // 3
    heads = third // HEAD_DIM
    bias[:half] = key_bias(limits[1], half, half)
    bias[half:] = key_bias(limits[2], half, half)
    for g in range(2):
        queries_out, keys_out, values_out = [], [], []
        for h in range(heads):
            _, _, keys, values = head_parts(qkv, far, swapped, g, h, full)
            columns = slice(h * HEAD_DIM, (h + 1) * HEAD_DIM)
            gq, gk, gv = attend_back_unit(
                keys,
                values,
                qkv[g][full:, columns],
                dctx[g][full:, columns],
                lse[g * heads + h : g * heads + h + 1, :],
                bias[...],
            )
            queries_out.append(gq)
            keys_out.append(gk)
            values_out.append(gv)
        dq[g][...] = jnp.concatenate(queries_out, axis=0).T.astype(BF16) * 0.125
        both = jnp.concatenate(keys_out + values_out, axis=1)
        own[:, 2 * third * g : 2 * third * (g + 1)] = both[:half]
        other = 1 - g
        sent[:, 2 * third * other : 2 * third * (other + 1)] = both[half:].astype(BF16)


def full_back_kernel(limits, qkv0, qkv1, dctx0, dctx1, lse, dqkv0, dqkv1, bias):
    qkv, dctx, dqkv = (qkv0, qkv1), (dctx0, dctx1), (dqkv0, dqkv1)
    full, half = bias.shape
    third = qkv0.shape[1] // 3
    heads = third // HEAD_DIM
    bias[...] = key_bias(limits[0], full, half)
    for g in range(2):
        queries_out, keys_out, values_out = [[], []], [], []
        for h in range(heads):
            columns = slice(h * HEAD_DIM, (h + 1) * HEAD_DIM)
            keys = qkv[g][:full, third + h * HEAD_DIM : third + (h + 1) * HEAD_DIM]
            values = qkv[g][:full, 2 * third + h * HEAD_DIM : 2 * third + (h + 1) * HEAD_DIM]
            sums = None
            for part in range(2):
                rows = slice(part * half, (part + 1) * half)
                gq, gk, gv = attend_back_unit(
                    keys,
                    values,
                    qkv[g][rows, columns],
                    dctx[g][rows, columns],
                    lse[g * heads + h : g * heads + h + 1, rows],
                    bias[...],
                )
                queries_out[part].append(gq)
                sums = (gk, gv) if sums is None else (sums[0] + gk, sums[1] + gv)
            keys_out.append(sums[0].astype(BF16))
            values_out.append(sums[1].astype(BF16))
        for part in range(2):
            rows = slice(part * half, (part + 1) * half)
            dqkv[g][rows, :third] = jnp.concatenate(queries_out[part], axis=0).T.astype(BF16) * 0.125
        dqkv[g][:, third:] = jnp.concatenate(keys_out + values_out, axis=1)


def half_fill_kernel(dq0, dq1, own, came, dqkv0, dqkv1):
    third = dq0.shape[1]
    for g, (dq, dqkv) in enumerate(((dq0, dqkv0), (dq1, dqkv1))):
        columns = slice(2 * third * g, 2 * third * (g + 1))
        both = (own[:, columns] + came[:, columns].astype(F32)).astype(BF16)
        dqkv[...] = jnp.concatenate([dq[...], both], axis=1)


VMEM = pl.BlockSpec(memory_space=pltpu.VMEM)
ANY = pl.BlockSpec(memory_space=pl.ANY)
SMEM = pl.BlockSpec(memory_space=pltpu.SMEM)
ROOM = pltpu.CompilerParams(vmem_limit_bytes=8 * 1024 * 1024)
CHEAP = pl.CostEstimate(flops=1, bytes_accessed=1, transcendentals=0)


def call(kernel, outs, ins, scratch=(), name=None, place=VMEM):
    specs = [SMEM if a.dtype == jnp.int32 else place for a in ins]
    results = pl.pallas_call(
        kernel,
        out_shape=[jax.ShapeDtypeStruct(s, d) for s, d in outs],
        in_specs=specs,
        out_specs=[VMEM] * len(outs),
        scratch_shapes=list(scratch),
        compiler_params=ROOM,
        cost_estimate=CHEAP,
        name=name,
    )(*ins)
    return list(results)


def attend_full(limits, qkv):
    tokens, third = qkv[0].shape[0], qkv[0].shape[1] // 3
    half = tokens // 3
    ctx0, ctx1, lse = call(
        full_kernel,
        [((2 * half, third), BF16)] * 2 + [((2 * third // HEAD_DIM, 2 * half), F32)],
        (limits, *qkv),
        [pltpu.VMEM((2 * half, half), F32)],
        name="attend_full",
    )
    return [ctx0, ctx1], lse


def attend_half(limits, qkv, far, swapped):
    half, third = far.shape[0], qkv[0].shape[1] // 3
    ctx0, ctx1, lse = call(
        functools.partial(half_kernel, swapped),
        [((half, third), BF16)] * 2 + [((2 * third // HEAD_DIM, half), F32)],
        (limits, *qkv, far),
        [pltpu.VMEM((2 * half, half), F32)],
        name="attend_half",
    )
    return [ctx0, ctx1], lse


def attend_half_back(limits, qkv, far, dctx, lse, swapped):
    half, third = far.shape[0], qkv[0].shape[1] // 3
    dq0, dq1, own, sent = call(
        functools.partial(half_back_kernel, swapped),
        [((half, third), BF16)] * 2 + [((half, 4 * third), F32), ((half, 4 * third), BF16)],
        (limits, *qkv, far, *dctx, lse),
        [pltpu.VMEM((2 * half, half), F32)],
        name="attend_half_back",
    )
    return (dq0, dq1), own, sent


def attend_full_back(limits, qkv, dctx, lse):
    half = qkv[0].shape[0] // 3
    return call(
        full_back_kernel,
        [((2 * half, qkv[0].shape[1]), BF16)] * 2,
        (limits, *qkv, *dctx, lse),
        [pltpu.VMEM((2 * half, half), F32)],
        name="attend_full_back",
    )


def fill_half(dq, own, came):
    shape = (own.shape[0], 3 * dq[0].shape[1])
    return call(half_fill_kernel, [(shape, BF16)] * 2, (*dq, own, came), name="fill_half")


def wgrad_kernel(count, pieces, order, places, *refs):
    step = count * pieces
    lefts, rights = refs[:count], (refs[count : count + step], refs[count + step : count + 2 * step])
    keep0, keep1, give0, give1, whole = refs[count + 2 * step :]
    first, at_y, at_z = places[0] == 0, places[1], places[2]
    rows = keep0.shape[1]
    turned = [left[...].T for left in lefts]
    for g in range(2):
        at = 0
        for k, left in enumerate(turned):
            right = [ref[...] for ref in rights[g][k * pieces : (k + 1) * pieces]]
            right = right[0] if pieces == 1 else jnp.concatenate(right)
            wide = right.shape[1]
            whole[:, at : at + wide] = dot(left, right, NN).astype(BF16)
            at += wide
        for y in range(2):
            same = at_y == y
            if g == 0:
                targets = ((same, keep0), (~same & first, keep1), (~same & ~first, give0))
            else:
                targets = ((same & first, give0), (same & ~first, keep1), (~same, give1))
            for when, ref in targets:

                @pl.when(when)
                def _(ref=ref, y=y):
                    for m, distance in enumerate(order):
                        from_row = pl.ds(pl.multiple_of((2 * (distance ^ at_z) + y) * rows, 16), rows)
                        ref[m] = whole[from_row, :]


def weight_grads(links, lefts, rights):
    features = lefts[0].shape[1]
    columns = sum(r[0].shape[1] for r in rights[0])
    blocks = links.n_dp // 2
    rows = features // links.n_dp
    if links.aligned:
        return call(
            functools.partial(wgrad_kernel, len(lefts), len(rights[0][0]), links.order),
            [((blocks, rows, columns), BF16)] * 4,
            (links.places, *lefts, *[piece for group in rights for right in group for piece in right]),
            [pltpu.VMEM((features, columns), BF16)],
            name="weight_grads",
        )
    low, first = links.at_y == 0, links.core == 0
    parts = []
    for group in rights:
        grad = jnp.concatenate([dot(a, jnp.concatenate(b), TN) for a, b in zip(lefts, group)], axis=1).astype(BF16)
        grad = jnp.take(grad.reshape(blocks, 2, rows, columns), jnp.array(links.order) ^ links.at_z, axis=0)
        parts += [jnp.where(low, grad[:, 0], grad[:, 1]), jnp.where(low, grad[:, 1], grad[:, 0])]
    own_same, own_far, other_same, other_far = parts
    return own_same, jnp.where(first, own_far, other_same), jnp.where(first, other_same, own_far), other_far


def both_cores(links, parts):
    return (*parts, *[links.swap_as("core", links.swap_core, part) for part in parts])


def in_parts(shape):
    return [((shape[0] // PARTS, shape[1]), BF16)] * PARTS


def core_sum(parts, at, rows):
    return parts[at][rows, :].astype(F32) + parts[at + PARTS][rows, :].astype(F32)


def put_parts(outs, at, value):
    step = outs[0].shape[0]
    done = 0
    while done < value.shape[0]:
        part, inner = divmod(at + done, step)
        count = min(step - inner, value.shape[0] - done)
        outs[part][inner : inner + count, :] = value[done : done + count, :].astype(BF16)
        done += count


def norm_kernel(step, *refs):
    parts, (residual, rows, out, low, scaled, inverse) = refs[: 2 * PARTS], refs[2 * PARTS :]
    wide = out.shape[1]
    third = parts[0].shape[0]
    for part in range(PARTS):

        @pl.loop(0, third // step)
        def _(i, part=part):
            inner = pl.ds(i * step, step)
            at = pl.ds(part * third + i * step, step)
            total = residual[at, :] + (core_sum(parts, part, inner) + rows[0:1, :])
            center = total - jnp.sum(total, axis=-1, keepdims=True) * (1.0 / wide)
            inv_std = lax.rsqrt(jnp.sum(center * center, axis=-1, keepdims=True) * (1.0 / wide) + EPS_NORM)
            normal = center * inv_std
            result = normal * rows[1:2, :] + rows[2:3, :]
            out[at, :] = result
            low[at, :] = result.astype(BF16)
            scaled[at, :] = normal
            inverse[at, :] = inv_std


def add_norm(parts, residual, rows):
    shape = residual.shape
    return call(
        functools.partial(norm_kernel, 64),
        [(shape, F32), (shape, BF16), (shape, F32), ((shape[0], 1), F32)],
        (*parts, residual, rows),
        name="add_norm",
    )


def norm_back_kernel(step, *refs):
    base, *parts, scaled, inverse, gain, out, low, sums = refs
    wide = out.shape[1]
    third = out.shape[0] // PARTS
    sums[...] = jnp.zeros_like(sums)
    for part in range(PARTS):

        @pl.loop(0, third // step)
        def _(i, part=part):
            at = pl.ds(part * third + i * step, step)
            grad = base[at, :]
            if parts:
                grad = grad + core_sum(parts, part, pl.ds(i * step, step))
            normal = scaled[at, :]
            upstream = grad * gain[...]
            mean_up = jnp.sum(upstream, axis=-1, keepdims=True) * (1.0 / wide)
            mean_cross = jnp.sum(upstream * normal, axis=-1, keepdims=True) * (1.0 / wide)
            result = inverse[at, :] * (upstream - mean_up - normal * mean_cross)
            out[at, :] = result
            low[at, :] = result.astype(BF16)
            for k, term in enumerate((result, grad * normal, grad)):
                sums[8 * k : 8 * (k + 1), :] += jnp.sum(term.reshape(-1, 8, wide), axis=0)


def norm_back(parts, scaled, inverse, gain):
    shape = scaled.shape
    return call(
        functools.partial(norm_back_kernel, 64),
        [(shape, F32), (shape, BF16), ((24, shape[1]), F32)],
        (*parts, scaled, inverse, gain),
        name="norm_back",
    )


def final_sum_kernel(base, *refs):
    parts, out = refs[: 2 * PARTS], refs[2 * PARTS]
    third = parts[0].shape[0]
    for part in range(PARTS):
        at = slice(part * third, (part + 1) * third)
        out[at, :] = (base[at, :] + core_sum(parts, part, slice(None))).astype(BF16)


def chunks(count, step=256):
    return [slice(at, at + step) for at in range(0, count, step)]


def qkv_kernel(low, w0, w1, bias, *refs):
    *other, out0, out1, extra = refs
    columns = out0.shape[1]
    third = columns // 3
    half = extra.shape[0]
    scale = jnp.where(lax.broadcasted_iota(jnp.int32, (1, columns), 1) < third, 0.125, 1.0)
    for g, (weight, out) in enumerate(((w0, out0), (w1, out1))):
        at = slice(2 * third * g, 2 * third * (g + 1))
        for rows in chunks(low.shape[0]):
            out[rows, :] = ((dot(low[rows, :], weight[:, :columns], NN) + bias[g : g + 1, :]) * scale).astype(BF16)
        if other:
            more = dot(other[0][...], weight[:, :columns], NN) + bias[g : g + 1, :]
            extra[:, at] = more[:, third:].astype(BF16)
        else:
            extra[:, at] = out[2 * half :, third:]


def project(low, weights, bias, other=None):
    tokens, columns = low.shape[0], bias.shape[1]
    half = tokens // 3
    ins = (low, *weights, bias) + (() if other is None else (other,))
    q0, q1, extra = call(
        qkv_kernel,
        [((tokens, columns), BF16)] * 2 + [((half, 4 * columns // 3), BF16)],
        ins,
        name="queries_keys_values",
    )
    return [q0, q1], extra


def row_thirds(full0, full1, half0, half1):
    half = half0.shape[0]
    rows = [slice(0, half), slice(half, 2 * half), slice(0, half)]
    return [((full0, full1) if k < 2 else (half0, half1), rows[k]) for k in range(3)]


def out_kernel(full0, full1, half0, half1, w0, w1, *outs):
    third = full0.shape[1]
    at = w0.shape[1] - third
    tails = (w0[:, at:], w1[:, at:])
    for k, (pair, rows) in enumerate(row_thirds(full0, full1, half0, half1)):
        put_parts(outs, k * half0.shape[0], dot(pair[0][rows, :], tails[0], NT) + dot(pair[1][rows, :], tails[1], NT))


def ffn_kernel(low, w0, w1, bias, act0, act1, slope0, slope1, *outs):
    wide = bias.shape[1]
    groups = ((w0, act0, slope0), (w1, act1, slope1))
    for rows in chunks(low.shape[0], 128):
        total = None
        for g, (weight, act, slope) in enumerate(groups):
            pre = dot(low[rows, :], weight[:, :wide], NN) + bias[g : g + 1, :]
            cdf = 0.5 * (1.0 + lax.erf(pre * 0.7071067811865476))
            slope[rows, :] = cdf + pre * (jnp.exp(-0.5 * pre * pre) * 0.3989422804014327)
            active = (pre * cdf).astype(BF16)
            act[rows, :] = active
            part = dot(active, weight[:, wide:], NT)
            total = part if total is None else total + part
        put_parts(outs, rows.start, total)


def feed_forward(low, weights, bias):
    shape = (low.shape[0], bias.shape[1])
    act0, act1, slope0, slope1, *partial = call(
        ffn_kernel,
        [(shape, BF16)] * 2 + [(shape, F32)] * 2 + in_parts(low.shape),
        (low, *weights, bias),
        name="feed_forward",
    )
    return [(act0, slope0), (act1, slope1)], partial


def add_rows(array):
    return jnp.sum(array.astype(F32).reshape(-1, 8, array.shape[1]), axis=0)


def ffn_back_kernel(low, w0, w1, slope0, slope1, pre0, pre1, sums):
    wide = slope0.shape[1]
    for g, (weight, slope, pre) in enumerate(((w0, slope0, pre0), (w1, slope1, pre1))):
        total = None
        for rows in chunks(low.shape[0]):
            grad = (dot(low[rows, :], weight[:, wide:], NN) * slope[rows, :]).astype(BF16)
            pre[rows, :] = grad
            part = add_rows(grad)
            total = part if total is None else total + part
        sums[8 * g : 8 * (g + 1), :] = total


def ffn_back_first(low, weights, slopes):
    shape = slopes[0].shape
    pre0, pre1, sums = call(
        ffn_back_kernel,
        [(shape, BF16)] * 2 + [((16, shape[1]), F32)],
        (low, *weights, *slopes),
        name="pre_grad",
    )
    return [pre0, pre1], sums


def back_out_kernel(d0, d1, w0, w1, *outs):
    wide = d0.shape[1]
    for rows in chunks(d0.shape[0]):
        put_parts(outs, rows.start, dot(d0[rows, :], w0[:, :wide], NT) + dot(d1[rows, :], w1[:, :wide], NT))


def qkv_back_kernel(full0, full1, half0, half1, w0, w1, *refs):
    *outs, sums = refs
    wide = full0.shape[1]
    totals = [None, None]
    for k, (pair, rows) in enumerate(row_thirds(full0, full1, half0, half1)):
        parts = [ref[rows, :] for ref in pair]
        put_parts(outs, k * half0.shape[0], dot(parts[0], w0[:, :wide], NT) + dot(parts[1], w1[:, :wide], NT))
        for g in range(2):
            part = add_rows(parts[g])
            totals[g] = part if totals[g] is None else totals[g] + part
    for g in range(2):
        sums[8 * g : 8 * (g + 1), :] = totals[g]


def context_grad_kernel(low, w0, w1, out0, out1):
    third = out0.shape[1]
    at = w0.shape[1] - third
    for weight, out in ((w0, out0), (w1, out1)):
        tail = weight[:, at:]
        for rows in chunks(low.shape[0]):
            out[rows, :] = dot(low[rows, :], tail, NN).astype(BF16)


def adam_kernel(splits, count, *refs):
    keep, came, *refs = refs
    ins, outs = refs[: 3 * len(splits)], refs[3 * len(splits) + count :]
    for i, ranges in enumerate(splits):
        master, moment, second = ins[3 * i : 3 * i + 3]
        results = outs[4 * i : 4 * i + 4]
        for k, (low, high) in enumerate(ranges):
            at = (0, k) if len(ranges) > 1 else (0,)
            grad = keep[0, :, low:high] + came[0, :, low:high].astype(F32)
            new = adam_step(master[at], moment[at], second[at], grad, RATE_MATRIX, DECAY_MATRIX)
            for ref, value in zip(results, (*new, new[0].astype(BF16))):
                ref[at] = value


def adam_layer(layer, splits, keep, came, states, before):
    def block(array):
        rest = array.shape[1:]
        return pl.BlockSpec((1,) + rest, lambda i, n=len(rest): (layer,) + (0,) * n)

    flat = [a for state in states for a in state]
    outs, specs = [], []
    for state in states:
        outs += [jax.ShapeDtypeStruct(state[0].shape, d) for d in (F32, F32, F32, BF16)]
        specs += [block(state[0])] * 4
    before = [] if before is None else before
    results = pl.pallas_call(
        functools.partial(adam_kernel, splits, len(before)),
        grid=(1,),
        out_shape=outs,
        in_specs=[VMEM] * 2 + [block(a) for a in flat] + [pl.BlockSpec(memory_space=pl.ANY)] * len(before),
        out_specs=specs,
        input_output_aliases={2 + len(flat) + i: i for i in range(len(before))},
        compiler_params=ROOM,
        cost_estimate=CHEAP,
        name="adam",
    )(keep, came, *flat, *before)
    return list(results)


def pack_kernel(*refs):
    *parts, own, other = refs
    own[...] = jnp.zeros_like(own)
    other[...] = jnp.zeros_like(other)
    for layer in range(LAYERS):
        upper, pre, lower, heads = parts[4 * layer : 4 * layer + 4]
        third = heads.shape[1] // 3

        def total(ref, k):
            return jnp.sum(ref[8 * k : 8 * (k + 1), :], axis=0, keepdims=True)

        rows = [(lower, 0), (upper, 0), (lower, 1), (lower, 2), (upper, 1), (upper, 2)]
        for k, row in enumerate(rows):
            value = total(*row)
            own[6 * layer + k : 6 * layer + k + 1, :] = value
            other[6 * layer + k : 6 * layer + k + 1, :] = value
        for g, ref in enumerate((own, other)):
            at = 6 * LAYERS + layer
            ref[at : at + 1, :] = total(pre, g)
            head = total(heads, g)
            at += LAYERS
            ref[at : at + 1, : 2 * third] = jnp.concatenate([head[:, :third], head[:, 2 * third :]], axis=1)


def vector_adam_kernel(grads, *refs):
    ins, outs = refs[:9], refs[9:]
    third = ins[0].shape[2]

    def update(i, at, grad):
        new = adam_step(ins[3 * i][at], ins[3 * i + 1][at], ins[3 * i + 2][at], grad, RATE_VECTOR, 0.0)
        for k, value in enumerate(new):
            outs[3 * i + k][at] = value

    for layer in range(LAYERS):
        at = 7 * LAYERS + layer
        for k in range(2):
            grad = grads[at : at + 1, k * third : (k + 1) * third]
            update(0, (layer, slice(k, k + 1)), grad)
        update(1, (slice(layer, layer + 1),), grads[at - LAYERS : at - LAYERS + 1, :])
        update(2, (layer,), grads[6 * layer : 6 * layer + 6, :])


def rows_kernel(places, low, piece, twin, out):
    first, at_x = places[0] == 0, places[3]
    half = low.shape[0] // 3
    part = piece.shape[0]

    def put(start, rows):
        out[pl.ds(pl.multiple_of(start, 8), rows.shape[0]), :] = rows.astype(F32)

    def put_other(upper, lower):
        put((1 - at_x) * 4 * half, upper[...])
        put((1 - at_x) * 4 * half + part, lower[: 2 * half - part, :])
        put(2 * half + (1 - at_x) * half, lower[2 * half - part :, :])

    put(at_x * 4 * half, low[: 2 * half, :])
    put(2 * half + at_x * half, low[2 * half :, :])

    @pl.when(first)
    def _():
        put_other(piece, twin)

    @pl.when(~first)
    def _():
        put_other(twin, piece)


def local(n_dp, *args):
    (
        inputs,
        cotangent,
        word_lengths,
        word_count,
        attn_in,
        attn_out,
        ffn_up,
        ffn_down,
        head_bias,
        ffn_bias,
        row_params,
    ) = args[:11]
    moments, seconds = args[11:18], args[18:25]
    links = Links(n_dp, attn_out.shape[1])
    at_x, core = links.at_x, links.core
    seq_len = inputs.shape[0] // word_count.shape[0]
    half = seq_len // 2
    third, wide = attn_in.shape[3], ffn_up.shape[2]

    def own_rows(array):
        whole = lax.dynamic_slice_in_dim(array, at_x * 2 * seq_len, seq_len)
        return jnp.concatenate([whole, lax.dynamic_slice_in_dim(array, seq_len + at_x * half, half)])

    def rows_first(low):
        part = low.shape[0] // 2
        return links.swap_as("rows_x", links.swap_x, lax.dynamic_slice_in_dim(low, core * part, part))

    def rows_second(piece):
        return links.swap_as("rows_core", links.swap_core, piece)

    def all_rows(low, piece, twin):
        return call(rows_kernel, [(inputs.shape, F32)], (links.places, low, piece, twin), name="all_rows")[0]

    def packed_attn(layer):
        attn = [attn_in[layer, 0], attn_in[layer, 1], attn_in[layer, 2], attn_out[layer]]
        return jnp.concatenate([a.astype(BF16) for a in attn], axis=1)[None]

    def packed_ffn(layer):
        return jnp.concatenate([ffn_up[layer].astype(BF16), ffn_down[layer].astype(BF16)], axis=1)[None]

    z_one, z_rest = links.z_masks[:1], links.z_masks[1:]
    join = jnp.concatenate

    a0 = packed_attn(0)
    a0_in = links.swap_as("attn0_z2", links.swap_z, a0, links.z_masks[0])
    later = join([packed_attn(1), packed_ffn(1)], axis=2)
    biases = jnp.concatenate([head_bias.reshape(-1), ffn_bias.reshape(-1)])
    a0_in, f0, later, biases = tie(a0_in, packed_ffn(0), later, biases)
    a0 = join([a0, a0_in])
    a0, a0_in = links.swap_as("attn0_z1", links.last_z, a0, z_rest)
    f0_in = links.swap_as("ffn0_z2", links.swap_z, f0, links.z_masks[0])
    later_near = links.swap_as("layer1_near", links.swap_near, later)
    bias_far = links.swap_as("biases", links.swap_x, biases)
    a0_in, f0_in, later_near, bias_far = tie(a0_in, f0_in, later_near, bias_far)
    a0, f0 = join([a0, a0_in]), join([f0, f0_in])
    near = links.swap_as("attn0_near", links.swap_near, a0)
    a0far = links.swap_as("attn0_far", links.swap_far, a0)
    f0, f0_in = links.swap_as("ffn0_z1", links.last_z, f0, z_rest)
    later = jnp.stack([later, later_near])
    a1, f1 = later[..., : 4 * third], later[..., 4 * third :]
    a1_in = links.swap_as("attn1_z2", links.swap_z, a1, links.z_masks[0])
    near, f1 = tie(near, f1)
    a0last = links.swap_as("attn0_far_near", links.swap_far, near)
    a0far, a0last, f0_in, a1_in, f1 = tie(a0far, a0last, f0_in, a1_in, f1)
    f0 = join([f0, f0_in])
    f0near = links.swap_as("ffn0_near", links.swap_near, f0)
    f0far = links.swap_as("ffn0_far", links.swap_far, f0)
    a1 = join([a1, a1_in], axis=1)
    a1, a1_in = links.swap_as("attn1_z1", links.last_z, a1, z_rest)
    f1_in = links.swap_as("ffn1_z2", links.swap_z, f1, links.z_masks[0])
    a0 = links.assemble(a0, near, a0far, a0last)
    head_b = (head_bias, bias_far[: head_bias.size].reshape(head_bias.shape))
    ffn_b = (ffn_bias, bias_far[head_bias.size :].reshape(ffn_bias.shape))
    zeros = jnp.zeros((third,), F32)
    qkv_b = [
        jnp.stack([jnp.concatenate([b[layer, 0], zeros, b[layer, 1]]) for b in head_b]) for layer in range(LAYERS)
    ]
    ffn_b = [jnp.stack([b[layer] for b in ffn_b]) for layer in range(LAYERS)]

    slots = jnp.arange(word_lengths.shape[1], dtype=jnp.int32)
    used = jnp.sum(jnp.where(slots[None, :] < word_count[:, None], word_lengths, 0), axis=1)
    used_full = jnp.where(at_x == 0, used[0], used[2])
    limits = jnp.stack([used_full, used[1] - at_x * half, used[1] - (1 - at_x) * half]).astype(jnp.int32)
    places = jnp.arange(seq_len, dtype=jnp.int32)
    row_mask = jnp.concatenate([places < limits[0], places[:half] < limits[1]]).astype(F32)[:, None]

    hidden = own_rows(inputs)
    low_other = lax.dynamic_slice_in_dim(inputs, seq_len + (1 - at_x) * half, half).astype(BF16)
    in_low = [hidden.astype(BF16), None]
    qkv, far, ctx, lse = [None] * 2, [None] * 2, [None] * 2, [None] * 2
    weight_a, weight_f = [a0, None], [None, None]

    def out_part(layer):
        return call(
            out_kernel, in_parts(hidden.shape), (*ctx[layer][0], *ctx[layer][1], *weight_a[layer]), name="attention_out"
        )

    norms = [None] * 2
    ffn_parts = [None] * 2

    row_parts = [
        [jnp.stack([row_params[i, k] for k in ks]) for ks in ((0, 2, 3), (1, 4, 5))] for i in range(LAYERS)
    ]
    row_parts = [
        [jnp.stack([row_params[i, k] for k in ks]) for ks in ((0, 2, 3), (1, 4, 5))] for i in range(LAYERS)
    ]
    qkv[0], far[0] = project(in_low[0], a0, qkv_b[0], low_other)
    whole, whole_lse = attend_full(limits, qkv[0])
    *whole, f0near, a1_in, f1_in = tie(*whole, f0near, a1_in, f1_in)
    f0last = links.swap_as("ffn0_far_near", links.swap_far, f0near)
    a1 = join([a1, a1_in], axis=1)
    f1 = join([f1, f1_in], axis=1)
    f1, f1_in = links.swap_as("ffn1_z1", links.last_z, f1, z_rest)
    split, split_lse = attend_half(limits, qkv[0], far[0], 0)
    *split, f0far = tie(*split, f0far)
    ctx[0], lse[0] = (whole, split), (whole_lse, split_lse)
    normed, normed_low, scaled_one, inv_one = add_norm(both_cores(links, out_part(0)), hidden, row_parts[0][0])
    normed_low, f0last, a1 = tie(normed_low, f0last, a1)
    a1far = links.swap_as("attn1_far", links.swap_far, a1)
    f0 = links.assemble(f0, f0near, f0far, f0last)
    weight_f[0] = f0
    ffn_parts[0], partial = feed_forward(normed_low, f0, ffn_b[0])
    *partial, a1far, f1_in = tie(*partial, a1far, f1_in)
    f1_own, f1_near = join([f1[0], f1_in[0]]), join([f1[1], f1_in[1]])
    f1far = links.swap_as("ffn1_far", links.swap_far, f1_own)
    fed = both_cores(links, partial)
    hidden, low, scaled_two, inv_two = add_norm(fed, normed, row_parts[0][1])
    norms[0] = (normed_low, scaled_one, inv_one, scaled_two, inv_two)

    a1 = links.assemble(a1, a1far)
    weight_a[1] = a1
    in_low[1] = low
    qkv[1], sent = project(low, a1, qkv_b[1])
    far[1] = links.swap_as("keys_values", links.swap_x, sent)
    whole, whole_lse = attend_full(limits, qkv[1])
    *whole, far[1], f1_near, f1far = tie(*whole, far[1], f1_near, f1far)
    f1last = links.swap_as("ffn1_far_near", links.swap_far, f1_near)
    split, split_lse = attend_half(limits, qkv[1], far[1], 1)
    ctx[1], lse[1] = (whole, split), (whole_lse, split_lse)
    fed = both_cores(links, out_part(1))
    normed, normed_low, scaled_one, inv_one = add_norm(fed, hidden, row_parts[1][0])
    normed_low, f1last = tie(normed_low, f1last)
    f1 = links.assemble(f1_own, f1_near, f1far, f1last)
    weight_f[1] = f1
    ffn_parts[1], partial = feed_forward(normed_low, f1, ffn_b[1])
    fed = both_cores(links, partial)
    hidden, low, scaled_two, inv_two = add_norm(fed, normed, row_parts[1][1])
    norms[1] = (normed_low, scaled_one, inv_one, scaled_two, inv_two)
    state = {}

    def ffn_back(layer, grad_parts, middle):
        normed_low, _, _, scaled_two, inv_two = norms[layer]
        upper, upper_low, row_sums = norm_back(grad_parts, scaled_two, inv_two, row_params[layer, 4:5])
        slopes = [part[1] for part in ffn_parts[layer]]
        grad_pre, pre_sums = ffn_back_first(upper_low, weight_f[layer], slopes)
        grad_pre = middle(grad_pre)
        partial = call(back_out_kernel, in_parts(upper.shape), (*grad_pre, *weight_f[layer]), name="up_back")
        fed = both_cores(links, partial)
        g0, g1, *_ = tie(*grad_pre, *partial)
        grad_pre = [g0, g1]
        grads = weight_grads(
            links,
            (normed_low, upper_low),
            [((grad_pre[g],), (ffn_parts[layer][g][0],)) for g in range(2)],
        )
        return upper, fed, grads, (row_sums, pre_sums)

    def attn_back(layer, grad_parts, first, early, during):
        _, scaled_one, inv_one, _, _ = norms[layer]
        lower, lower_low, row_sums = norm_back(grad_parts, scaled_one, inv_one, row_params[layer, 2:3])
        lower_low = first(lower_low)
        weight = weight_a[layer]
        shape = (lower.shape[0], third)
        dctx = call(context_grad_kernel, [(shape, BF16)] * 2, (lower_low, *weight), name="context_grad")
        dq, own, sent = attend_half_back(limits, qkv[layer], far[layer], dctx, lse[layer][1], layer)
        d0, d1, sent = early(*dctx, sent)
        came = links.swap_as("keys_values_grad", links.swap_x, sent)
        dqkv = attend_full_back(limits, qkv[layer], (d0, d1), lse[layer][0])
        dqkv, came = during(dqkv, came)
        dqkv = (dqkv, fill_half(dq, own, came))
        *partial, sums = call(
            qkv_back_kernel,
            in_parts(lower.shape) + [((16, 3 * third), F32)],
            (*dqkv[0], *dqkv[1], *weight),
            name="qkv_back",
        )
        fed = both_cores(links, partial)
        d0, d1, *_ = tie(*dqkv[0], *partial)
        dqkv = ([d0, d1], dqkv[1])
        rights = [((dqkv[0][g], dqkv[1][g]), (ctx[layer][0][g], ctx[layer][1][g])) for g in range(2)]
        grads = weight_grads(links, (in_low[layer], lower_low), rights)
        return lower, fed, grads, (row_sums, sums)

    def add(keep, *came):
        total = keep.astype(F32)
        for part in came:
            total = total + part.astype(F32)
        return total

    def swap_far(name, give):
        return links.swap_as(name + "_far", links.swap_far, give)

    def swap_near(name, keep, came):
        return links.swap_as(name + "_near", links.swap_near, add(keep, came).astype(BF16))

    def scatter_z(name, parts, masks):
        return links.swap_as(name, links.scatter_z, parts, masks)

    z_top, z_last = links.z_masks[:0:-1], z_one
    state = {}
    vectors = [None, None]

    grad_top = own_rows(cotangent) * row_mask
    encoded_low = low
    piece = rows_first(low)
    upper, fed, (f1k0, f1k1, f1g0, f1g1), fvec = ffn_back(1, (grad_top,), lambda g: g)
    *fed, f1g0, f1g1, piece = tie(*fed, f1g0, f1g1, piece)
    f1c1 = swap_far("ffn1_grad_1", f1g1)
    twin = rows_second(piece)

    def during1(dqkv, kv):
        d0, d1, kv, state["f1_far_1"], given = tie(*dqkv, kv, f1c1, f1g0)
        state["f1_far_0"] = swap_far("ffn1_grad_0", given)
        return [d0, d1], kv

    lower, fed, (a1k0, a1k1, a1g0, a1g1), avec = attn_back(1, (upper, *fed), lambda low: low, tie, during1)
    vectors[1] = (fvec, avec)
    *fed, a1g0, a1g1 = tie(*fed, a1g0, a1g1)
    a1c = swap_far("attn1_grad", jnp.stack([a1g0, a1g1]))

    def middle0(grad_pre):
        g0, g1, came = tie(*grad_pre, state["f1_far_0"])
        state["f1"] = scatter_z("ffn1_grad_z1", jnp.stack([add(f1k0, came), add(f1k1, state["f1_far_1"])]), z_top)
        return [g0, g1]

    upper, fed, (f0k0, f0k1, f0g0, f0g1), fvec = ffn_back(0, (lower, *fed), middle0)
    *fed, f0g0, f0g1, a1c = tie(*fed, f0g0, f0g1, a1c)
    state["a1_near"] = swap_near("attn1_grad", a1k1, a1c[1])
    f0c1 = swap_far("ffn0_grad_1", f0g1)
    f0c0 = swap_far("ffn0_grad_0", f0g0)


    def first0(lower_low):
        lower_low, state["twin"] = tie(lower_low, twin)
        return lower_low

    def during0(dqkv, kv):
        d0, d1, kv, came, f1_in, near = tie(*dqkv, kv, f0c1, state["f1"][1], state["a1_near"])
        state["f0"] = swap_near("ffn0_grad", f0k1, came)
        state["a1"] = scatter_z("attn1_grad_z1", add(a1k0, a1c[0], near), z_top)
        state["f1"] = scatter_z("ffn1_grad_z2", add(state["f1"][0], f1_in), z_last)
        return [d0, d1], kv

    lower, fed, (a0k0, a0k1, a0g0, a0g1), avec = attn_back(0, (upper, *fed), first0, tie, during0)
    vectors[0] = (fvec, avec)
    sums = [part for f, a in vectors for part in (*f, *a)]
    vector, given = call(pack_kernel, [((8 * LAYERS, inputs.shape[1]), F32)] * 2, sums, name="vector_grads")
    *fed, a0g0, a0g1, given = tie(*fed, a0g0, a0g1, given)
    a0c1 = swap_far("attn0_grad_1", a0g1)
    a0c0 = swap_far("attn0_grad_0", a0g0)
    v_in = links.swap_as("vectors_x", links.swap_x, given)
    grad_hidden = call(final_sum_kernel, [(lower.shape, BF16)], (lower, *fed), name="input_grad")[0]
    attn_splits = ([(k * third, (k + 1) * third) for k in range(3)], [(3 * third, 4 * third)])
    ffn_splits = ([(0, wide)], [(wide, 2 * wide)])
    params = (attn_in, attn_out, ffn_up, ffn_down, head_bias, ffn_bias, row_params)
    states = [(params[i], moments[i], seconds[i]) for i in range(7)]

    attn_splits = ([(k * third, (k + 1) * third) for k in range(3)], [(3 * third, 4 * third)])
    ffn_splits = ([(0, wide)], [(wide, 2 * wide)])
    params = (attn_in, attn_out, ffn_up, ffn_down, head_bias, ffn_bias, row_params)
    states = [(params[i], moments[i], seconds[i]) for i in range(7)]

    order = links.places
    grad_hidden, v_in, f0c0, f0near, a1_in, order = tie(
        grad_hidden, v_in, f0c0, state["f0"], state["a1"][1], order
    )
    f0s = scatter_z("ffn0_grad_z1", add(f0k0, f0c0, f0near), z_top)
    a1s = scatter_z("attn1_grad_z2", add(state["a1"][0], a1_in), z_last)
    vector = vector + v_in
    v_in = links.swap_as("vectors_y", links.swap, vector, 4)
    encoded = all_rows(encoded_low, piece, state["twin"])
    came, a0c0, v_in, f1_in, encoded, order = tie(a0c1, a0c0, v_in, state["f1"][1], encoded, order)
    a0near = swap_near("attn0_grad", a0k1, came)
    f1s = add(state["f1"][0], f1_in)
    f1near = links.swap_as("ffn1_grad_near", links.swap_near, f1s[1].astype(BF16))
    vector = vector + v_in
    v_in = links.swap_as("vectors_z", links.swap_z, vector, links.z_masks[0])
    a0near, v_in, f1near, a1_in, order = tie(a0near, v_in, f1near, a1s[1], order)
    a1s = (a1s[0], a1_in)
    a0s = scatter_z("attn0_grad_z1", add(a0k0, a0c0, a0near), z_top)
    vector = vector + v_in
    for mask in links.z_masks[1:]:
        vector = vector + links.swap_as("vectors_z", links.swap_z, vector, mask)
    f0_in, grad_hidden, order = tie(f0s[1], grad_hidden, order)
    f0s = scatter_z("ffn0_grad_z2", add(f0s[0], f0_in), z_last)
    piece = rows_first(grad_hidden)
    ffn_new = adam_layer(1, ffn_splits, f1s[0], f1near, states[2:4], None)
    attn_new = adam_layer(1, attn_splits, *a1s, states[:2], None)
    came, f0_in, vector, ffn_new[0], attn_new[0], order = tie(
        a0s[1], f0s[1], vector, ffn_new[0], attn_new[0], order
    )
    a0s = scatter_z("attn0_grad_z2", add(a0s[0], came), z_last)
    piece, order = tie(piece, order)
    twin = rows_second(piece)
    flat = [a for state in states[4:] for a in state]
    vector_new = call(vector_adam_kernel, [(a.shape, F32) for a in flat], (vector, *flat), name="vector_adam")
    ffn_new = adam_layer(0, ffn_splits, f0s[0], f0_in, states[2:4], ffn_new)
    input_grad = all_rows(grad_hidden, piece, twin)
    a0_in, input_grad, order = tie(a0s[1], input_grad, order)
    attn_new = adam_layer(0, attn_splits, a0s[0], a0_in, states[:2], attn_new)

    new = [attn_new[:4], attn_new[4:], ffn_new[:4], ffn_new[4:]] + [vector_new[3 * i : 3 * i + 3] for i in range(3)]
    return (encoded, input_grad) + tuple(new[i][k] for k in range(3) for i in range(7)) + tuple(n[3] for n in new[:4])


def solution(mesh):
    n_dp = mesh.shape["dp"]
    row = P("dp", None)
    state = (
        P(None, None, "dp", "mp"),
        P(None, "dp", "mp"),
        P(None, "dp", "mp"),
        P(None, "dp", "mp"),
        P(None, None, "mp"),
        P(None, "mp"),
        P(),
    )

    def step(*args):
        return local(n_dp, *args)

    return jax.shard_map(
        step,
        mesh=mesh,
        in_specs=(row, row, row, P("dp")) + state * 3,
        out_specs=(row, row) + state * 3 + state[:4],
        check_vma=False,
    )
```

```python
import functools

import jax
import jax.numpy as jnp
from jax import lax
from jax.experimental import pallas as pl
from jax.experimental.pallas import tpu as pltpu
from jax.sharding import PartitionSpec as P

HEAD_DIM = 64
LAYERS = 2
ADAM_STEP = 10

EPS_NORM = 1e-12
EPS_ADAM = 1e-08
RATE_MATRIX = 0.04
RATE_VECTOR = 0.3
DECAY_MATRIX = 0.01

F32 = jnp.float32
BF16 = jnp.bfloat16
AXES = ("dp", "mp")
NN = ((1,), (0,))
NT = ((1,), (1,))
TN = ((0,), (0,))
PARTS = 3


def dot(a, b, dims):
    return lax.dot_general(a, b, (dims, ((), ())), preferred_element_type=F32)


def tie(*arrays):
    return lax.optimization_barrier(arrays)


class Links:
    def __init__(self, n_dp, rows):
        self.n_dp = n_dp
        self.count = n_dp * 4
        self.z_masks = [1 << bit for bit in reversed(range(n_dp.bit_length() - 2))]
        self.order = [0]
        for mask in self.z_masks:
            self.order += [place ^ mask for place in self.order]
        self.aligned = rows % 16 == 0
        dp_at = lax.axis_index("dp")
        mp_at = lax.axis_index("mp")
        self.at_x = mp_at // 2
        self.core = mp_at % 2
        self.at_y = dp_at % 2
        self.at_z = dp_at // 2
        self.places = jnp.stack([self.core, self.at_y, self.at_z, self.at_x]).astype(jnp.int32)

    def swap(self, array, mask0, mask1=None):
        mask1 = mask0 if mask1 is None else mask1
        pairs = [(i, i ^ (mask1 if i & 1 else mask0)) for i in range(self.count)]
        return lax.ppermute(array, AXES, pairs)

    def swap_as(self, name, swap, *args):
        with jax.named_scope(name):
            return swap(*args)

    def swap_core(self, array):
        return self.swap(array, 1)

    def swap_x(self, array):
        return self.swap(array, 2)

    def swap_z(self, array, mask):
        return self.swap(array, 8 * mask)

    def swap_near(self, array):
        return self.swap(array, 4, 2)

    def swap_far(self, array):
        return self.swap(array, 2, 4)

    def last_z(self, block, masks):
        for mask in masks[:-1]:
            block = jnp.concatenate([block, self.swap_z(block, mask)], axis=-3)
        return block, self.swap_z(block, masks[-1])

    def scatter_z(self, parts, masks):
        for mask in masks[:-1]:
            half = parts.shape[-3] // 2
            parts = parts[..., :half, :, :] + self.swap_z(parts[..., half:, :, :].astype(BF16), mask).astype(F32)
        half = parts.shape[-3] // 2
        return parts[..., :half, :, :], self.swap_z(parts[..., half:, :, :].astype(BF16), masks[-1])

    def assemble(self, *parts):
        if self.aligned:
            shape = parts[0].shape[-3:]
            kernel = functools.partial(assemble_kernel, self.order)
            outs = [((shape[0], 2) + shape[1:], parts[0].dtype)] * 2
            both = call(kernel, outs, (self.places, *parts), name="assemble")
        else:
            if len(parts) == 2:
                parts = [part[k] for part in parts for k in range(2)]
            order = jnp.array(inverse(self.order))[jnp.arange(parts[0].shape[0]) ^ self.at_z]
            block, near, far_block, far_near = (jnp.take(part, order, axis=0) for part in parts)
            first, low = self.core == 0, self.at_y == 0
            own_far = jnp.where(first, near, far_block)
            other_same = jnp.where(first, far_block, near)
            both = [
                jnp.stack([jnp.where(low, same, other), jnp.where(low, other, same)], axis=1)
                for same, other in ((block, own_far), (other_same, far_near))
            ]
        return [w.reshape(-1, w.shape[-1]) for w in both]


def inverse(order):
    return [order.index(place) for place in range(len(order))]


def assemble_kernel(order, places, *refs):
    *parts, own, other = refs
    if len(parts) == 2:
        parts = [part.at[k] for part in parts for k in range(2)]
    block, near, far_block, far_near = parts
    first, at_y, at_z = places[0] == 0, places[1], places[2]
    for m, distance in enumerate(order):
        j = distance ^ at_z
        own[j, at_y] = block[m]
        other[j, 1 - at_y] = far_near[m]

        @pl.when(first)
        def _(j=j, m=m):
            own[j, 1 - at_y] = near[m]
            other[j, at_y] = far_block[m]

        @pl.when(~first)
        def _(j=j, m=m):
            own[j, 1 - at_y] = far_block[m]
            other[j, at_y] = near[m]


def adam_step(master, moment, second, gradient, step_rate, decay_rate):
    correction = 1.0 - 0.5**ADAM_STEP
    moment_new = 0.5 * moment + 0.5 * gradient
    second_new = 0.5 * second + 0.5 * gradient * gradient
    update = (
        moment_new / correction / (jnp.sqrt(second_new / correction) + EPS_ADAM)
        + decay_rate * master
    )
    return (master - step_rate * update, moment_new, second_new)


def key_bias(limit, count, lanes):
    places = lax.broadcasted_iota(jnp.int32, (count, lanes), 0)
    return jnp.where(places < limit, 0.0, -1000000000.0)


def head_parts(qkv, far, swapped, g, h, full):
    third = qkv[g].shape[1] // 3
    k_at, v_at = third + h * HEAD_DIM, 2 * third + h * HEAD_DIM
    f_at = (g ^ swapped) * 2 * third + h * HEAD_DIM
    keys = qkv[g][:full, k_at : k_at + HEAD_DIM]
    values = qkv[g][:full, v_at : v_at + HEAD_DIM]
    keys_half = jnp.concatenate([qkv[g][full:, k_at : k_at + HEAD_DIM], far[:, f_at : f_at + HEAD_DIM]])
    f_at += third
    values_half = jnp.concatenate([qkv[g][full:, v_at : v_at + HEAD_DIM], far[:, f_at : f_at + HEAD_DIM]])
    return keys, values, keys_half, values_half


def attend_unit(keys, values, queries, bias_rows):
    scores = dot(keys, queries, NT) + bias_rows
    peak = jnp.max(scores, axis=0, keepdims=True)
    shifted = jnp.exp(scores - peak)
    total = jnp.sum(shifted, axis=0, keepdims=True)
    probs = (shifted * (1.0 / total)).astype(BF16)
    return dot(values, probs, TN), peak + jnp.log(total)


def full_kernel(limits, qkv0, qkv1, ctx0, ctx1, lse, bias):
    qkv, ctx = (qkv0, qkv1), (ctx0, ctx1)
    full, half = bias.shape
    third = qkv0.shape[1] // 3
    heads = third // HEAD_DIM
    bias[...] = key_bias(limits[0], full, half)
    for g in range(2):
        outs = [[], []]
        for h in range(heads):
            columns = slice(h * HEAD_DIM, (h + 1) * HEAD_DIM)
            keys = qkv[g][:full, third + h * HEAD_DIM : third + (h + 1) * HEAD_DIM]
            values = qkv[g][:full, 2 * third + h * HEAD_DIM : 2 * third + (h + 1) * HEAD_DIM]
            for part in range(2):
                rows = slice(part * half, (part + 1) * half)
                out, log_total = attend_unit(keys, values, qkv[g][rows, columns], bias[...])
                lse[g * heads + h : g * heads + h + 1, rows] = log_total
                outs[part].append(out)
        for part in range(2):
            rows = slice(part * half, (part + 1) * half)
            ctx[g][rows, :] = jnp.concatenate(outs[part], axis=0).T.astype(BF16)


def half_kernel(swapped, limits, qkv0, qkv1, far, ctx0, ctx1, lse, bias):
    qkv, ctx = (qkv0, qkv1), (ctx0, ctx1)
    half = far.shape[0]
    full = 2 * half
    heads = qkv0.shape[1] // 3 // HEAD_DIM
    bias[:half] = key_bias(limits[1], half, half)
    bias[half:] = key_bias(limits[2], half, half)
    for g in range(2):
        outs = []
        for h in range(heads):
            _, _, keys, values = head_parts(qkv, far, swapped, g, h, full)
            columns = slice(h * HEAD_DIM, (h + 1) * HEAD_DIM)
            out, log_total = attend_unit(keys, values, qkv[g][full:, columns], bias[...])
            lse[g * heads + h : g * heads + h + 1, :] = log_total
            outs.append(out)
        ctx[g][...] = jnp.concatenate(outs, axis=0).T.astype(BF16)


def attend_back_unit(keys, values, queries, grad_rows, log_total, bias_rows):
    probs = jnp.exp(dot(keys, queries, NT) + bias_rows - log_total)
    grad_probs = dot(values, grad_rows, NT)
    inner = jnp.sum(probs * grad_probs, axis=0, keepdims=True)
    grad_scores = (probs * (grad_probs - inner)).astype(BF16)
    grad_values = dot(probs.astype(BF16), grad_rows, NN)
    grad_keys = dot(grad_scores, queries, NN)
    grad_queries = dot(keys, grad_scores, TN)
    return grad_queries, grad_keys, grad_values


def half_back_kernel(swapped, limits, qkv0, qkv1, far, dctx0, dctx1, lse, dq0, dq1, own, sent, bias):
    qkv, dctx, dq = (qkv0, qkv1), (dctx0, dctx1), (dq0, dq1)
    half = far.shape[0]
    full = 2 * half
    third = qkv0.shape[1] // 3
    heads = third // HEAD_DIM
    bias[:half] = key_bias(limits[1], half, half)
    bias[half:] = key_bias(limits[2], half, half)
    for g in range(2):
        queries_out, keys_out, values_out = [], [], []
        for h in range(heads):
            _, _, keys, values = head_parts(qkv, far, swapped, g, h, full)
            columns = slice(h * HEAD_DIM, (h + 1) * HEAD_DIM)
            gq, gk, gv = attend_back_unit(
                keys,
                values,
                qkv[g][full:, columns],
                dctx[g][full:, columns],
                lse[g * heads + h : g * heads + h + 1, :],
                bias[...],
            )
            queries_out.append(gq)
            keys_out.append(gk)
            values_out.append(gv)
        dq[g][...] = jnp.concatenate(queries_out, axis=0).T.astype(BF16) * 0.125
        both = jnp.concatenate(keys_out + values_out, axis=1)
        own[:, 2 * third * g : 2 * third * (g + 1)] = both[:half]
        other = 1 - g
        sent[:, 2 * third * other : 2 * third * (other + 1)] = both[half:].astype(BF16)


def full_back_kernel(limits, qkv0, qkv1, dctx0, dctx1, lse, dqkv0, dqkv1, bias):
    qkv, dctx, dqkv = (qkv0, qkv1), (dctx0, dctx1), (dqkv0, dqkv1)
    full, half = bias.shape
    third = qkv0.shape[1] // 3
    heads = third // HEAD_DIM
    bias[...] = key_bias(limits[0], full, half)
    for g in range(2):
        queries_out, keys_out, values_out = [[], []], [], []
        for h in range(heads):
            columns = slice(h * HEAD_DIM, (h + 1) * HEAD_DIM)
            keys = qkv[g][:full, third + h * HEAD_DIM : third + (h + 1) * HEAD_DIM]
            values = qkv[g][:full, 2 * third + h * HEAD_DIM : 2 * third + (h + 1) * HEAD_DIM]
            sums = None
            for part in range(2):
                rows = slice(part * half, (part + 1) * half)
                gq, gk, gv = attend_back_unit(
                    keys,
                    values,
                    qkv[g][rows, columns],
                    dctx[g][rows, columns],
                    lse[g * heads + h : g * heads + h + 1, rows],
                    bias[...],
                )
                queries_out[part].append(gq)
                sums = (gk, gv) if sums is None else (sums[0] + gk, sums[1] + gv)
            keys_out.append(sums[0].astype(BF16))
            values_out.append(sums[1].astype(BF16))
        for part in range(2):
            rows = slice(part * half, (part + 1) * half)
            dqkv[g][rows, :third] = jnp.concatenate(queries_out[part], axis=0).T.astype(BF16) * 0.125
        dqkv[g][:, third:] = jnp.concatenate(keys_out + values_out, axis=1)


def half_fill_kernel(dq0, dq1, own, came, dqkv0, dqkv1):
    third = dq0.shape[1]
    for g, (dq, dqkv) in enumerate(((dq0, dqkv0), (dq1, dqkv1))):
        columns = slice(2 * third * g, 2 * third * (g + 1))
        both = (own[:, columns] + came[:, columns].astype(F32)).astype(BF16)
        dqkv[...] = jnp.concatenate([dq[...], both], axis=1)


VMEM = pl.BlockSpec(memory_space=pltpu.VMEM)
ANY = pl.BlockSpec(memory_space=pl.ANY)
SMEM = pl.BlockSpec(memory_space=pltpu.SMEM)
ROOM = pltpu.CompilerParams(vmem_limit_bytes=8 * 1024 * 1024)
CHEAP = pl.CostEstimate(flops=1, bytes_accessed=1, transcendentals=0)


def call(kernel, outs, ins, scratch=(), name=None, place=VMEM):
    specs = [SMEM if a.dtype == jnp.int32 else place for a in ins]
    results = pl.pallas_call(
        kernel,
        out_shape=[jax.ShapeDtypeStruct(s, d) for s, d in outs],
        in_specs=specs,
        out_specs=[VMEM] * len(outs),
        scratch_shapes=list(scratch),
        compiler_params=ROOM,
        cost_estimate=CHEAP,
        name=name,
    )(*ins)
    return list(results)


def attend_full(limits, qkv):
    tokens, third = qkv[0].shape[0], qkv[0].shape[1] // 3
    half = tokens // 3
    ctx0, ctx1, lse = call(
        full_kernel,
        [((2 * half, third), BF16)] * 2 + [((2 * third // HEAD_DIM, 2 * half), F32)],
        (limits, *qkv),
        [pltpu.VMEM((2 * half, half), F32)],
        name="attend_full",
    )
    return [ctx0, ctx1], lse


def attend_half(limits, qkv, far, swapped):
    half, third = far.shape[0], qkv[0].shape[1] // 3
    ctx0, ctx1, lse = call(
        functools.partial(half_kernel, swapped),
        [((half, third), BF16)] * 2 + [((2 * third // HEAD_DIM, half), F32)],
        (limits, *qkv, far),
        [pltpu.VMEM((2 * half, half), F32)],
        name="attend_half",
    )
    return [ctx0, ctx1], lse


def attend_half_back(limits, qkv, far, dctx, lse, swapped):
    half, third = far.shape[0], qkv[0].shape[1] // 3
    dq0, dq1, own, sent = call(
        functools.partial(half_back_kernel, swapped),
        [((half, third), BF16)] * 2 + [((half, 4 * third), F32), ((half, 4 * third), BF16)],
        (limits, *qkv, far, *dctx, lse),
        [pltpu.VMEM((2 * half, half), F32)],
        name="attend_half_back",
    )
    return (dq0, dq1), own, sent


def attend_full_back(limits, qkv, dctx, lse):
    half = qkv[0].shape[0] // 3
    return call(
        full_back_kernel,
        [((2 * half, qkv[0].shape[1]), BF16)] * 2,
        (limits, *qkv, *dctx, lse),
        [pltpu.VMEM((2 * half, half), F32)],
        name="attend_full_back",
    )


def fill_half(dq, own, came):
    shape = (own.shape[0], 3 * dq[0].shape[1])
    return call(half_fill_kernel, [(shape, BF16)] * 2, (*dq, own, came), name="fill_half")


def wgrad_kernel(count, pieces, order, places, *refs):
    step = count * pieces
    lefts, rights = refs[:count], (refs[count : count + step], refs[count + step : count + 2 * step])
    keep0, keep1, give0, give1, whole = refs[count + 2 * step :]
    first, at_y, at_z = places[0] == 0, places[1], places[2]
    rows = keep0.shape[1]
    turned = [left[...].T for left in lefts]
    for g in range(2):
        at = 0
        for k, left in enumerate(turned):
            right = [ref[...] for ref in rights[g][k * pieces : (k + 1) * pieces]]
            right = right[0] if pieces == 1 else jnp.concatenate(right)
            wide = right.shape[1]
            whole[:, at : at + wide] = dot(left, right, NN).astype(BF16)
            at += wide
        for y in range(2):
            same = at_y == y
            if g == 0:
                targets = ((same, keep0), (~same & first, keep1), (~same & ~first, give0))
            else:
                targets = ((same & first, give0), (same & ~first, keep1), (~same, give1))
            for when, ref in targets:

                @pl.when(when)
                def _(ref=ref, y=y):
                    for m, distance in enumerate(order):
                        from_row = pl.ds(pl.multiple_of((2 * (distance ^ at_z) + y) * rows, 16), rows)
                        ref[m] = whole[from_row, :]


def weight_grads(links, lefts, rights):
    features = lefts[0].shape[1]
    columns = sum(r[0].shape[1] for r in rights[0])
    blocks = links.n_dp // 2
    rows = features // links.n_dp
    if links.aligned:
        return call(
            functools.partial(wgrad_kernel, len(lefts), len(rights[0][0]), links.order),
            [((blocks, rows, columns), BF16)] * 4,
            (links.places, *lefts, *[piece for group in rights for right in group for piece in right]),
            [pltpu.VMEM((features, columns), BF16)],
            name="weight_grads",
        )
    low, first = links.at_y == 0, links.core == 0
    parts = []
    for group in rights:
        grad = jnp.concatenate([dot(a, jnp.concatenate(b), TN) for a, b in zip(lefts, group)], axis=1).astype(BF16)
        grad = jnp.take(grad.reshape(blocks, 2, rows, columns), jnp.array(links.order) ^ links.at_z, axis=0)
        parts += [jnp.where(low, grad[:, 0], grad[:, 1]), jnp.where(low, grad[:, 1], grad[:, 0])]
    own_same, own_far, other_same, other_far = parts
    return own_same, jnp.where(first, own_far, other_same), jnp.where(first, other_same, own_far), other_far


def both_cores(links, parts):
    return (*parts, *[links.swap_as("core", links.swap_core, part) for part in parts])


def in_parts(shape):
    return [((shape[0] // PARTS, shape[1]), BF16)] * PARTS


def core_sum(parts, at, rows):
    return parts[at][rows, :].astype(F32) + parts[at + PARTS][rows, :].astype(F32)


def put_parts(outs, at, value):
    step = outs[0].shape[0]
    done = 0
    while done < value.shape[0]:
        part, inner = divmod(at + done, step)
        count = min(step - inner, value.shape[0] - done)
        outs[part][inner : inner + count, :] = value[done : done + count, :].astype(BF16)
        done += count


def norm_kernel(step, *refs):
    parts, (residual, rows, out, low, scaled, inverse) = refs[: 2 * PARTS], refs[2 * PARTS :]
    wide = out.shape[1]
    third = parts[0].shape[0]
    for part in range(PARTS):

        @pl.loop(0, third // step)
        def _(i, part=part):
            inner = pl.ds(i * step, step)
            at = pl.ds(part * third + i * step, step)
            total = residual[at, :] + (core_sum(parts, part, inner) + rows[0:1, :])
            center = total - jnp.sum(total, axis=-1, keepdims=True) * (1.0 / wide)
            inv_std = lax.rsqrt(jnp.sum(center * center, axis=-1, keepdims=True) * (1.0 / wide) + EPS_NORM)
            normal = center * inv_std
            result = normal * rows[1:2, :] + rows[2:3, :]
            out[at, :] = result
            low[at, :] = result.astype(BF16)
            scaled[at, :] = normal
            inverse[at, :] = inv_std


def add_norm(parts, residual, rows):
    shape = residual.shape
    return call(
        functools.partial(norm_kernel, 64),
        [(shape, F32), (shape, BF16), (shape, F32), ((shape[0], 1), F32)],
        (*parts, residual, rows),
        name="add_norm",
    )


def norm_back_kernel(step, *refs):
    base, *parts, scaled, inverse, gain, out, low, sums = refs
    wide = out.shape[1]
    third = out.shape[0] // PARTS
    sums[...] = jnp.zeros_like(sums)
    for part in range(PARTS):

        @pl.loop(0, third // step)
        def _(i, part=part):
            at = pl.ds(part * third + i * step, step)
            grad = base[at, :]
            if parts:
                grad = grad + core_sum(parts, part, pl.ds(i * step, step))
            normal = scaled[at, :]
            upstream = grad * gain[...]
            mean_up = jnp.sum(upstream, axis=-1, keepdims=True) * (1.0 / wide)
            mean_cross = jnp.sum(upstream * normal, axis=-1, keepdims=True) * (1.0 / wide)
            result = inverse[at, :] * (upstream - mean_up - normal * mean_cross)
            out[at, :] = result
            low[at, :] = result.astype(BF16)
            for k, term in enumerate((result, grad * normal, grad)):
                sums[8 * k : 8 * (k + 1), :] += jnp.sum(term.reshape(-1, 8, wide), axis=0)


def norm_back(parts, scaled, inverse, gain):
    shape = scaled.shape
    return call(
        functools.partial(norm_back_kernel, 64),
        [(shape, F32), (shape, BF16), ((24, shape[1]), F32)],
        (*parts, scaled, inverse, gain),
        name="norm_back",
    )


def final_sum_kernel(base, *refs):
    parts, out = refs[: 2 * PARTS], refs[2 * PARTS]
    third = parts[0].shape[0]
    for part in range(PARTS):
        at = slice(part * third, (part + 1) * third)
        out[at, :] = (base[at, :] + core_sum(parts, part, slice(None))).astype(BF16)


def chunks(count, step=256):
    return [slice(at, at + step) for at in range(0, count, step)]


def qkv_kernel(low, w0, w1, bias, *refs):
    *other, out0, out1, extra = refs
    columns = out0.shape[1]
    third = columns // 3
    half = extra.shape[0]
    scale = jnp.where(lax.broadcasted_iota(jnp.int32, (1, columns), 1) < third, 0.125, 1.0)
    for g, (weight, out) in enumerate(((w0, out0), (w1, out1))):
        at = slice(2 * third * g, 2 * third * (g + 1))
        for rows in chunks(low.shape[0]):
            out[rows, :] = ((dot(low[rows, :], weight[:, :columns], NN) + bias[g : g + 1, :]) * scale).astype(BF16)
        if other:
            more = dot(other[0][...], weight[:, :columns], NN) + bias[g : g + 1, :]
            extra[:, at] = more[:, third:].astype(BF16)
        else:
            extra[:, at] = out[2 * half :, third:]


def project(low, weights, bias, other=None):
    tokens, columns = low.shape[0], bias.shape[1]
    half = tokens // 3
    ins = (low, *weights, bias) + (() if other is None else (other,))
    q0, q1, extra = call(
        qkv_kernel,
        [((tokens, columns), BF16)] * 2 + [((half, 4 * columns // 3), BF16)],
        ins,
        name="queries_keys_values",
    )
    return [q0, q1], extra


def row_thirds(full0, full1, half0, half1):
    half = half0.shape[0]
    rows = [slice(0, half), slice(half, 2 * half), slice(0, half)]
    return [((full0, full1) if k < 2 else (half0, half1), rows[k]) for k in range(3)]


def out_kernel(full0, full1, half0, half1, w0, w1, *outs):
    third = full0.shape[1]
    at = w0.shape[1] - third
    tails = (w0[:, at:], w1[:, at:])
    for k, (pair, rows) in enumerate(row_thirds(full0, full1, half0, half1)):
        put_parts(outs, k * half0.shape[0], dot(pair[0][rows, :], tails[0], NT) + dot(pair[1][rows, :], tails[1], NT))


def ffn_kernel(low, w0, w1, bias, act0, act1, slope0, slope1, *outs):
    wide = bias.shape[1]
    groups = ((w0, act0, slope0), (w1, act1, slope1))
    for rows in chunks(low.shape[0], 128):
        total = None
        for g, (weight, act, slope) in enumerate(groups):
            pre = dot(low[rows, :], weight[:, :wide], NN) + bias[g : g + 1, :]
            cdf = 0.5 * (1.0 + lax.erf(pre * 0.7071067811865476))
            slope[rows, :] = cdf + pre * (jnp.exp(-0.5 * pre * pre) * 0.3989422804014327)
            active = (pre * cdf).astype(BF16)
            act[rows, :] = active
            part = dot(active, weight[:, wide:], NT)
            total = part if total is None else total + part
        put_parts(outs, rows.start, total)


def feed_forward(low, weights, bias):
    shape = (low.shape[0], bias.shape[1])
    act0, act1, slope0, slope1, *partial = call(
        ffn_kernel,
        [(shape, BF16)] * 2 + [(shape, F32)] * 2 + in_parts(low.shape),
        (low, *weights, bias),
        name="feed_forward",
    )
    return [(act0, slope0), (act1, slope1)], partial


def add_rows(array):
    return jnp.sum(array.astype(F32).reshape(-1, 8, array.shape[1]), axis=0)


def ffn_back_kernel(low, w0, w1, slope0, slope1, pre0, pre1, sums):
    wide = slope0.shape[1]
    for g, (weight, slope, pre) in enumerate(((w0, slope0, pre0), (w1, slope1, pre1))):
        total = None
        for rows in chunks(low.shape[0]):
            grad = (dot(low[rows, :], weight[:, wide:], NN) * slope[rows, :]).astype(BF16)
            pre[rows, :] = grad
            part = add_rows(grad)
            total = part if total is None else total + part
        sums[8 * g : 8 * (g + 1), :] = total


def ffn_back_first(low, weights, slopes):
    shape = slopes[0].shape
    pre0, pre1, sums = call(
        ffn_back_kernel,
        [(shape, BF16)] * 2 + [((16, shape[1]), F32)],
        (low, *weights, *slopes),
        name="pre_grad",
    )
    return [pre0, pre1], sums


def back_out_kernel(d0, d1, w0, w1, *outs):
    wide = d0.shape[1]
    for rows in chunks(d0.shape[0]):
        put_parts(outs, rows.start, dot(d0[rows, :], w0[:, :wide], NT) + dot(d1[rows, :], w1[:, :wide], NT))


def qkv_back_kernel(full0, full1, half0, half1, w0, w1, *refs):
    *outs, sums = refs
    wide = full0.shape[1]
    totals = [None, None]
    for k, (pair, rows) in enumerate(row_thirds(full0, full1, half0, half1)):
        parts = [ref[rows, :] for ref in pair]
        put_parts(outs, k * half0.shape[0], dot(parts[0], w0[:, :wide], NT) + dot(parts[1], w1[:, :wide], NT))
        for g in range(2):
            part = add_rows(parts[g])
            totals[g] = part if totals[g] is None else totals[g] + part
    for g in range(2):
        sums[8 * g : 8 * (g + 1), :] = totals[g]


def context_grad_kernel(low, w0, w1, out0, out1):
    third = out0.shape[1]
    at = w0.shape[1] - third
    for weight, out in ((w0, out0), (w1, out1)):
        tail = weight[:, at:]
        for rows in chunks(low.shape[0]):
            out[rows, :] = dot(low[rows, :], tail, NN).astype(BF16)


def adam_kernel(splits, count, *refs):
    keep, came, *refs = refs
    ins, outs = refs[: 3 * len(splits)], refs[3 * len(splits) + count :]
    for i, ranges in enumerate(splits):
        master, moment, second = ins[3 * i : 3 * i + 3]
        results = outs[4 * i : 4 * i + 4]
        for k, (low, high) in enumerate(ranges):
            at = (0, k) if len(ranges) > 1 else (0,)
            grad = keep[0, :, low:high] + came[0, :, low:high].astype(F32)
            new = adam_step(master[at], moment[at], second[at], grad, RATE_MATRIX, DECAY_MATRIX)
            for ref, value in zip(results, (*new, new[0].astype(BF16))):
                ref[at] = value


def adam_layer(layer, splits, keep, came, states, before):
    def block(array):
        rest = array.shape[1:]
        return pl.BlockSpec((1,) + rest, lambda i, n=len(rest): (layer,) + (0,) * n)

    flat = [a for state in states for a in state]
    outs, specs = [], []
    for state in states:
        outs += [jax.ShapeDtypeStruct(state[0].shape, d) for d in (F32, F32, F32, BF16)]
        specs += [block(state[0])] * 4
    before = [] if before is None else before
    results = pl.pallas_call(
        functools.partial(adam_kernel, splits, len(before)),
        grid=(1,),
        out_shape=outs,
        in_specs=[VMEM] * 2 + [block(a) for a in flat] + [pl.BlockSpec(memory_space=pl.ANY)] * len(before),
        out_specs=specs,
        input_output_aliases={2 + len(flat) + i: i for i in range(len(before))},
        compiler_params=ROOM,
        cost_estimate=CHEAP,
        name="adam",
    )(keep, came, *flat, *before)
    return list(results)


def pack_kernel(*refs):
    *parts, own, other = refs
    own[...] = jnp.zeros_like(own)
    other[...] = jnp.zeros_like(other)
    for layer in range(LAYERS):
        upper, pre, lower, heads = parts[4 * layer : 4 * layer + 4]
        third = heads.shape[1] // 3

        def total(ref, k):
            return jnp.sum(ref[8 * k : 8 * (k + 1), :], axis=0, keepdims=True)

        rows = [(lower, 0), (upper, 0), (lower, 1), (lower, 2), (upper, 1), (upper, 2)]
        for k, row in enumerate(rows):
            value = total(*row)
            own[6 * layer + k : 6 * layer + k + 1, :] = value
            other[6 * layer + k : 6 * layer + k + 1, :] = value
        for g, ref in enumerate((own, other)):
            at = 6 * LAYERS + layer
            ref[at : at + 1, :] = total(pre, g)
            head = total(heads, g)
            at += LAYERS
            ref[at : at + 1, : 2 * third] = jnp.concatenate([head[:, :third], head[:, 2 * third :]], axis=1)


def vector_adam_kernel(grads, *refs):
    ins, outs = refs[:9], refs[9:]
    third = ins[0].shape[2]

    def update(i, at, grad):
        new = adam_step(ins[3 * i][at], ins[3 * i + 1][at], ins[3 * i + 2][at], grad, RATE_VECTOR, 0.0)
        for k, value in enumerate(new):
            outs[3 * i + k][at] = value

    for layer in range(LAYERS):
        at = 7 * LAYERS + layer
        for k in range(2):
            grad = grads[at : at + 1, k * third : (k + 1) * third]
            update(0, (layer, slice(k, k + 1)), grad)
        update(1, (slice(layer, layer + 1),), grads[at - LAYERS : at - LAYERS + 1, :])
        update(2, (layer,), grads[6 * layer : 6 * layer + 6, :])


def rows_kernel(places, low, piece, twin, out):
    first, at_x = places[0] == 0, places[3]
    half = low.shape[0] // 3
    part = piece.shape[0]

    def put(start, rows):
        out[pl.ds(pl.multiple_of(start, 8), rows.shape[0]), :] = rows.astype(F32)

    def put_other(upper, lower):
        put((1 - at_x) * 4 * half, upper[...])
        put((1 - at_x) * 4 * half + part, lower[: 2 * half - part, :])
        put(2 * half + (1 - at_x) * half, lower[2 * half - part :, :])

    put(at_x * 4 * half, low[: 2 * half, :])
    put(2 * half + at_x * half, low[2 * half :, :])

    @pl.when(first)
    def _():
        put_other(piece, twin)

    @pl.when(~first)
    def _():
        put_other(twin, piece)


def local(n_dp, *args):
    (
        inputs,
        cotangent,
        word_lengths,
        word_count,
        attn_in,
        attn_out,
        ffn_up,
        ffn_down,
        head_bias,
        ffn_bias,
        row_params,
    ) = args[:11]
    moments, seconds = args[11:18], args[18:25]
    links = Links(n_dp, attn_out.shape[1])
    at_x, core = links.at_x, links.core
    seq_len = inputs.shape[0] // word_count.shape[0]
    half = seq_len // 2
    third, wide = attn_in.shape[3], ffn_up.shape[2]

    def own_rows(array):
        whole = lax.dynamic_slice_in_dim(array, at_x * 2 * seq_len, seq_len)
        return jnp.concatenate([whole, lax.dynamic_slice_in_dim(array, seq_len + at_x * half, half)])

    def rows_first(low):
        part = low.shape[0] // 2
        return links.swap_as("rows_x", links.swap_x, lax.dynamic_slice_in_dim(low, core * part, part))

    def rows_second(piece):
        return links.swap_as("rows_core", links.swap_core, piece)

    def all_rows(low, piece, twin):
        return call(rows_kernel, [(inputs.shape, F32)], (links.places, low, piece, twin), name="all_rows")[0]

    def packed_attn(layer):
        attn = [attn_in[layer, 0], attn_in[layer, 1], attn_in[layer, 2], attn_out[layer]]
        return jnp.concatenate([a.astype(BF16) for a in attn], axis=1)[None]

    def packed_ffn(layer):
        return jnp.concatenate([ffn_up[layer].astype(BF16), ffn_down[layer].astype(BF16)], axis=1)[None]

    z_one, z_rest = links.z_masks[:1], links.z_masks[1:]
    join = jnp.concatenate

    a0 = packed_attn(0)
    a0_in = links.swap_as("attn0_z2", links.swap_z, a0, links.z_masks[0])
    later = join([packed_attn(1), packed_ffn(1)], axis=2)
    biases = jnp.concatenate([head_bias.reshape(-1), ffn_bias.reshape(-1)])
    a0_in, f0, later, biases = tie(a0_in, packed_ffn(0), later, biases)
    a0 = join([a0, a0_in])
    a0, a0_in = links.swap_as("attn0_z1", links.last_z, a0, z_rest)
    f0_in = links.swap_as("ffn0_z2", links.swap_z, f0, links.z_masks[0])
    later_near = links.swap_as("layer1_near", links.swap_near, later)
    bias_far = links.swap_as("biases", links.swap_x, biases)
    a0_in, f0_in, later_near, bias_far = tie(a0_in, f0_in, later_near, bias_far)
    a0, f0 = join([a0, a0_in]), join([f0, f0_in])
    near = links.swap_as("attn0_near", links.swap_near, a0)
    a0far = links.swap_as("attn0_far", links.swap_far, a0)
    f0, f0_in = links.swap_as("ffn0_z1", links.last_z, f0, z_rest)
    later = jnp.stack([later, later_near])
    a1, f1 = later[..., : 4 * third], later[..., 4 * third :]
    a1_in = links.swap_as("attn1_z2", links.swap_z, a1, links.z_masks[0])
    near, f1 = tie(near, f1)
    a0last = links.swap_as("attn0_far_near", links.swap_far, near)
    a0far, a0last, f0_in, a1_in, f1 = tie(a0far, a0last, f0_in, a1_in, f1)
    f0 = join([f0, f0_in])
    f0near = links.swap_as("ffn0_near", links.swap_near, f0)
    f0far = links.swap_as("ffn0_far", links.swap_far, f0)
    a1 = join([a1, a1_in], axis=1)
    a1, a1_in = links.swap_as("attn1_z1", links.last_z, a1, z_rest)
    f1_in = links.swap_as("ffn1_z2", links.swap_z, f1, links.z_masks[0])
    a0 = links.assemble(a0, near, a0far, a0last)
    head_b = (head_bias, bias_far[: head_bias.size].reshape(head_bias.shape))
    ffn_b = (ffn_bias, bias_far[head_bias.size :].reshape(ffn_bias.shape))
    zeros = jnp.zeros((third,), F32)
    qkv_b = [
        jnp.stack([jnp.concatenate([b[layer, 0], zeros, b[layer, 1]]) for b in head_b]) for layer in range(LAYERS)
    ]
    ffn_b = [jnp.stack([b[layer] for b in ffn_b]) for layer in range(LAYERS)]

    slots = jnp.arange(word_lengths.shape[1], dtype=jnp.int32)
    used = jnp.sum(jnp.where(slots[None, :] < word_count[:, None], word_lengths, 0), axis=1)
    used_full = jnp.where(at_x == 0, used[0], used[2])
    limits = jnp.stack([used_full, used[1] - at_x * half, used[1] - (1 - at_x) * half]).astype(jnp.int32)
    places = jnp.arange(seq_len, dtype=jnp.int32)
    row_mask = jnp.concatenate([places < limits[0], places[:half] < limits[1]]).astype(F32)[:, None]

    hidden = own_rows(inputs)
    low_other = lax.dynamic_slice_in_dim(inputs, seq_len + (1 - at_x) * half, half).astype(BF16)
    in_low = [hidden.astype(BF16), None]
    qkv, far, ctx, lse = [None] * 2, [None] * 2, [None] * 2, [None] * 2
    weight_a, weight_f = [a0, None], [None, None]

    def out_part(layer):
        return call(
            out_kernel, in_parts(hidden.shape), (*ctx[layer][0], *ctx[layer][1], *weight_a[layer]), name="attention_out"
        )

    norms = [None] * 2
    ffn_parts = [None] * 2

    row_parts = [
        [jnp.stack([row_params[i, k] for k in ks]) for ks in ((0, 2, 3), (1, 4, 5))] for i in range(LAYERS)
    ]
    row_parts = [
        [jnp.stack([row_params[i, k] for k in ks]) for ks in ((0, 2, 3), (1, 4, 5))] for i in range(LAYERS)
    ]
    qkv[0], far[0] = project(in_low[0], a0, qkv_b[0], low_other)
    whole, whole_lse = attend_full(limits, qkv[0])
    *whole, f0near, a1_in, f1_in = tie(*whole, f0near, a1_in, f1_in)
    f0last = links.swap_as("ffn0_far_near", links.swap_far, f0near)
    a1 = join([a1, a1_in], axis=1)
    f1 = join([f1, f1_in], axis=1)
    far[0], f1 = tie(far[0], f1)
    f1, f1_in = links.swap_as("ffn1_z1", links.last_z, f1, z_rest)
    split, split_lse = attend_half(limits, qkv[0], far[0], 0)
    *split, f0far = tie(*split, f0far)
    ctx[0], lse[0] = (whole, split), (whole_lse, split_lse)
    normed, normed_low, scaled_one, inv_one = add_norm(both_cores(links, out_part(0)), hidden, row_parts[0][0])
    normed_low, f0last, a1 = tie(normed_low, f0last, a1)
    a1far = links.swap_as("attn1_far", links.swap_far, a1)
    f0 = links.assemble(f0, f0near, f0far, f0last)
    weight_f[0] = f0
    ffn_parts[0], partial = feed_forward(normed_low, f0, ffn_b[0])
    *partial, a1far, f1_in = tie(*partial, a1far, f1_in)
    f1_own, f1_near = join([f1[0], f1_in[0]]), join([f1[1], f1_in[1]])
    f1far = links.swap_as("ffn1_far", links.swap_far, f1_own)
    fed = both_cores(links, partial)
    hidden, low, scaled_two, inv_two = add_norm(fed, normed, row_parts[0][1])
    norms[0] = (normed_low, scaled_one, inv_one, scaled_two, inv_two)

    a1 = links.assemble(a1, a1far)
    weight_a[1] = a1
    in_low[1] = low
    qkv[1], sent = project(low, a1, qkv_b[1])
    far[1] = links.swap_as("keys_values", links.swap_x, sent)
    whole, whole_lse = attend_full(limits, qkv[1])
    *whole, far[1], f1_near, f1far = tie(*whole, far[1], f1_near, f1far)
    f1last = links.swap_as("ffn1_far_near", links.swap_far, f1_near)
    split, split_lse = attend_half(limits, qkv[1], far[1], 1)
    ctx[1], lse[1] = (whole, split), (whole_lse, split_lse)
    fed = both_cores(links, out_part(1))
    normed, normed_low, scaled_one, inv_one = add_norm(fed, hidden, row_parts[1][0])
    normed_low, f1last = tie(normed_low, f1last)
    f1 = links.assemble(f1_own, f1_near, f1far, f1last)
    weight_f[1] = f1
    ffn_parts[1], partial = feed_forward(normed_low, f1, ffn_b[1])
    fed = both_cores(links, partial)
    hidden, low, scaled_two, inv_two = add_norm(fed, normed, row_parts[1][1])
    norms[1] = (normed_low, scaled_one, inv_one, scaled_two, inv_two)
    state = {}

    def ffn_back(layer, grad_parts, middle):
        normed_low, _, _, scaled_two, inv_two = norms[layer]
        upper, upper_low, row_sums = norm_back(grad_parts, scaled_two, inv_two, row_params[layer, 4:5])
        slopes = [part[1] for part in ffn_parts[layer]]
        grad_pre, pre_sums = ffn_back_first(upper_low, weight_f[layer], slopes)
        grad_pre = middle(grad_pre)
        partial = call(back_out_kernel, in_parts(upper.shape), (*grad_pre, *weight_f[layer]), name="up_back")
        fed = both_cores(links, partial)
        g0, g1, *_ = tie(*grad_pre, *partial)
        grad_pre = [g0, g1]
        grads = weight_grads(
            links,
            (normed_low, upper_low),
            [((grad_pre[g],), (ffn_parts[layer][g][0],)) for g in range(2)],
        )
        return upper, fed, grads, (row_sums, pre_sums)

    def attn_back(layer, grad_parts, first, early, during):
        _, scaled_one, inv_one, _, _ = norms[layer]
        lower, lower_low, row_sums = norm_back(grad_parts, scaled_one, inv_one, row_params[layer, 2:3])
        lower_low = first(lower_low)
        weight = weight_a[layer]
        shape = (lower.shape[0], third)
        dctx = call(context_grad_kernel, [(shape, BF16)] * 2, (lower_low, *weight), name="context_grad")
        dq, own, sent = attend_half_back(limits, qkv[layer], far[layer], dctx, lse[layer][1], layer)
        d0, d1, sent = early(*dctx, sent)
        came = links.swap_as("keys_values_grad", links.swap_x, sent)
        dqkv = attend_full_back(limits, qkv[layer], (d0, d1), lse[layer][0])
        dqkv, came = during(dqkv, came)
        dqkv = (dqkv, fill_half(dq, own, came))
        *partial, sums = call(
            qkv_back_kernel,
            in_parts(lower.shape) + [((16, 3 * third), F32)],
            (*dqkv[0], *dqkv[1], *weight),
            name="qkv_back",
        )
        fed = both_cores(links, partial)
        d0, d1, *_ = tie(*dqkv[0], *partial)
        dqkv = ([d0, d1], dqkv[1])
        rights = [((dqkv[0][g], dqkv[1][g]), (ctx[layer][0][g], ctx[layer][1][g])) for g in range(2)]
        grads = weight_grads(links, (in_low[layer], lower_low), rights)
        return lower, fed, grads, (row_sums, sums)

    def add(keep, *came):
        total = keep.astype(F32)
        for part in came:
            total = total + part.astype(F32)
        return total

    def swap_far(name, give):
        return links.swap_as(name + "_far", links.swap_far, give)

    def swap_near(name, keep, came):
        return links.swap_as(name + "_near", links.swap_near, add(keep, came).astype(BF16))

    def scatter_z(name, parts, masks):
        return links.swap_as(name, links.scatter_z, parts, masks)

    z_top, z_last = links.z_masks[:0:-1], z_one
    state = {}
    vectors = [None, None]

    grad_top = own_rows(cotangent) * row_mask
    encoded_low = low
    piece = rows_first(low)
    upper, fed, (f1k0, f1k1, f1g0, f1g1), fvec = ffn_back(1, (grad_top,), lambda g: g)
    *fed, f1g0, f1g1, piece = tie(*fed, f1g0, f1g1, piece)
    f1c1 = swap_far("ffn1_grad_1", f1g1)
    twin = rows_second(piece)

    def during1(dqkv, kv):
        d0, d1, kv, state["f1_far_1"], given = tie(*dqkv, kv, f1c1, f1g0)
        state["f1_far_0"] = swap_far("ffn1_grad_0", given)
        return [d0, d1], kv

    lower, fed, (a1k0, a1k1, a1g0, a1g1), avec = attn_back(1, (upper, *fed), lambda low: low, tie, during1)
    vectors[1] = (fvec, avec)
    *fed, a1g0, a1g1 = tie(*fed, a1g0, a1g1)
    a1c = swap_far("attn1_grad", jnp.stack([a1g0, a1g1]))

    def middle0(grad_pre):
        g0, g1, came = tie(*grad_pre, state["f1_far_0"])
        state["f1"] = scatter_z("ffn1_grad_z1", jnp.stack([add(f1k0, came), add(f1k1, state["f1_far_1"])]), z_top)
        return [g0, g1]

    upper, fed, (f0k0, f0k1, f0g0, f0g1), fvec = ffn_back(0, (lower, *fed), middle0)
    *fed, f0g0, f0g1, a1c = tie(*fed, f0g0, f0g1, a1c)
    state["a1_near"] = swap_near("attn1_grad", a1k1, a1c[1])
    f0c1 = swap_far("ffn0_grad_1", f0g1)
    f0c0 = swap_far("ffn0_grad_0", f0g0)


    def first0(lower_low):
        lower_low, state["twin"] = tie(lower_low, twin)
        return lower_low

    def during0(dqkv, kv):
        d0, d1, kv, came, f1_in, near = tie(*dqkv, kv, f0c1, state["f1"][1], state["a1_near"])
        state["f0"] = swap_near("ffn0_grad", f0k1, came)
        state["a1"] = scatter_z("attn1_grad_z1", add(a1k0, a1c[0], near), z_top)
        state["f1"] = scatter_z("ffn1_grad_z2", add(state["f1"][0], f1_in), z_last)
        return [d0, d1], kv

    lower, fed, (a0k0, a0k1, a0g0, a0g1), avec = attn_back(0, (upper, *fed), first0, tie, during0)
    vectors[0] = (fvec, avec)
    sums = [part for f, a in vectors for part in (*f, *a)]
    vector, given = call(pack_kernel, [((8 * LAYERS, inputs.shape[1]), F32)] * 2, sums, name="vector_grads")
    *fed, a0g0, a0g1, given = tie(*fed, a0g0, a0g1, given)
    a0c1 = swap_far("attn0_grad_1", a0g1)
    a0c0 = swap_far("attn0_grad_0", a0g0)
    v_in = links.swap_as("vectors_x", links.swap_x, given)
    grad_hidden = call(final_sum_kernel, [(lower.shape, BF16)], (lower, *fed), name="input_grad")[0]
    attn_splits = ([(k * third, (k + 1) * third) for k in range(3)], [(3 * third, 4 * third)])
    ffn_splits = ([(0, wide)], [(wide, 2 * wide)])
    params = (attn_in, attn_out, ffn_up, ffn_down, head_bias, ffn_bias, row_params)
    states = [(params[i], moments[i], seconds[i]) for i in range(7)]

    attn_splits = ([(k * third, (k + 1) * third) for k in range(3)], [(3 * third, 4 * third)])
    ffn_splits = ([(0, wide)], [(wide, 2 * wide)])
    params = (attn_in, attn_out, ffn_up, ffn_down, head_bias, ffn_bias, row_params)
    states = [(params[i], moments[i], seconds[i]) for i in range(7)]

    order = links.places
    grad_hidden, v_in, f0c0, f0near, a1_in, order = tie(
        grad_hidden, v_in, f0c0, state["f0"], state["a1"][1], order
    )
    f0s = scatter_z("ffn0_grad_z1", add(f0k0, f0c0, f0near), z_top)
    a1s = scatter_z("attn1_grad_z2", add(state["a1"][0], a1_in), z_last)
    vector = vector + v_in
    v_in = links.swap_as("vectors_y", links.swap, vector, 4)
    encoded = all_rows(encoded_low, piece, state["twin"])
    came, a0c0, f0_in, f1_in, encoded, order = tie(a0c1, a0c0, f0s[1], state["f1"][1], encoded, order)
    a0near = swap_near("attn0_grad", a0k1, came)
    f0s = scatter_z("ffn0_grad_z2", add(f0s[0], f0_in), z_last)
    f1s = add(state["f1"][0], f1_in)
    f1near = links.swap_as("ffn1_grad_near", links.swap_near, f1s[1].astype(BF16))
    a0near, v_in, f1near, a1_in, order = tie(a0near, v_in, f1near, a1s[1], order)
    a1s = (a1s[0], a1_in)
    a0s = scatter_z("attn0_grad_z1", add(a0k0, a0c0, a0near), z_top)
    vector = vector + v_in
    v_in = links.swap_as("vectors_z", links.swap_z, vector, links.z_masks[0])
    grad_hidden, order = tie(grad_hidden, order)
    piece = rows_first(grad_hidden)
    ffn_new = adam_layer(1, ffn_splits, f1s[0], f1near, states[2:4], None)
    attn_new = adam_layer(1, attn_splits, *a1s, states[:2], None)
    came, f0_in, v_in, ffn_new[0], attn_new[0], order = tie(
        a0s[1], f0s[1], v_in, ffn_new[0], attn_new[0], order
    )
    a0s = scatter_z("attn0_grad_z2", add(a0s[0], came), z_last)
    vector = vector + v_in
    for mask in links.z_masks[1:]:
        vector = vector + links.swap_as("vectors_z", links.swap_z, vector, mask)
    piece, order = tie(piece, order)
    twin = rows_second(piece)
    flat = [a for state in states[4:] for a in state]
    vector_new = call(vector_adam_kernel, [(a.shape, F32) for a in flat], (vector, *flat), name="vector_adam")
    ffn_new = adam_layer(0, ffn_splits, f0s[0], f0_in, states[2:4], ffn_new)
    input_grad = all_rows(grad_hidden, piece, twin)
    a0_in, input_grad, order = tie(a0s[1], input_grad, order)
    attn_new = adam_layer(0, attn_splits, a0s[0], a0_in, states[:2], attn_new)

    new = [attn_new[:4], attn_new[4:], ffn_new[:4], ffn_new[4:]] + [vector_new[3 * i : 3 * i + 3] for i in range(3)]
    return (encoded, input_grad) + tuple(new[i][k] for k in range(3) for i in range(7)) + tuple(n[3] for n in new[:4])


def solution(mesh):
    n_dp = mesh.shape["dp"]
    row = P("dp", None)
    state = (
        P(None, None, "dp", "mp"),
        P(None, "dp", "mp"),
        P(None, "dp", "mp"),
        P(None, "dp", "mp"),
        P(None, None, "mp"),
        P(None, "mp"),
        P(),
    )

    def step(*args):
        return local(n_dp, *args)

    return jax.shard_map(
        step,
        mesh=mesh,
        in_specs=(row, row, row, P("dp")) + state * 3,
        out_specs=(row, row) + state * 3 + state[:4],
        check_vma=False,
    )
```

```python
import functools

import jax
import jax.numpy as jnp
from jax import lax
from jax.experimental import pallas as pl
from jax.experimental.pallas import tpu as pltpu
from jax.sharding import PartitionSpec as P

HEAD_DIM = 64
LAYERS = 2
ADAM_STEP = 10

EPS_NORM = 1e-12
EPS_ADAM = 1e-08
RATE_MATRIX = 0.04
RATE_VECTOR = 0.3
DECAY_MATRIX = 0.01

F32 = jnp.float32
BF16 = jnp.bfloat16
AXES = ("dp", "mp")
NN = ((1,), (0,))
NT = ((1,), (1,))
TN = ((0,), (0,))
PARTS = 3


def dot(a, b, dims):
    return lax.dot_general(a, b, (dims, ((), ())), preferred_element_type=F32)


def tie(*arrays):
    return lax.optimization_barrier(arrays)


class Links:
    def __init__(self, n_dp, rows):
        self.n_dp = n_dp
        self.count = n_dp * 4
        self.z_masks = [1 << bit for bit in reversed(range(n_dp.bit_length() - 2))]
        self.order = [0]
        for mask in self.z_masks:
            self.order += [place ^ mask for place in self.order]
        self.aligned = rows % 16 == 0
        dp_at = lax.axis_index("dp")
        mp_at = lax.axis_index("mp")
        self.at_x = mp_at // 2
        self.core = mp_at % 2
        self.at_y = dp_at % 2
        self.at_z = dp_at // 2
        self.places = jnp.stack([self.core, self.at_y, self.at_z, self.at_x]).astype(jnp.int32)

    def swap(self, array, mask0, mask1=None):
        mask1 = mask0 if mask1 is None else mask1
        pairs = [(i, i ^ (mask1 if i & 1 else mask0)) for i in range(self.count)]
        return lax.ppermute(array, AXES, pairs)

    def swap_as(self, name, swap, *args):
        with jax.named_scope(name):
            return swap(*args)

    def swap_core(self, array):
        return self.swap(array, 1)

    def swap_x(self, array):
        return self.swap(array, 2)

    def swap_z(self, array, mask):
        return self.swap(array, 8 * mask)

    def swap_near(self, array):
        return self.swap(array, 4, 2)

    def swap_far(self, array):
        return self.swap(array, 2, 4)

    def last_z(self, block, masks):
        for mask in masks[:-1]:
            block = jnp.concatenate([block, self.swap_z(block, mask)], axis=-3)
        return block, self.swap_z(block, masks[-1])

    def scatter_z(self, parts, masks):
        for mask in masks[:-1]:
            half = parts.shape[-3] // 2
            parts = parts[..., :half, :, :] + self.swap_z(parts[..., half:, :, :].astype(BF16), mask).astype(F32)
        half = parts.shape[-3] // 2
        return parts[..., :half, :, :], self.swap_z(parts[..., half:, :, :].astype(BF16), masks[-1])

    def assemble(self, *parts):
        if self.aligned:
            shape = parts[0].shape[-3:]
            kernel = functools.partial(assemble_kernel, self.order)
            outs = [((shape[0], 2) + shape[1:], parts[0].dtype)] * 2
            both = call(kernel, outs, (self.places, *parts), name="assemble")
        else:
            if len(parts) == 2:
                parts = [part[k] for part in parts for k in range(2)]
            order = jnp.array(inverse(self.order))[jnp.arange(parts[0].shape[0]) ^ self.at_z]
            block, near, far_block, far_near = (jnp.take(part, order, axis=0) for part in parts)
            first, low = self.core == 0, self.at_y == 0
            own_far = jnp.where(first, near, far_block)
            other_same = jnp.where(first, far_block, near)
            both = [
                jnp.stack([jnp.where(low, same, other), jnp.where(low, other, same)], axis=1)
                for same, other in ((block, own_far), (other_same, far_near))
            ]
        return [w.reshape(-1, w.shape[-1]) for w in both]


def inverse(order):
    return [order.index(place) for place in range(len(order))]


def assemble_kernel(order, places, *refs):
    *parts, own, other = refs
    if len(parts) == 2:
        parts = [part.at[k] for part in parts for k in range(2)]
    block, near, far_block, far_near = parts
    first, at_y, at_z = places[0] == 0, places[1], places[2]
    for m, distance in enumerate(order):
        j = distance ^ at_z
        own[j, at_y] = block[m]
        other[j, 1 - at_y] = far_near[m]

        @pl.when(first)
        def _(j=j, m=m):
            own[j, 1 - at_y] = near[m]
            other[j, at_y] = far_block[m]

        @pl.when(~first)
        def _(j=j, m=m):
            own[j, 1 - at_y] = far_block[m]
            other[j, at_y] = near[m]


def adam_step(master, moment, second, gradient, step_rate, decay_rate):
    correction = 1.0 - 0.5**ADAM_STEP
    moment_new = 0.5 * moment + 0.5 * gradient
    second_new = 0.5 * second + 0.5 * gradient * gradient
    update = (
        moment_new / correction / (jnp.sqrt(second_new / correction) + EPS_ADAM)
        + decay_rate * master
    )
    return (master - step_rate * update, moment_new, second_new)


def key_bias(limit, count, lanes):
    places = lax.broadcasted_iota(jnp.int32, (count, lanes), 0)
    return jnp.where(places < limit, 0.0, -1000000000.0)


def head_parts(qkv, far, swapped, g, h, full):
    third = qkv[g].shape[1] // 3
    k_at, v_at = third + h * HEAD_DIM, 2 * third + h * HEAD_DIM
    f_at = (g ^ swapped) * 2 * third + h * HEAD_DIM
    keys = qkv[g][:full, k_at : k_at + HEAD_DIM]
    values = qkv[g][:full, v_at : v_at + HEAD_DIM]
    keys_half = jnp.concatenate([qkv[g][full:, k_at : k_at + HEAD_DIM], far[:, f_at : f_at + HEAD_DIM]])
    f_at += third
    values_half = jnp.concatenate([qkv[g][full:, v_at : v_at + HEAD_DIM], far[:, f_at : f_at + HEAD_DIM]])
    return keys, values, keys_half, values_half


def attend_unit(keys, values, queries, bias_rows):
    scores = dot(keys, queries, NT) + bias_rows
    peak = jnp.max(scores, axis=0, keepdims=True)
    shifted = jnp.exp(scores - peak)
    total = jnp.sum(shifted, axis=0, keepdims=True)
    probs = (shifted * (1.0 / total)).astype(BF16)
    return dot(values, probs, TN), peak + jnp.log(total)


def full_kernel(limits, qkv0, qkv1, ctx0, ctx1, lse, bias):
    qkv, ctx = (qkv0, qkv1), (ctx0, ctx1)
    full, half = bias.shape
    third = qkv0.shape[1] // 3
    heads = third // HEAD_DIM
    bias[...] = key_bias(limits[0], full, half)
    for g in range(2):
        outs = [[], []]
        for h in range(heads):
            columns = slice(h * HEAD_DIM, (h + 1) * HEAD_DIM)
            keys = qkv[g][:full, third + h * HEAD_DIM : third + (h + 1) * HEAD_DIM]
            values = qkv[g][:full, 2 * third + h * HEAD_DIM : 2 * third + (h + 1) * HEAD_DIM]
            for part in range(2):
                rows = slice(part * half, (part + 1) * half)
                out, log_total = attend_unit(keys, values, qkv[g][rows, columns], bias[...])
                lse[g * heads + h : g * heads + h + 1, rows] = log_total
                outs[part].append(out)
        for part in range(2):
            rows = slice(part * half, (part + 1) * half)
            ctx[g][rows, :] = jnp.concatenate(outs[part], axis=0).T.astype(BF16)


def half_kernel(swapped, limits, qkv0, qkv1, far, ctx0, ctx1, lse, bias):
    qkv, ctx = (qkv0, qkv1), (ctx0, ctx1)
    half = far.shape[0]
    full = 2 * half
    heads = qkv0.shape[1] // 3 // HEAD_DIM
    bias[:half] = key_bias(limits[1], half, half)
    bias[half:] = key_bias(limits[2], half, half)
    for g in range(2):
        outs = []
        for h in range(heads):
            _, _, keys, values = head_parts(qkv, far, swapped, g, h, full)
            columns = slice(h * HEAD_DIM, (h + 1) * HEAD_DIM)
            out, log_total = attend_unit(keys, values, qkv[g][full:, columns], bias[...])
            lse[g * heads + h : g * heads + h + 1, :] = log_total
            outs.append(out)
        ctx[g][...] = jnp.concatenate(outs, axis=0).T.astype(BF16)


def attend_back_unit(keys, values, queries, grad_rows, log_total, bias_rows):
    probs = jnp.exp(dot(keys, queries, NT) + bias_rows - log_total)
    grad_probs = dot(values, grad_rows, NT)
    inner = jnp.sum(probs * grad_probs, axis=0, keepdims=True)
    grad_scores = (probs * (grad_probs - inner)).astype(BF16)
    grad_values = dot(probs.astype(BF16), grad_rows, NN)
    grad_keys = dot(grad_scores, queries, NN)
    grad_queries = dot(keys, grad_scores, TN)
    return grad_queries, grad_keys, grad_values


def half_back_kernel(swapped, limits, qkv0, qkv1, far, dctx0, dctx1, lse, dq0, dq1, own, sent, bias):
    qkv, dctx, dq = (qkv0, qkv1), (dctx0, dctx1), (dq0, dq1)
    half = far.shape[0]
    full = 2 * half
    third = qkv0.shape[1] // 3
    heads = third // HEAD_DIM
    bias[:half] = key_bias(limits[1], half, half)
    bias[half:] = key_bias(limits[2], half, half)
    for g in range(2):
        queries_out, keys_out, values_out = [], [], []
        for h in range(heads):
            _, _, keys, values = head_parts(qkv, far, swapped, g, h, full)
            columns = slice(h * HEAD_DIM, (h + 1) * HEAD_DIM)
            gq, gk, gv = attend_back_unit(
                keys,
                values,
                qkv[g][full:, columns],
                dctx[g][full:, columns],
                lse[g * heads + h : g * heads + h + 1, :],
                bias[...],
            )
            queries_out.append(gq)
            keys_out.append(gk)
            values_out.append(gv)
        dq[g][...] = jnp.concatenate(queries_out, axis=0).T.astype(BF16) * 0.125
        both = jnp.concatenate(keys_out + values_out, axis=1)
        own[:, 2 * third * g : 2 * third * (g + 1)] = both[:half]
        other = 1 - g
        sent[:, 2 * third * other : 2 * third * (other + 1)] = both[half:].astype(BF16)


def full_back_kernel(limits, qkv0, qkv1, dctx0, dctx1, lse, dqkv0, dqkv1, bias):
    qkv, dctx, dqkv = (qkv0, qkv1), (dctx0, dctx1), (dqkv0, dqkv1)
    full, half = bias.shape
    third = qkv0.shape[1] // 3
    heads = third // HEAD_DIM
    bias[...] = key_bias(limits[0], full, half)
    for g in range(2):
        queries_out, keys_out, values_out = [[], []], [], []
        for h in range(heads):
            columns = slice(h * HEAD_DIM, (h + 1) * HEAD_DIM)
            keys = qkv[g][:full, third + h * HEAD_DIM : third + (h + 1) * HEAD_DIM]
            values = qkv[g][:full, 2 * third + h * HEAD_DIM : 2 * third + (h + 1) * HEAD_DIM]
            sums = None
            for part in range(2):
                rows = slice(part * half, (part + 1) * half)
                gq, gk, gv = attend_back_unit(
                    keys,
                    values,
                    qkv[g][rows, columns],
                    dctx[g][rows, columns],
                    lse[g * heads + h : g * heads + h + 1, rows],
                    bias[...],
                )
                queries_out[part].append(gq)
                sums = (gk, gv) if sums is None else (sums[0] + gk, sums[1] + gv)
            keys_out.append(sums[0].astype(BF16))
            values_out.append(sums[1].astype(BF16))
        for part in range(2):
            rows = slice(part * half, (part + 1) * half)
            dqkv[g][rows, :third] = jnp.concatenate(queries_out[part], axis=0).T.astype(BF16) * 0.125
        dqkv[g][:, third:] = jnp.concatenate(keys_out + values_out, axis=1)


def half_fill_kernel(dq0, dq1, own, came, dqkv0, dqkv1):
    third = dq0.shape[1]
    for g, (dq, dqkv) in enumerate(((dq0, dqkv0), (dq1, dqkv1))):
        columns = slice(2 * third * g, 2 * third * (g + 1))
        both = (own[:, columns] + came[:, columns].astype(F32)).astype(BF16)
        dqkv[...] = jnp.concatenate([dq[...], both], axis=1)


VMEM = pl.BlockSpec(memory_space=pltpu.VMEM)
ANY = pl.BlockSpec(memory_space=pl.ANY)
SMEM = pl.BlockSpec(memory_space=pltpu.SMEM)
ROOM = pltpu.CompilerParams(vmem_limit_bytes=8 * 1024 * 1024)
CHEAP = pl.CostEstimate(flops=1, bytes_accessed=1, transcendentals=0)


def call(kernel, outs, ins, scratch=(), name=None, place=VMEM):
    specs = [SMEM if a.dtype == jnp.int32 else place for a in ins]
    results = pl.pallas_call(
        kernel,
        out_shape=[jax.ShapeDtypeStruct(s, d) for s, d in outs],
        in_specs=specs,
        out_specs=[VMEM] * len(outs),
        scratch_shapes=list(scratch),
        compiler_params=ROOM,
        cost_estimate=CHEAP,
        name=name,
    )(*ins)
    return list(results)


def attend_full(limits, qkv):
    tokens, third = qkv[0].shape[0], qkv[0].shape[1] // 3
    half = tokens // 3
    ctx0, ctx1, lse = call(
        full_kernel,
        [((2 * half, third), BF16)] * 2 + [((2 * third // HEAD_DIM, 2 * half), F32)],
        (limits, *qkv),
        [pltpu.VMEM((2 * half, half), F32)],
        name="attend_full",
    )
    return [ctx0, ctx1], lse


def attend_half(limits, qkv, far, swapped):
    half, third = far.shape[0], qkv[0].shape[1] // 3
    ctx0, ctx1, lse = call(
        functools.partial(half_kernel, swapped),
        [((half, third), BF16)] * 2 + [((2 * third // HEAD_DIM, half), F32)],
        (limits, *qkv, far),
        [pltpu.VMEM((2 * half, half), F32)],
        name="attend_half",
    )
    return [ctx0, ctx1], lse


def attend_half_back(limits, qkv, far, dctx, lse, swapped):
    half, third = far.shape[0], qkv[0].shape[1] // 3
    dq0, dq1, own, sent = call(
        functools.partial(half_back_kernel, swapped),
        [((half, third), BF16)] * 2 + [((half, 4 * third), F32), ((half, 4 * third), BF16)],
        (limits, *qkv, far, *dctx, lse),
        [pltpu.VMEM((2 * half, half), F32)],
        name="attend_half_back",
    )
    return (dq0, dq1), own, sent


def attend_full_back(limits, qkv, dctx, lse):
    half = qkv[0].shape[0] // 3
    return call(
        full_back_kernel,
        [((2 * half, qkv[0].shape[1]), BF16)] * 2,
        (limits, *qkv, *dctx, lse),
        [pltpu.VMEM((2 * half, half), F32)],
        name="attend_full_back",
    )


def fill_half(dq, own, came):
    shape = (own.shape[0], 3 * dq[0].shape[1])
    return call(half_fill_kernel, [(shape, BF16)] * 2, (*dq, own, came), name="fill_half")


def wgrad_kernel(count, pieces, order, places, *refs):
    step = count * pieces
    lefts, rights = refs[:count], (refs[count : count + step], refs[count + step : count + 2 * step])
    keep0, keep1, give0, give1, whole = refs[count + 2 * step :]
    first, at_y, at_z = places[0] == 0, places[1], places[2]
    rows = keep0.shape[1]
    turned = [left[...].T for left in lefts]
    for g in range(2):
        at = 0
        for k, left in enumerate(turned):
            right = [ref[...] for ref in rights[g][k * pieces : (k + 1) * pieces]]
            right = right[0] if pieces == 1 else jnp.concatenate(right)
            wide = right.shape[1]
            whole[:, at : at + wide] = dot(left, right, NN).astype(BF16)
            at += wide
        for y in range(2):
            same = at_y == y
            if g == 0:
                targets = ((same, keep0), (~same & first, keep1), (~same & ~first, give0))
            else:
                targets = ((same & first, give0), (same & ~first, keep1), (~same, give1))
            for when, ref in targets:

                @pl.when(when)
                def _(ref=ref, y=y):
                    for m, distance in enumerate(order):
                        from_row = pl.ds(pl.multiple_of((2 * (distance ^ at_z) + y) * rows, 16), rows)
                        ref[m] = whole[from_row, :]


def weight_grads(links, lefts, rights):
    features = lefts[0].shape[1]
    columns = sum(r[0].shape[1] for r in rights[0])
    blocks = links.n_dp // 2
    rows = features // links.n_dp
    if links.aligned:
        return call(
            functools.partial(wgrad_kernel, len(lefts), len(rights[0][0]), links.order),
            [((blocks, rows, columns), BF16)] * 4,
            (links.places, *lefts, *[piece for group in rights for right in group for piece in right]),
            [pltpu.VMEM((features, columns), BF16)],
            name="weight_grads",
        )
    low, first = links.at_y == 0, links.core == 0
    parts = []
    for group in rights:
        grad = jnp.concatenate([dot(a, jnp.concatenate(b), TN) for a, b in zip(lefts, group)], axis=1).astype(BF16)
        grad = jnp.take(grad.reshape(blocks, 2, rows, columns), jnp.array(links.order) ^ links.at_z, axis=0)
        parts += [jnp.where(low, grad[:, 0], grad[:, 1]), jnp.where(low, grad[:, 1], grad[:, 0])]
    own_same, own_far, other_same, other_far = parts
    return own_same, jnp.where(first, own_far, other_same), jnp.where(first, other_same, own_far), other_far


def both_cores(links, parts):
    return (*parts, *[links.swap_as("core", links.swap_core, part) for part in parts])


def in_parts(shape):
    return [((shape[0] // PARTS, shape[1]), BF16)] * PARTS


def core_sum(parts, at, rows):
    return parts[at][rows, :].astype(F32) + parts[at + PARTS][rows, :].astype(F32)


def put_parts(outs, at, value):
    step = outs[0].shape[0]
    done = 0
    while done < value.shape[0]:
        part, inner = divmod(at + done, step)
        count = min(step - inner, value.shape[0] - done)
        outs[part][inner : inner + count, :] = value[done : done + count, :].astype(BF16)
        done += count


def norm_kernel(step, *refs):
    parts, (residual, rows, out, low, scaled, inverse) = refs[: 2 * PARTS], refs[2 * PARTS :]
    wide = out.shape[1]
    third = parts[0].shape[0]
    for part in range(PARTS):

        @pl.loop(0, third // step)
        def _(i, part=part):
            inner = pl.ds(i * step, step)
            at = pl.ds(part * third + i * step, step)
            total = residual[at, :] + (core_sum(parts, part, inner) + rows[0:1, :])
            center = total - jnp.sum(total, axis=-1, keepdims=True) * (1.0 / wide)
            inv_std = lax.rsqrt(jnp.sum(center * center, axis=-1, keepdims=True) * (1.0 / wide) + EPS_NORM)
            normal = center * inv_std
            result = normal * rows[1:2, :] + rows[2:3, :]
            out[at, :] = result
            low[at, :] = result.astype(BF16)
            scaled[at, :] = normal
            inverse[at, :] = inv_std


def add_norm(parts, residual, rows):
    shape = residual.shape
    return call(
        functools.partial(norm_kernel, 64),
        [(shape, F32), (shape, BF16), (shape, F32), ((shape[0], 1), F32)],
        (*parts, residual, rows),
        name="add_norm",
    )


def norm_back_kernel(step, *refs):
    base, *parts, scaled, inverse, gain, out, low, sums = refs
    wide = out.shape[1]
    third = out.shape[0] // PARTS
    sums[...] = jnp.zeros_like(sums)
    for part in range(PARTS):

        @pl.loop(0, third // step)
        def _(i, part=part):
            at = pl.ds(part * third + i * step, step)
            grad = base[at, :]
            if parts:
                grad = grad + core_sum(parts, part, pl.ds(i * step, step))
            normal = scaled[at, :]
            upstream = grad * gain[...]
            mean_up = jnp.sum(upstream, axis=-1, keepdims=True) * (1.0 / wide)
            mean_cross = jnp.sum(upstream * normal, axis=-1, keepdims=True) * (1.0 / wide)
            result = inverse[at, :] * (upstream - mean_up - normal * mean_cross)
            out[at, :] = result
            low[at, :] = result.astype(BF16)
            for k, term in enumerate((result, grad * normal, grad)):
                sums[8 * k : 8 * (k + 1), :] += jnp.sum(term.reshape(-1, 8, wide), axis=0)


def norm_back(parts, scaled, inverse, gain):
    shape = scaled.shape
    return call(
        functools.partial(norm_back_kernel, 64),
        [(shape, F32), (shape, BF16), ((24, shape[1]), F32)],
        (*parts, scaled, inverse, gain),
        name="norm_back",
    )


def final_sum_kernel(base, *refs):
    parts, out = refs[: 2 * PARTS], refs[2 * PARTS]
    third = parts[0].shape[0]
    for part in range(PARTS):
        at = slice(part * third, (part + 1) * third)
        out[at, :] = (base[at, :] + core_sum(parts, part, slice(None))).astype(BF16)


def chunks(count, step=256):
    return [slice(at, at + step) for at in range(0, count, step)]


def qkv_kernel(low, w0, w1, bias, *refs):
    *other, out0, out1, extra = refs
    columns = out0.shape[1]
    third = columns // 3
    half = extra.shape[0]
    scale = jnp.where(lax.broadcasted_iota(jnp.int32, (1, columns), 1) < third, 0.125, 1.0)
    for g, (weight, out) in enumerate(((w0, out0), (w1, out1))):
        at = slice(2 * third * g, 2 * third * (g + 1))
        for rows in chunks(low.shape[0]):
            out[rows, :] = ((dot(low[rows, :], weight[:, :columns], NN) + bias[g : g + 1, :]) * scale).astype(BF16)
        if other:
            more = dot(other[0][...], weight[:, :columns], NN) + bias[g : g + 1, :]
            extra[:, at] = more[:, third:].astype(BF16)
        else:
            extra[:, at] = out[2 * half :, third:]


def project(low, weights, bias, other=None):
    tokens, columns = low.shape[0], bias.shape[1]
    half = tokens // 3
    ins = (low, *weights, bias) + (() if other is None else (other,))
    q0, q1, extra = call(
        qkv_kernel,
        [((tokens, columns), BF16)] * 2 + [((half, 4 * columns // 3), BF16)],
        ins,
        name="queries_keys_values",
    )
    return [q0, q1], extra


def row_thirds(full0, full1, half0, half1):
    half = half0.shape[0]
    rows = [slice(0, half), slice(half, 2 * half), slice(0, half)]
    return [((full0, full1) if k < 2 else (half0, half1), rows[k]) for k in range(3)]


def out_kernel(full0, full1, half0, half1, w0, w1, *outs):
    third = full0.shape[1]
    at = w0.shape[1] - third
    tails = (w0[:, at:], w1[:, at:])
    for k, (pair, rows) in enumerate(row_thirds(full0, full1, half0, half1)):
        put_parts(outs, k * half0.shape[0], dot(pair[0][rows, :], tails[0], NT) + dot(pair[1][rows, :], tails[1], NT))


def ffn_kernel(low, w0, w1, bias, act0, act1, slope0, slope1, *outs):
    wide = bias.shape[1]
    groups = ((w0, act0, slope0), (w1, act1, slope1))
    for rows in chunks(low.shape[0], 128):
        total = None
        for g, (weight, act, slope) in enumerate(groups):
            pre = dot(low[rows, :], weight[:, :wide], NN) + bias[g : g + 1, :]
            cdf = 0.5 * (1.0 + lax.erf(pre * 0.7071067811865476))
            slope[rows, :] = cdf + pre * (jnp.exp(-0.5 * pre * pre) * 0.3989422804014327)
            active = (pre * cdf).astype(BF16)
            act[rows, :] = active
            part = dot(active, weight[:, wide:], NT)
            total = part if total is None else total + part
        put_parts(outs, rows.start, total)


def feed_forward(low, weights, bias):
    shape = (low.shape[0], bias.shape[1])
    act0, act1, slope0, slope1, *partial = call(
        ffn_kernel,
        [(shape, BF16)] * 2 + [(shape, F32)] * 2 + in_parts(low.shape),
        (low, *weights, bias),
        name="feed_forward",
    )
    return [(act0, slope0), (act1, slope1)], partial


def add_rows(array):
    return jnp.sum(array.astype(F32).reshape(-1, 8, array.shape[1]), axis=0)


def ffn_back_kernel(low, w0, w1, slope0, slope1, pre0, pre1, sums):
    wide = slope0.shape[1]
    for g, (weight, slope, pre) in enumerate(((w0, slope0, pre0), (w1, slope1, pre1))):
        total = None
        for rows in chunks(low.shape[0]):
            grad = (dot(low[rows, :], weight[:, wide:], NN) * slope[rows, :]).astype(BF16)
            pre[rows, :] = grad
            part = add_rows(grad)
            total = part if total is None else total + part
        sums[8 * g : 8 * (g + 1), :] = total


def ffn_back_first(low, weights, slopes):
    shape = slopes[0].shape
    pre0, pre1, sums = call(
        ffn_back_kernel,
        [(shape, BF16)] * 2 + [((16, shape[1]), F32)],
        (low, *weights, *slopes),
        name="pre_grad",
    )
    return [pre0, pre1], sums


def back_out_kernel(d0, d1, w0, w1, *outs):
    wide = d0.shape[1]
    for rows in chunks(d0.shape[0]):
        put_parts(outs, rows.start, dot(d0[rows, :], w0[:, :wide], NT) + dot(d1[rows, :], w1[:, :wide], NT))


def qkv_back_kernel(full0, full1, half0, half1, w0, w1, *refs):
    *outs, sums = refs
    wide = full0.shape[1]
    totals = [None, None]
    for k, (pair, rows) in enumerate(row_thirds(full0, full1, half0, half1)):
        parts = [ref[rows, :] for ref in pair]
        put_parts(outs, k * half0.shape[0], dot(parts[0], w0[:, :wide], NT) + dot(parts[1], w1[:, :wide], NT))
        for g in range(2):
            part = add_rows(parts[g])
            totals[g] = part if totals[g] is None else totals[g] + part
    for g in range(2):
        sums[8 * g : 8 * (g + 1), :] = totals[g]


def context_grad_kernel(low, w0, w1, out0, out1):
    third = out0.shape[1]
    at = w0.shape[1] - third
    for weight, out in ((w0, out0), (w1, out1)):
        tail = weight[:, at:]
        for rows in chunks(low.shape[0]):
            out[rows, :] = dot(low[rows, :], tail, NN).astype(BF16)


def adam_kernel(splits, count, *refs):
    keep, came, *refs = refs
    ins, outs = refs[: 3 * len(splits)], refs[3 * len(splits) + count :]
    for i, ranges in enumerate(splits):
        master, moment, second = ins[3 * i : 3 * i + 3]
        results = outs[4 * i : 4 * i + 4]
        for k, (low, high) in enumerate(ranges):
            at = (0, k) if len(ranges) > 1 else (0,)
            grad = keep[0, :, low:high] + came[0, :, low:high].astype(F32)
            new = adam_step(master[at], moment[at], second[at], grad, RATE_MATRIX, DECAY_MATRIX)
            for ref, value in zip(results, (*new, new[0].astype(BF16))):
                ref[at] = value


def adam_layer(layer, splits, keep, came, states, before):
    def block(array):
        rest = array.shape[1:]
        return pl.BlockSpec((1,) + rest, lambda i, n=len(rest): (layer,) + (0,) * n)

    flat = [a for state in states for a in state]
    outs, specs = [], []
    for state in states:
        outs += [jax.ShapeDtypeStruct(state[0].shape, d) for d in (F32, F32, F32, BF16)]
        specs += [block(state[0])] * 4
    before = [] if before is None else before
    results = pl.pallas_call(
        functools.partial(adam_kernel, splits, len(before)),
        grid=(1,),
        out_shape=outs,
        in_specs=[VMEM] * 2 + [block(a) for a in flat] + [pl.BlockSpec(memory_space=pl.ANY)] * len(before),
        out_specs=specs,
        input_output_aliases={2 + len(flat) + i: i for i in range(len(before))},
        compiler_params=ROOM,
        cost_estimate=CHEAP,
        name="adam",
    )(keep, came, *flat, *before)
    return list(results)


def pack_kernel(*refs):
    *parts, own, other = refs
    own[...] = jnp.zeros_like(own)
    other[...] = jnp.zeros_like(other)
    for layer in range(LAYERS):
        upper, pre, lower, heads = parts[4 * layer : 4 * layer + 4]
        third = heads.shape[1] // 3

        def total(ref, k):
            return jnp.sum(ref[8 * k : 8 * (k + 1), :], axis=0, keepdims=True)

        rows = [(lower, 0), (upper, 0), (lower, 1), (lower, 2), (upper, 1), (upper, 2)]
        for k, row in enumerate(rows):
            value = total(*row)
            own[6 * layer + k : 6 * layer + k + 1, :] = value
            other[6 * layer + k : 6 * layer + k + 1, :] = value
        for g, ref in enumerate((own, other)):
            at = 6 * LAYERS + layer
            ref[at : at + 1, :] = total(pre, g)
            head = total(heads, g)
            at += LAYERS
            ref[at : at + 1, : 2 * third] = jnp.concatenate([head[:, :third], head[:, 2 * third :]], axis=1)


def vector_adam_kernel(grads, *refs):
    ins, outs = refs[:9], refs[9:]
    third = ins[0].shape[2]

    def update(i, at, grad):
        new = adam_step(ins[3 * i][at], ins[3 * i + 1][at], ins[3 * i + 2][at], grad, RATE_VECTOR, 0.0)
        for k, value in enumerate(new):
            outs[3 * i + k][at] = value

    for layer in range(LAYERS):
        at = 7 * LAYERS + layer
        for k in range(2):
            grad = grads[at : at + 1, k * third : (k + 1) * third]
            update(0, (layer, slice(k, k + 1)), grad)
        update(1, (slice(layer, layer + 1),), grads[at - LAYERS : at - LAYERS + 1, :])
        update(2, (layer,), grads[6 * layer : 6 * layer + 6, :])


def rows_kernel(places, low, piece, twin, out):
    first, at_x = places[0] == 0, places[3]
    half = low.shape[0] // 3
    part = piece.shape[0]

    def put(start, rows):
        out[pl.ds(pl.multiple_of(start, 8), rows.shape[0]), :] = rows.astype(F32)

    def put_other(upper, lower):
        put((1 - at_x) * 4 * half, upper[...])
        put((1 - at_x) * 4 * half + part, lower[: 2 * half - part, :])
        put(2 * half + (1 - at_x) * half, lower[2 * half - part :, :])

    put(at_x * 4 * half, low[: 2 * half, :])
    put(2 * half + at_x * half, low[2 * half :, :])

    @pl.when(first)
    def _():
        put_other(piece, twin)

    @pl.when(~first)
    def _():
        put_other(twin, piece)


def local(n_dp, *args):
    (
        inputs,
        cotangent,
        word_lengths,
        word_count,
        attn_in,
        attn_out,
        ffn_up,
        ffn_down,
        head_bias,
        ffn_bias,
        row_params,
    ) = args[:11]
    moments, seconds = args[11:18], args[18:25]
    links = Links(n_dp, attn_out.shape[1])
    at_x, core = links.at_x, links.core
    seq_len = inputs.shape[0] // word_count.shape[0]
    half = seq_len // 2
    third, wide = attn_in.shape[3], ffn_up.shape[2]

    def own_rows(array):
        whole = lax.dynamic_slice_in_dim(array, at_x * 2 * seq_len, seq_len)
        return jnp.concatenate([whole, lax.dynamic_slice_in_dim(array, seq_len + at_x * half, half)])

    def rows_first(low):
        part = low.shape[0] // 2
        return links.swap_as("rows_x", links.swap_x, lax.dynamic_slice_in_dim(low, core * part, part))

    def rows_second(piece):
        return links.swap_as("rows_core", links.swap_core, piece)

    def all_rows(low, piece, twin):
        return call(rows_kernel, [(inputs.shape, F32)], (links.places, low, piece, twin), name="all_rows")[0]

    def packed_attn(layer):
        attn = [attn_in[layer, 0], attn_in[layer, 1], attn_in[layer, 2], attn_out[layer]]
        return jnp.concatenate([a.astype(BF16) for a in attn], axis=1)[None]

    def packed_ffn(layer):
        return jnp.concatenate([ffn_up[layer].astype(BF16), ffn_down[layer].astype(BF16)], axis=1)[None]

    z_one, z_rest = links.z_masks[:1], links.z_masks[1:]
    join = jnp.concatenate

    a0 = packed_attn(0)
    a0_in = links.swap_as("attn0_z2", links.swap_z, a0, links.z_masks[0])
    later = join([packed_attn(1), packed_ffn(1)], axis=2)
    biases = jnp.concatenate([head_bias.reshape(-1), ffn_bias.reshape(-1)])
    a0_in, f0, later, biases = tie(a0_in, packed_ffn(0), later, biases)
    a0 = join([a0, a0_in])
    a0, a0_in = links.swap_as("attn0_z1", links.last_z, a0, z_rest)
    f0_in = links.swap_as("ffn0_z2", links.swap_z, f0, links.z_masks[0])
    later_near = links.swap_as("layer1_near", links.swap_near, later)
    bias_far = links.swap_as("biases", links.swap_x, biases)
    a0_in, f0_in, later_near, bias_far = tie(a0_in, f0_in, later_near, bias_far)
    a0, f0 = join([a0, a0_in]), join([f0, f0_in])
    near = links.swap_as("attn0_near", links.swap_near, a0)
    a0far = links.swap_as("attn0_far", links.swap_far, a0)
    f0, f0_in = links.swap_as("ffn0_z1", links.last_z, f0, z_rest)
    later = jnp.stack([later, later_near])
    a1, f1 = later[..., : 4 * third], later[..., 4 * third :]
    a1_in = links.swap_as("attn1_z2", links.swap_z, a1, links.z_masks[0])
    near, f1 = tie(near, f1)
    a0last = links.swap_as("attn0_far_near", links.swap_far, near)
    a0far, a0last, f0_in, a1_in, f1 = tie(a0far, a0last, f0_in, a1_in, f1)
    f0 = join([f0, f0_in])
    f0near = links.swap_as("ffn0_near", links.swap_near, f0)
    f0far = links.swap_as("ffn0_far", links.swap_far, f0)
    a1 = join([a1, a1_in], axis=1)
    a1, a1_in = links.swap_as("attn1_z1", links.last_z, a1, z_rest)
    f1_in = links.swap_as("ffn1_z2", links.swap_z, f1, links.z_masks[0])
    a0 = links.assemble(a0, near, a0far, a0last)
    head_b = (head_bias, bias_far[: head_bias.size].reshape(head_bias.shape))
    ffn_b = (ffn_bias, bias_far[head_bias.size :].reshape(ffn_bias.shape))
    zeros = jnp.zeros((third,), F32)
    qkv_b = [
        jnp.stack([jnp.concatenate([b[layer, 0], zeros, b[layer, 1]]) for b in head_b]) for layer in range(LAYERS)
    ]
    ffn_b = [jnp.stack([b[layer] for b in ffn_b]) for layer in range(LAYERS)]

    slots = jnp.arange(word_lengths.shape[1], dtype=jnp.int32)
    used = jnp.sum(jnp.where(slots[None, :] < word_count[:, None], word_lengths, 0), axis=1)
    used_full = jnp.where(at_x == 0, used[0], used[2])
    limits = jnp.stack([used_full, used[1] - at_x * half, used[1] - (1 - at_x) * half]).astype(jnp.int32)
    places = jnp.arange(seq_len, dtype=jnp.int32)
    row_mask = jnp.concatenate([places < limits[0], places[:half] < limits[1]]).astype(F32)[:, None]

    hidden = own_rows(inputs)
    low_other = lax.dynamic_slice_in_dim(inputs, seq_len + (1 - at_x) * half, half).astype(BF16)
    in_low = [hidden.astype(BF16), None]
    qkv, far, ctx, lse = [None] * 2, [None] * 2, [None] * 2, [None] * 2
    weight_a, weight_f = [a0, None], [None, None]

    def out_part(layer):
        return call(
            out_kernel, in_parts(hidden.shape), (*ctx[layer][0], *ctx[layer][1], *weight_a[layer]), name="attention_out"
        )

    norms = [None] * 2
    ffn_parts = [None] * 2

    row_parts = [
        [jnp.stack([row_params[i, k] for k in ks]) for ks in ((0, 2, 3), (1, 4, 5))] for i in range(LAYERS)
    ]
    row_parts = [
        [jnp.stack([row_params[i, k] for k in ks]) for ks in ((0, 2, 3), (1, 4, 5))] for i in range(LAYERS)
    ]
    qkv[0], far[0] = project(in_low[0], a0, qkv_b[0], low_other)
    whole, whole_lse = attend_full(limits, qkv[0])
    *whole, f0near, a1_in, f1_in = tie(*whole, f0near, a1_in, f1_in)
    f0last = links.swap_as("ffn0_far_near", links.swap_far, f0near)
    a1 = join([a1, a1_in], axis=1)
    f1 = join([f1, f1_in], axis=1)
    far[0], f1 = tie(far[0], f1)
    f1, f1_in = links.swap_as("ffn1_z1", links.last_z, f1, z_rest)
    split, split_lse = attend_half(limits, qkv[0], far[0], 0)
    *split, f0far = tie(*split, f0far)
    ctx[0], lse[0] = (whole, split), (whole_lse, split_lse)
    normed, normed_low, scaled_one, inv_one = add_norm(both_cores(links, out_part(0)), hidden, row_parts[0][0])
    normed_low, f0last, a1 = tie(normed_low, f0last, a1)
    a1far = links.swap_as("attn1_far", links.swap_far, a1)
    f0 = links.assemble(f0, f0near, f0far, f0last)
    weight_f[0] = f0
    ffn_parts[0], partial = feed_forward(normed_low, f0, ffn_b[0])
    *partial, a1far, f1_in = tie(*partial, a1far, f1_in)
    f1_own, f1_near = join([f1[0], f1_in[0]]), join([f1[1], f1_in[1]])
    f1far = links.swap_as("ffn1_far", links.swap_far, f1_own)
    fed = both_cores(links, partial)
    hidden, low, scaled_two, inv_two = add_norm(fed, normed, row_parts[0][1])
    norms[0] = (normed_low, scaled_one, inv_one, scaled_two, inv_two)

    a1 = links.assemble(a1, a1far)
    weight_a[1] = a1
    in_low[1] = low
    qkv[1], sent = project(low, a1, qkv_b[1])
    far[1] = links.swap_as("keys_values", links.swap_x, sent)
    whole, whole_lse = attend_full(limits, qkv[1])
    *whole, far[1], f1_near, f1far = tie(*whole, far[1], f1_near, f1far)
    f1last = links.swap_as("ffn1_far_near", links.swap_far, f1_near)
    split, split_lse = attend_half(limits, qkv[1], far[1], 1)
    ctx[1], lse[1] = (whole, split), (whole_lse, split_lse)
    fed = both_cores(links, out_part(1))
    normed, normed_low, scaled_one, inv_one = add_norm(fed, hidden, row_parts[1][0])
    normed_low, f1last = tie(normed_low, f1last)
    f1 = links.assemble(f1_own, f1_near, f1far, f1last)
    weight_f[1] = f1
    ffn_parts[1], partial = feed_forward(normed_low, f1, ffn_b[1])
    fed = both_cores(links, partial)
    hidden, low, scaled_two, inv_two = add_norm(fed, normed, row_parts[1][1])
    norms[1] = (normed_low, scaled_one, inv_one, scaled_two, inv_two)
    state = {}

    def ffn_back(layer, grad_parts, middle):
        normed_low, _, _, scaled_two, inv_two = norms[layer]
        upper, upper_low, row_sums = norm_back(grad_parts, scaled_two, inv_two, row_params[layer, 4:5])
        slopes = [part[1] for part in ffn_parts[layer]]
        grad_pre, pre_sums = ffn_back_first(upper_low, weight_f[layer], slopes)
        grad_pre = middle(grad_pre)
        partial = call(back_out_kernel, in_parts(upper.shape), (*grad_pre, *weight_f[layer]), name="up_back")
        fed = both_cores(links, partial)
        g0, g1, *_ = tie(*grad_pre, *partial)
        grad_pre = [g0, g1]
        grads = weight_grads(
            links,
            (normed_low, upper_low),
            [((grad_pre[g],), (ffn_parts[layer][g][0],)) for g in range(2)],
        )
        return upper, fed, grads, (row_sums, pre_sums)

    def attn_back(layer, grad_parts, first, early, during):
        _, scaled_one, inv_one, _, _ = norms[layer]
        lower, lower_low, row_sums = norm_back(grad_parts, scaled_one, inv_one, row_params[layer, 2:3])
        lower_low = first(lower_low)
        weight = weight_a[layer]
        shape = (lower.shape[0], third)
        dctx = call(context_grad_kernel, [(shape, BF16)] * 2, (lower_low, *weight), name="context_grad")
        dq, own, sent = attend_half_back(limits, qkv[layer], far[layer], dctx, lse[layer][1], layer)
        d0, d1, sent = early(*dctx, sent)
        came = links.swap_as("keys_values_grad", links.swap_x, sent)
        dqkv = attend_full_back(limits, qkv[layer], (d0, d1), lse[layer][0])
        dqkv, came = during(dqkv, came)
        dqkv = (dqkv, fill_half(dq, own, came))
        *partial, sums = call(
            qkv_back_kernel,
            in_parts(lower.shape) + [((16, 3 * third), F32)],
            (*dqkv[0], *dqkv[1], *weight),
            name="qkv_back",
        )
        fed = both_cores(links, partial)
        d0, d1, *_ = tie(*dqkv[0], *partial)
        dqkv = ([d0, d1], dqkv[1])
        rights = [((dqkv[0][g], dqkv[1][g]), (ctx[layer][0][g], ctx[layer][1][g])) for g in range(2)]
        grads = weight_grads(links, (in_low[layer], lower_low), rights)
        return lower, fed, grads, (row_sums, sums)

    def add(keep, *came):
        total = keep.astype(F32)
        for part in came:
            total = total + part.astype(F32)
        return total

    def swap_far(name, give):
        return links.swap_as(name + "_far", links.swap_far, give)

    def swap_near(name, keep, came):
        return links.swap_as(name + "_near", links.swap_near, add(keep, came).astype(BF16))

    def scatter_z(name, parts, masks):
        return links.swap_as(name, links.scatter_z, parts, masks)

    z_top, z_last = links.z_masks[:0:-1], z_one
    state = {}
    vectors = [None, None]

    grad_top = own_rows(cotangent) * row_mask
    encoded_low = low
    piece = rows_first(low)
    upper, fed, (f1k0, f1k1, f1g0, f1g1), fvec = ffn_back(1, (grad_top,), lambda g: g)
    *fed, f1g0, f1g1, piece = tie(*fed, f1g0, f1g1, piece)
    f1c1 = swap_far("ffn1_grad_1", f1g1)
    twin = rows_second(piece)

    def during1(dqkv, kv):
        d0, d1, kv, state["f1_far_1"], given = tie(*dqkv, kv, f1c1, f1g0)
        state["f1_far_0"] = swap_far("ffn1_grad_0", given)
        return [d0, d1], kv

    lower, fed, (a1k0, a1k1, a1g0, a1g1), avec = attn_back(1, (upper, *fed), lambda low: low, tie, during1)
    vectors[1] = (fvec, avec)
    *fed, a1g0, a1g1 = tie(*fed, a1g0, a1g1)
    a1c = swap_far("attn1_grad", jnp.stack([a1g0, a1g1]))

    def middle0(grad_pre):
        g0, g1, came = tie(*grad_pre, state["f1_far_0"])
        state["f1"] = scatter_z("ffn1_grad_z1", jnp.stack([add(f1k0, came), add(f1k1, state["f1_far_1"])]), z_top)
        return [g0, g1]

    upper, fed, (f0k0, f0k1, f0g0, f0g1), fvec = ffn_back(0, (lower, *fed), middle0)
    *fed, f0g0, f0g1, a1c = tie(*fed, f0g0, f0g1, a1c)
    state["a1_near"] = swap_near("attn1_grad", a1k1, a1c[1])
    f0c1 = swap_far("ffn0_grad_1", f0g1)
    f0c0 = swap_far("ffn0_grad_0", f0g0)


    def first0(lower_low):
        lower_low, state["twin"] = tie(lower_low, twin)
        return lower_low

    def during0(dqkv, kv):
        d0, d1, kv, came, f1_in, near = tie(*dqkv, kv, f0c1, state["f1"][1], state["a1_near"])
        state["f0"] = swap_near("ffn0_grad", f0k1, came)
        state["a1"] = scatter_z("attn1_grad_z1", add(a1k0, a1c[0], near), z_top)
        state["f1"] = scatter_z("ffn1_grad_z2", add(state["f1"][0], f1_in), z_last)
        return [d0, d1], kv

    lower, fed, (a0k0, a0k1, a0g0, a0g1), avec = attn_back(0, (upper, *fed), first0, tie, during0)
    vectors[0] = (fvec, avec)
    sums = [part for f, a in vectors for part in (*f, *a)]
    vector, given = call(pack_kernel, [((8 * LAYERS, inputs.shape[1]), F32)] * 2, sums, name="vector_grads")
    *fed, a0g0, a0g1, given = tie(*fed, a0g0, a0g1, given)
    a0c1 = swap_far("attn0_grad_1", a0g1)
    a0c0 = swap_far("attn0_grad_0", a0g0)
    v_in = links.swap_as("vectors_x", links.swap_x, given)
    grad_hidden = call(final_sum_kernel, [(lower.shape, BF16)], (lower, *fed), name="input_grad")[0]
    attn_splits = ([(k * third, (k + 1) * third) for k in range(3)], [(3 * third, 4 * third)])
    ffn_splits = ([(0, wide)], [(wide, 2 * wide)])
    params = (attn_in, attn_out, ffn_up, ffn_down, head_bias, ffn_bias, row_params)
    states = [(params[i], moments[i], seconds[i]) for i in range(7)]

    attn_splits = ([(k * third, (k + 1) * third) for k in range(3)], [(3 * third, 4 * third)])
    ffn_splits = ([(0, wide)], [(wide, 2 * wide)])
    params = (attn_in, attn_out, ffn_up, ffn_down, head_bias, ffn_bias, row_params)
    states = [(params[i], moments[i], seconds[i]) for i in range(7)]

    order = links.places
    grad_hidden, v_in, f0c0, f0near, order = tie(grad_hidden, v_in, f0c0, state["f0"], order)
    f0s = scatter_z("ffn0_grad_z1", add(f0k0, f0c0, f0near), z_top)
    vector = vector + v_in
    v_in = links.swap_as("vectors_y", links.swap, vector, 4)
    encoded = all_rows(encoded_low, piece, state["twin"])
    came, a0c0, f0_in, f1_in, a1_in, encoded, order = tie(
        a0c1, a0c0, f0s[1], state["f1"][1], state["a1"][1], encoded, order
    )
    a0near = swap_near("attn0_grad", a0k1, came)
    a1s = scatter_z("attn1_grad_z2", add(state["a1"][0], a1_in), z_last)
    f0s = scatter_z("ffn0_grad_z2", add(f0s[0], f0_in), z_last)
    f1s = add(state["f1"][0], f1_in)
    f1near = links.swap_as("ffn1_grad_near", links.swap_near, f1s[1].astype(BF16))
    a0near, v_in, f1near, a1_in, order = tie(a0near, v_in, f1near, a1s[1], order)
    a1s = (a1s[0], a1_in)
    a0s = scatter_z("attn0_grad_z1", add(a0k0, a0c0, a0near), z_top)
    vector = vector + v_in
    v_in = links.swap_as("vectors_z", links.swap_z, vector, links.z_masks[0])
    grad_hidden, order = tie(grad_hidden, order)
    piece = rows_first(grad_hidden)
    ffn_new = adam_layer(1, ffn_splits, f1s[0], f1near, states[2:4], None)
    attn_new = adam_layer(1, attn_splits, *a1s, states[:2], None)
    came, f0_in, v_in, ffn_new[0], attn_new[0], order = tie(
        a0s[1], f0s[1], v_in, ffn_new[0], attn_new[0], order
    )
    a0s = scatter_z("attn0_grad_z2", add(a0s[0], came), z_last)
    vector = vector + v_in
    for mask in links.z_masks[1:]:
        vector = vector + links.swap_as("vectors_z", links.swap_z, vector, mask)
    piece, order = tie(piece, order)
    twin = rows_second(piece)
    flat = [a for state in states[4:] for a in state]
    vector_new = call(vector_adam_kernel, [(a.shape, F32) for a in flat], (vector, *flat), name="vector_adam")
    ffn_new = adam_layer(0, ffn_splits, f0s[0], f0_in, states[2:4], ffn_new)
    input_grad = all_rows(grad_hidden, piece, twin)
    a0_in, input_grad, order = tie(a0s[1], input_grad, order)
    attn_new = adam_layer(0, attn_splits, a0s[0], a0_in, states[:2], attn_new)

    new = [attn_new[:4], attn_new[4:], ffn_new[:4], ffn_new[4:]] + [vector_new[3 * i : 3 * i + 3] for i in range(3)]
    return (encoded, input_grad) + tuple(new[i][k] for k in range(3) for i in range(7)) + tuple(n[3] for n in new[:4])


def solution(mesh):
    n_dp = mesh.shape["dp"]
    row = P("dp", None)
    state = (
        P(None, None, "dp", "mp"),
        P(None, "dp", "mp"),
        P(None, "dp", "mp"),
        P(None, "dp", "mp"),
        P(None, None, "mp"),
        P(None, "mp"),
        P(),
    )

    def step(*args):
        return local(n_dp, *args)

    return jax.shard_map(
        step,
        mesh=mesh,
        in_specs=(row, row, row, P("dp")) + state * 3,
        out_specs=(row, row) + state * 3 + state[:4],
        check_vma=False,
    )
```
